32 devices in a mesh: dp: 4 (over z), ctx: 4 (over x, core), tensor: 2 (over y).
Axes of the slice: x: 2, y: 2, z: 4, core: 2. Of those that a mesh axis runs over, the one named last changes fastest.
Arguments:
- tokens: bfloat16 [8192, 768], P(('dp', 'ctx')), may hold values from -6 to 6
- out_grad: bfloat16 [8192, 768], P(('dp', 'ctx')), may hold values from -6 to 6
- lengths: int32 [4, 3], P('dp'), may hold values from 1 to 1024, 2048 in all within a row
- query_weight: bfloat16 [768, 768], P(None, 'tensor'), may hold values from -0.21875 to 0.21875
- query_bias: float32 [768], P('tensor'), may hold values from -3 to 3
- key_weight: bfloat16 [768, 768], P(None, 'tensor'), may hold values from -0.21875 to 0.21875
- key_bias: float32 [768], P('tensor'), may hold values from -3 to 3
- value_weight: bfloat16 [768, 768], P(None, 'tensor'), may hold values from -0.21875 to 0.21875
- value_bias: float32 [768], P('tensor'), may hold values from -3 to 3
- output_weight: bfloat16 [768, 768], P('tensor'), may hold values from -0.875 to 0.875
- output_bias: float32 [768], replicated, may hold values from -3 to 3
- first_gain: float32 [768], replicated, may hold values from 0.5 to 1.5
- first_shift: float32 [768], replicated, may hold values from -3 to 3
- inner_weight: bfloat16 [768, 3072], P(None, 'tensor'), may hold values from -0.21875 to 0.21875
- inner_bias: float32 [3072], P('tensor'), may hold values from -3 to 3
- outer_weight: bfloat16 [3072, 768], P('tensor'), may hold values from -0.109375 to 0.109375
- outer_bias: float32 [768], replicated, may hold values from -3 to 3
- second_gain: float32 [768], replicated, may hold values from 0.5 to 1.5
- second_shift: float32 [768], replicated, may hold values from -3 to 3
Outputs:
- layer_out: bfloat16 [8192, 768], P(('dp', 'ctx'))
- input_grad: bfloat16 [8192, 768], P(('dp', 'ctx'))
- query_weight_grad: float32 [768, 768], P(None, 'tensor')
- query_bias_grad: float32 [768], P('tensor')
- key_weight_grad: float32 [768, 768], P(None, 'tensor')
- key_bias_grad: float32 [768], P('tensor')
- value_weight_grad: float32 [768, 768], P(None, 'tensor')
- value_bias_grad: float32 [768], P('tensor')
- output_weight_grad: float32 [768, 768], P('tensor')
- output_bias_grad: float32 [768], replicated
- first_gain_grad: float32 [768], replicated
- first_shift_grad: float32 [768], replicated
- inner_weight_grad: float32 [768, 3072], P(None, 'tensor')
- inner_bias_grad: float32 [3072], P('tensor')
- outer_weight_grad: float32 [3072, 768], P('tensor')
- outer_bias_grad: float32 [768], replicated
- second_gain_grad: float32 [768], replicated
- second_shift_grad: float32 [768], replicated
The draws below stay inside these ranges and needn't reach their ends.
Inputs may be any that keep to these rules, and one draw needn't show every extreme that they name: Row g holds the lengths of the 3 sequences of data group g in order; they sum to 2048 and the longest is 1024.
All inputs are finite; a program needn't handle non-finite values.
Results may differ from the reference program's by a relative error of at most 0.03.
Values may be sent and summed in bfloat16 or wider, within the bound.
No kernel may reach another device: no remote copies, remote signals or barrier semaphores. Data moves between devices by JAX's collectives and lax.ppermute only.
A program may use at most 128 MiB of HBM per device.

```python
import math
import jax
import jax.numpy as jnp
import numpy as np
from jax import lax

D = 768
HEADS = 12
HEAD_DIM = 64
FF = 3072
SEQS = 3
GROUP_TOK = 2048
GROUPS = 4
TOKENS = 8192


def steps_of(stream_key, dims, cuts, smallest, largest):
    def one(dim, blocks):
        steps = jax.random.uniform(jax.random.fold_in(jax.random.fold_in(stream_key, 6), dim), (blocks,), jnp.float32, smallest / len(cuts), largest / len(cuts))
        return jnp.repeat(jnp.exp(steps), dims[dim] // blocks).reshape((-1,) + (1,) * (len(dims) - dim - 1))

    loudness = one(*cuts[0])
    for cut in cuts[1:]:
        loudness = loudness * one(*cut)
    return loudness


def split_up(amount, total, reach, slope):
    weights = [(1 << 20) // math.isqrt(rank ** slope) + 1 for rank in range(2, amount + 1)]
    rest, holding = total - reach - (amount - 1), [1] * (amount - 1)
    while rest > 0:
        free = [i for i in range(amount - 1) if holding[i] < reach]
        mass, budget = sum([weights[i] for i in free]), rest
        for i in free:
            addition = min(reach - holding[i], max(1, budget * weights[i] // mass), rest)
            holding[i] = holding[i] + addition
            rest = rest - addition
    return np.array([reach] + holding)


def uneven(key, amount, total, bound, skew):
    if amount == 2:
        one = jax.random.randint(key, (), max(1, total - bound), min(bound, total - 1) + 1)
        return jnp.stack([one, total - one])
    sizes = jnp.asarray(split_up(amount, total, bound, skew), jnp.int32)
    twos = (amount - 1) // 2
    source_of, receiver = sizes[1:1 + 2 * twos:2], sizes[2:2 + 2 * twos:2]
    room = jnp.minimum(source_of - 1, bound - receiver)
    passed = jax.random.randint(jax.random.fold_in(key, 1), (twos,), 0, 1 << 20) % (room + 1)
    sizes = sizes.at[1:1 + 2 * twos:2].set(source_of - passed).at[2:2 + 2 * twos:2].set(receiver + passed)
    return sizes[jax.random.permutation(jax.random.fold_in(key, 2), amount)]


def centred(key, shape, deviation, limit, pieces=(), kind=jnp.bfloat16):
    drawn = jax.random.normal(key, shape, jnp.float32) * deviation
    if len(pieces) > 0:
        drawn = steps_of(key, shape, pieces, -0.22, 0.18) * drawn
    return jnp.clip(drawn, min=-limit, max=limit).astype(kind)


def setup_inputs(seed: int = 0) -> dict:
    streams_of = jax.random.split(jax.random.key(seed), 20)
    return {
        "tokens": centred(streams_of[0], (TOKENS, D), 1.0, 6.0, ((0, 16),)),
        "out_grad": centred(streams_of[1], (TOKENS, D), 1.0, 6.0, ((0, 16),)),
        "lengths": jax.vmap(lambda own: uneven(own, SEQS, GROUP_TOK, GROUP_TOK // 2, 2))(jax.random.split(streams_of[2], GROUPS)).reshape((GROUPS, SEQS)).astype(jnp.int32),
        "query_weight": centred(streams_of[3], (D, D), D ** -0.5, 0.21875, ((1, 2),)),
        "query_bias": centred(streams_of[4], (D,), 0.5, 3.0, ((0, 2),), jnp.float32),
        "key_weight": centred(streams_of[5], (D, D), D ** -0.5, 0.21875, ((1, 2),)),
        "key_bias": centred(streams_of[6], (D,), 0.5, 3.0, ((0, 2),), jnp.float32),
        "value_weight": centred(streams_of[7], (D, D), D ** -0.5, 0.21875, ((1, 2),)),
        "value_bias": centred(streams_of[8], (D,), 0.5, 3.0, ((0, 2),), jnp.float32),
        "output_weight": centred(streams_of[9], (D, D), (D // 16) ** -0.5, 0.875, ((0, 2),)),
        "output_bias": centred(streams_of[10], (D,), 0.5, 3.0, (), jnp.float32),
        "first_gain": jnp.clip(1.0 + 0.1 * jax.random.normal(streams_of[11], (D,), jnp.float32), 0.5, 1.5),
        "first_shift": centred(streams_of[12], (D,), 0.5, 3.0, (), jnp.float32),
        "inner_weight": centred(streams_of[13], (D, FF), D ** -0.5, 0.21875, ((1, 2),)),
        "inner_bias": centred(streams_of[14], (FF,), 0.5, 3.0, ((0, 2),), jnp.float32),
        "outer_weight": centred(streams_of[15], (FF, D), FF ** -0.5, 0.109375, ((0, 2),)),
        "outer_bias": centred(streams_of[16], (D,), 0.5, 3.0, (), jnp.float32),
        "second_gain": jnp.clip(1.0 + 0.1 * jax.random.normal(streams_of[17], (D,), jnp.float32), 0.5, 1.5),
        "second_shift": centred(streams_of[18], (D,), 0.5, 3.0, (), jnp.float32),
    }


MASKED = -1e+30
EPSILON = 1e-06
HIGHEST = lax.Precision.HIGHEST

@jax.custom_vjp
def low(v):
    return lax.optimization_barrier(v.astype(jnp.bfloat16)).astype(jnp.float32)

@jax.custom_vjp
def low_back(v):
    return v

def low_keep(v):
    return (low(v), None)

def low_pass(kept, grad):
    return (grad,)

def back_keep(v):
    return (v, None)

def back_low(kept, grad):
    return (low(grad),)
low.defvjp(low_keep, low_pass)
low_back.defvjp(back_keep, back_low)

def product(left_side, right_side):
    return jnp.dot(left_side, right_side, precision=HIGHEST)

def rope_tables(position, head_width):
    half_dim = head_width // 2
    frequency = jnp.power(10000.0, -2.0 * jnp.arange(half_dim, dtype=jnp.float32) / head_width)
    angles = position.astype(jnp.float32)[:, None] * frequency[None, :]
    return (jnp.cos(angles), jnp.sin(angles))

def rotate(vector, cosine_table, sine_table):
    half_dim = vector.shape[-1] // 2
    front_half = vector[..., :half_dim]
    back_half = vector[..., half_dim:]
    cosine = cosine_table[:, None, :]
    sine_part = sine_table[:, None, :]
    return jnp.concatenate([front_half * cosine - back_half * sine_part, front_half * sine_part + back_half * cosine], axis=-1)

def layout(lengths_row, row_index):
    ends = jnp.cumsum(lengths_row).astype(jnp.int32)
    starts = (ends - lengths_row).astype(jnp.int32)
    segment = lax.optimization_barrier(jnp.sum((row_index[:, None] >= ends[None, :]).astype(jnp.int32), axis=1)).astype(jnp.int32)
    member = segment[:, None] == jnp.arange(lengths_row.shape[0], dtype=jnp.int32)[None, :]
    position = (row_index - lax.optimization_barrier(jnp.sum(jnp.where(member, starts[None, :], 0), axis=1))).astype(jnp.int32)
    return (segment, position)

def layer_norm(rows_in, gain_vec, shift_vec):
    row_mean = lax.optimization_barrier(jnp.mean(rows_in, axis=-1, keepdims=True))
    centered = rows_in - row_mean
    inverse = lax.rsqrt(lax.optimization_barrier(jnp.mean(centered * centered, axis=-1, keepdims=True)) + EPSILON)
    return centered * inverse * gain_vec + shift_vec

def group_layer(group_rows, lengths_row, weights):
    query_weight, query_bias, key_weight, key_bias, value_weight, value_bias, output_weight, output_bias, first_gain, first_shift, inner_weight, inner_bias, outer_weight, outer_bias, second_gain, second_shift = weights
    row_index = jnp.arange(GROUP_TOK, dtype=jnp.int32)
    segment, position = layout(lengths_row, row_index)
    cosine_table, sine_table = rope_tables(position, HEAD_DIM)
    query_pre = low_back(product(group_rows, query_weight) + query_bias).reshape(GROUP_TOK, HEADS, HEAD_DIM)
    key_pre = low_back(product(group_rows, key_weight) + key_bias).reshape(GROUP_TOK, HEADS, HEAD_DIM)
    value_pre = low_back(product(group_rows, value_weight) + value_bias).reshape(GROUP_TOK, HEADS, HEAD_DIM)
    queries = low(rotate(query_pre, cosine_table, sine_table))
    key_rows = low(rotate(key_pre, cosine_table, sine_table))
    values = low(value_pre)
    block_rows = min(512, GROUP_TOK)
    block_count = GROUP_TOK // block_rows

    def attend(inputs):
        query_block, query_index, query_segment = inputs
        scores = low_back(jnp.einsum('qhd,khd->hqk', query_block, key_rows, precision=HIGHEST) * 0.125)
        allowed = (query_segment[:, None] == segment[None, :]) & (row_index[None, :] <= query_index[:, None])
        attn_prob = jax.nn.softmax(jnp.where(allowed[None], scores, MASKED), axis=-1)
        return jnp.einsum('hqk,khd->qhd', low(attn_prob), values, precision=HIGHEST)
    attended = lax.map(jax.checkpoint(attend), (queries.reshape(block_count, block_rows, HEADS, HEAD_DIM), row_index.reshape(block_count, block_rows), segment.reshape(block_count, block_rows)))
    attended = low(low_back(attended.reshape(GROUP_TOK, D)))
    attn_out = low_back(product(attended, output_weight) + output_bias)
    first = layer_norm(group_rows + attn_out, first_gain, first_shift)
    pre_act = low_back(product(low(first), inner_weight) + inner_bias)
    hidden = low(jax.nn.gelu(pre_act, approximate=False))
    ffn = low_back(product(hidden, outer_weight) + outer_bias)
    return layer_norm(first + ffn, second_gain, second_shift)

def reference(tokens, out_grad, lengths, query_weight, query_bias, key_weight, key_bias, value_weight, value_bias, output_weight, output_bias, first_gain, first_shift, inner_weight, inner_bias, outer_weight, outer_bias, second_gain, second_shift):
    weights = tuple((item.astype(jnp.float32) for item in (query_weight, query_bias, key_weight, key_bias, value_weight, value_bias, output_weight, output_bias, first_gain, first_shift, inner_weight, inner_bias, outer_weight, outer_bias, second_gain, second_shift)))
    inputs32 = tokens.astype(jnp.float32)

    def forward(rows_all, *layer_weights):

        def layer_step(running, group_data):
            return (running, jax.checkpoint(group_layer)(group_data[0], group_data[1], layer_weights))
        unused, results = lax.scan(layer_step, jnp.zeros((), jnp.float32), (rows_all.reshape(GROUPS, GROUP_TOK, D), lengths))
        return results.reshape(TOKENS, D)
    result, pullback = jax.vjp(forward, inputs32, *weights)
    gradients = pullback(out_grad.astype(jnp.float32))
    return (result.astype(jnp.bfloat16), gradients[0].astype(jnp.bfloat16), gradients[1], gradients[2], gradients[3], gradients[4], gradients[5], gradients[6], gradients[7], gradients[8], gradients[9], gradients[10], gradients[11], gradients[12], gradients[13], gradients[14], gradients[15], gradients[16])
```

```python
import functools

import jax
import jax.numpy as jnp
import numpy as np
from jax import lax
from jax.experimental import pallas as pl
from jax.experimental.pallas import tpu as pltpu
from jax.sharding import PartitionSpec as P

HEAD_DIM = 64
PAIR = 2 * HEAD_DIM
MASKED = -1e30
EPSILON = 1e-06
TILE = 256
F32 = jnp.float32
BF16 = jnp.bfloat16
VMEM_BYTES = 56 * 1024 * 1024

NN = (((1,), (0,)), ((), ()))
NT = (((1,), (1,)), ((), ()))
TN = (((0,), (0,)), ((), ()))


def dot(left, right, dims=NN):
    return lax.dot_general(left, right, dims, preferred_element_type=F32)


def call(kernel, grid, in_specs, out_specs, out_shape, scratch=(), flops=0, bytes_accessed=0, scalars=0):
    return pl.pallas_call(
        kernel,
        grid_spec=pltpu.PrefetchScalarGridSpec(
            num_scalar_prefetch=scalars,
            grid=grid,
            in_specs=in_specs,
            out_specs=out_specs,
            scratch_shapes=scratch,
        ),
        out_shape=out_shape,
        compiler_params=pltpu.CompilerParams(vmem_limit_bytes=VMEM_BYTES),
        cost_estimate=pl.CostEstimate(
            flops=int(flops), bytes_accessed=int(bytes_accessed), transcendentals=0
        ),
    )


def whole(shape):
    return pl.BlockSpec(shape, lambda *_: (0,) * len(shape))


def columns(rows, width, scale=1, shift=0):
    return pl.BlockSpec((rows, width), lambda p, *_: (0, scale * p + shift))


def rowblock(height, width):
    return pl.BlockSpec((height, width), lambda p, *_: (p, 0))


def swap_halves(value):
    lane = lax.broadcasted_iota(jnp.int32, value.shape, 1)
    ahead = pltpu.roll(value, PAIR - HEAD_DIM // 2, 1)
    behind = pltpu.roll(value, HEAD_DIM // 2, 1)
    return jnp.where(lane % HEAD_DIM < HEAD_DIM // 2, ahead, behind)


def project_kernel(
    info, tokens, wq, wk, wv, bias, base_cos, base_sin, freq, q_out, kv_out, cos_out, sin_out
):
    rows = tokens.shape[0]

    @pl.when(pl.program_id(0) == 0)
    def _():
        offset, end0, end1 = info[0], info[1], info[2]
        row = offset + lax.broadcasted_iota(jnp.int32, (rows, 1), 0)
        turns = []
        for start in (0, end0, end1):
            angle = (offset - start).astype(F32) * freq[...]
            turns.append((jnp.cos(angle), jnp.sin(angle)))
        late, later = row >= end0, row >= end1
        cos_turn = jnp.where(later, turns[2][0], jnp.where(late, turns[1][0], turns[0][0]))
        sin_turn = jnp.where(later, turns[2][1], jnp.where(late, turns[1][1], turns[0][1]))
        cosine = base_cos[...] * cos_turn - base_sin[...] * sin_turn
        sine = base_sin[...] * cos_turn + base_cos[...] * sin_turn
        lane = lax.broadcasted_iota(jnp.int32, (rows, PAIR), 1)
        cos_out[...] = cosine
        sin_out[...] = jnp.where(lane % HEAD_DIM < HEAD_DIM // 2, -sine, sine)

    weight = jnp.concatenate([wq[...], wk[...], wv[...]], axis=1)
    pre = dot(tokens[...], weight)
    cosine, sine = cos_out[...], sin_out[...]
    query = pre[:, :PAIR] + bias[0:1, :]
    key = pre[:, PAIR : 2 * PAIR] + bias[1:2, :]
    q_out[...] = (query * cosine + swap_halves(query) * sine).astype(BF16)
    kv_out[:, :PAIR] = (key * cosine + swap_halves(key) * sine).astype(BF16)
    kv_out[:, PAIR:] = (pre[:, 2 * PAIR :] + bias[2:3, :]).astype(BF16)


def start_of(index, end0, end1):
    return jnp.where(index >= end1, end1, jnp.where(index >= end0, end0, 0))


def needed(info, query_row, key_row):
    end0, end1, span = info[1], info[2], info[3]
    return (
        (key_row <= query_row + TILE - 1)
        & (key_row + TILE - 1 >= start_of(query_row, end0, end1))
        & (query_row < span)
        & (key_row >= 0)
    )


def allowed(info, query_row, key_row):
    query = query_row + lax.broadcasted_iota(jnp.int32, (1, TILE), 1)
    key = key_row + lax.broadcasted_iota(jnp.int32, (TILE, 1), 0)
    return (key >= start_of(query, info[1], info[2])) & (key <= query)


def head_mask(shape, head):
    lane = lax.broadcasted_iota(jnp.int32, shape, 1)
    return (lane // HEAD_DIM) == head


def tile(index):
    return pl.ds(pl.multiple_of(index * TILE, TILE), TILE)


def attend_kernel(
    info, q, kv_own, kv_mate, kv_far, kv_cross, wo,
    low_out, high_out, lse_out, part_out, q_masked, peak, total, accum, attn_sum,
):
    rows = q.shape[0]
    tiles = rows // TILE
    offset = info[0]
    step = pl.program_id(0)
    for head in range(2):
        q_masked[head] = jnp.where(head_mask(q.shape, head), q[...] * 0.125, 0).astype(BF16)

    def visit(kv, query_tile, key_tile, query_row, key_row, first):
        mask = allowed(info, query_row, key_row)
        keys = kv[tile(key_tile), :PAIR]
        values = kv[tile(key_tile), PAIR:]
        for head in range(2):
            lanes = tile(query_tile)
            scores = dot(keys, q_masked[head, tile(query_tile), :], NT)
            scores = jnp.where(mask, scores, MASKED)
            top = jnp.max(scores, axis=0, keepdims=True)
            if first:
                prob = jnp.exp(scores - top)
                total[head : head + 1, lanes] = jnp.sum(prob, axis=0, keepdims=True)
                accum[head, :, lanes] = dot(values, prob.astype(BF16), TN)
                peak[head : head + 1, lanes] = top
            else:
                old = peak[head : head + 1, lanes]
                top = jnp.maximum(old, top)
                decay = jnp.exp(old - top)
                prob = jnp.exp(scores - top)
                total[head : head + 1, lanes] = total[
                    head : head + 1, lanes
                ] * decay + jnp.sum(prob, axis=0, keepdims=True)
                accum[head, :, lanes] = accum[head, :, lanes] * decay + dot(
                    values, prob.astype(BF16), TN
                )
                peak[head : head + 1, lanes] = top

    for query_tile in range(tiles):
        query_row = offset + query_tile * TILE
        visit(kv_own, query_tile, query_tile, query_row, query_row, True)
        for key_tile in range(query_tile):
            key_row = offset + key_tile * TILE

            @pl.when(needed(info, query_row, key_row))
            def _():
                visit(kv_own, query_tile, key_tile, query_row, key_row, False)

    for slot, kv in enumerate((kv_mate, kv_far, kv_cross)):
        for query_tile in range(tiles):
            for key_tile in range(tiles):
                query_row = offset + query_tile * TILE
                key_row = info[4 + slot] * rows + key_tile * TILE

                @pl.when((info[4 + slot] < info[0] // rows) & needed(info, query_row, key_row))
                def _():
                    visit(kv, query_tile, key_tile, query_row, key_row, False)

    for head in range(2):
        sums = total[head : head + 1, :]
        lse_out[0, head : head + 1, :] = peak[head : head + 1, :] + jnp.log(sums)
        high_out[HEAD_DIM * head : HEAD_DIM * (head + 1), :] = accum[
            head, HEAD_DIM * head : HEAD_DIM * (head + 1), :
        ] / sums
    low = high_out[...].T.astype(BF16)
    low_out[...] = low
    part = dot(low, wo[...])

    @pl.when(step == 0)
    def _():
        attn_sum[...] = part

    @pl.when(step > 0)
    def _():
        attn_sum[...] += part

    @pl.when(step == pl.num_programs(0) - 1)
    def _():
        part_out[...] = attn_sum[...].astype(BF16)


def mean(value):
    return jnp.mean(value, axis=-1, keepdims=True)


def normalize(rows_in):
    centered = rows_in - mean(rows_in)
    inverse = lax.rsqrt(mean(centered * centered) + EPSILON)
    return centered * inverse, inverse


def norm_back(grad, normed, inverse):
    return inverse * (grad - mean(grad) - normed * mean(grad * normed))


def forward_kernel(
    tokens, part, other, vectors, w_in, b_in, w_out,
    normed_out, inverse_out, first_out, hidden_out, slope_out, part_out, accum,
):
    step = pl.program_id(0)

    @pl.when(step == 0)
    def _():
        attn = part[...].astype(F32) + other[...].astype(F32) + vectors[0:1, :]
        normed, inverse = normalize(tokens[...].astype(F32) + attn)
        normed_out[...] = normed
        inverse_out[...] = inverse
        first_out[...] = (normed * vectors[1:2, :] + vectors[2:3, :]).astype(BF16)

    pre = dot(first_out[...], w_in[...]) + b_in[...]
    cdf = 0.5 * (1.0 + lax.erf(pre * 0.7071067811865476))
    hidden = (pre * cdf).astype(BF16)
    hidden_out[...] = hidden
    slope_out[...] = (cdf + pre * (jnp.exp(-0.5 * pre * pre) * 0.3989422804014327)).astype(BF16)
    product = dot(hidden, w_out[...])

    @pl.when(step == 0)
    def _():
        accum[...] = product

    @pl.when(step > 0)
    def _():
        accum[...] += product

    @pl.when(step == pl.num_programs(0) - 1)
    def _():
        part_out[...] = accum[...].astype(BF16)


def backward_kernel(
    normed_first, part, other, out_grad, vectors, slope, w_in, w_out,
    layer_out, ffn_grad_out, pre_grad_out, part_out, res_out, sums_out, inner_out, accum,
):
    step = pl.program_id(0)

    @pl.when(step == 0)
    def _():
        first = normed_first[...] * vectors[1:2, :] + vectors[2:3, :]
        ffn = part[...].astype(F32) + other[...].astype(F32) + vectors[3:4, :]
        normed, inverse = normalize(first + ffn)
        layer_out[...] = (normed * vectors[4:5, :] + vectors[5:6, :]).astype(BF16)
        upstream = out_grad[...].astype(F32)
        res_grad = norm_back(upstream * vectors[4:5, :], normed, inverse)
        ffn_grad = res_grad.astype(BF16)
        res_out[...] = res_grad
        ffn_grad_out[...] = ffn_grad
        sums_out[...] = jnp.zeros_like(sums_out)
        sums_out[0:1, :] = jnp.sum(upstream * normed, axis=0, keepdims=True)
        sums_out[1:2, :] = jnp.sum(upstream, axis=0, keepdims=True)
        sums_out[2:3, :] = jnp.sum(ffn_grad.astype(F32), axis=0, keepdims=True)

    hidden_grad = dot(ffn_grad_out[...], w_out[...], NT)
    pre_grad = (hidden_grad * slope[...].astype(F32)).astype(BF16)
    pre_grad_out[...] = pre_grad
    inner_out[...] = jnp.sum(pre_grad.astype(F32), axis=0, keepdims=True)
    product = dot(pre_grad, w_in[...], NT)

    @pl.when(step == 0)
    def _():
        accum[...] = product

    @pl.when(step > 0)
    def _():
        accum[...] += product

    @pl.when(step == pl.num_programs(0) - 1)
    def _():
        part_out[...] = accum[...].astype(BF16)


def middle_kernel(
    res_second, part, other, normed, inverse, vectors, wo, high,
    res_out, grad_out, head_out, dot_out, sums_out,
):
    first_grad = res_second[...] + part[...].astype(F32) + other[...].astype(F32)
    unit = normed[...]
    res_grad = norm_back(first_grad * vectors[1:2, :], unit, inverse[...])
    attn_grad = res_grad.astype(BF16)
    res_out[...] = res_grad
    grad_out[...] = attn_grad
    sums_out[...] = jnp.zeros_like(sums_out)
    sums_out[0:1, :] = jnp.sum(first_grad * unit, axis=0, keepdims=True)
    sums_out[1:2, :] = jnp.sum(first_grad, axis=0, keepdims=True)
    sums_out[2:3, :] = jnp.sum(attn_grad.astype(F32), axis=0, keepdims=True)
    head_out[...] = dot(attn_grad, wo[...], NT).astype(BF16)
    turned = dot(wo[...], attn_grad, NT).astype(BF16).astype(F32) * high[...]
    for head in range(wo.shape[0] // HEAD_DIM):
        dot_out[head // 2, head % 2, :] = jnp.sum(
            turned[HEAD_DIM * head : HEAD_DIM * (head + 1), :], axis=0
        )


def attend_back_kernel(
    info, q, grad, kv_own, lse, rowdot, kv_mate, kv_far, kv_cross,
    q_mate, q_far, q_cross, grad_mate, grad_far, grad_cross,
    lse_mate, lse_far, lse_cross, rowdot_mate, rowdot_far, rowdot_cross,
    tokens, wq, wk, wv, cosine, sine,
    q_grad_out, k_grad_out, v_grad_out, bias_out, part_out,
    q_masked, grad_masked, k_masked, v_masked, q_turned, k_turned, v_sum, tokens_turned, accum,
):
    rows = q.shape[0]
    tiles = rows // TILE
    offset = info[0]
    me = offset // rows
    step = pl.program_id(0)

    @pl.when(step == 0)
    def _():
        tokens_turned[...] = tokens[...].T

    for head in range(2):
        mask = head_mask(q.shape, head)
        q_masked[head] = jnp.where(mask, q[...] * 0.125, 0).astype(BF16)
        grad_masked[head] = jnp.where(mask, grad[...], 0).astype(BF16)
        k_masked[head] = jnp.where(mask, kv_own[:, :PAIR] * 0.125, 0).astype(BF16)
        v_masked[head] = jnp.where(mask, kv_own[:, PAIR:], 0).astype(BF16)
    q_turned[...] = jnp.zeros_like(q_turned)
    k_turned[...] = jnp.zeros_like(k_turned)
    v_sum[...] = jnp.zeros_like(v_sum)

    def pair_terms(keys, values, queries, grads, mask, log_row, dot_row):
        scores = jnp.where(mask, dot(keys, queries, NT), MASKED)
        prob = jnp.exp(scores - log_row)
        prob_grad = dot(values, grads, NT)
        return prob.astype(BF16), (prob * (prob_grad - dot_row)).astype(BF16)

    def visit_queries(kv, query_tile, key_tile, query_row, key_row, own):
        mask = allowed(info, query_row, key_row)
        lanes = tile(query_tile)
        keys = kv[tile(key_tile), :PAIR]
        values = kv[tile(key_tile), PAIR:]
        for head in range(2):
            prob, score_grad = pair_terms(
                keys, values, q_masked[head, lanes, :], grad_masked[head, lanes, :], mask,
                lse[0, head : head + 1, lanes], rowdot[0, head : head + 1, lanes],
            )
            span = slice(HEAD_DIM * head, HEAD_DIM * (head + 1))
            q_turned[span, lanes] += dot(keys, score_grad, TN)[span, :]
            if own:
                k_turned[head, tile(key_tile), :] += dot(score_grad, q[lanes, :])
                v_sum[head, tile(key_tile), :] += dot(prob, grad[lanes, :])

    def visit_keys(queries, grads, logs, dots, query_tile, key_tile, query_row, key_row):
        mask = allowed(info, query_row, key_row)
        lanes = tile(query_tile)
        for head in range(2):
            prob, score_grad = pair_terms(
                k_masked[head, tile(key_tile), :], v_masked[head, tile(key_tile), :],
                queries[lanes, :], grads[lanes, :], mask,
                logs[0, head : head + 1, lanes], dots[0, head : head + 1, lanes],
            )
            k_turned[head, tile(key_tile), :] += dot(score_grad, queries[lanes, :])
            v_sum[head, tile(key_tile), :] += dot(prob, grads[lanes, :])

    for query_tile in range(tiles):
        for key_tile in range(query_tile + 1):
            query_row = offset + query_tile * TILE
            key_row = offset + key_tile * TILE

            @pl.when(needed(info, query_row, key_row))
            def _():
                visit_queries(kv_own, query_tile, key_tile, query_row, key_row, True)

    for slot, kv in enumerate((kv_mate, kv_far, kv_cross)):
        for query_tile in range(tiles):
            for key_tile in range(tiles):
                query_row = offset + query_tile * TILE
                key_row = info[4 + slot] * rows + key_tile * TILE

                @pl.when((info[4 + slot] < me) & needed(info, query_row, key_row))
                def _():
                    visit_queries(kv, query_tile, key_tile, query_row, key_row, False)

    later = (
        (q_mate, grad_mate, lse_mate, rowdot_mate),
        (q_far, grad_far, lse_far, rowdot_far),
        (q_cross, grad_cross, lse_cross, rowdot_cross),
    )
    for slot, (queries, grads, logs, dots) in enumerate(later):
        for key_tile in range(tiles):
            for query_tile in range(tiles):
                query_row = info[7 + slot] * rows + query_tile * TILE
                key_row = offset + key_tile * TILE

                @pl.when((info[7 + slot] > me) & needed(info, query_row, key_row))
                def _():
                    visit_keys(
                        queries, grads, logs, dots, query_tile, key_tile, query_row, key_row
                    )

    first_head = head_mask(q.shape, 0)
    cosines, sines = cosine[...], sine[...]

    def turn_back(value):
        return (value * cosines - swap_halves(value) * sines).astype(BF16)

    q_grad = turn_back(q_turned[...].T * 0.125)
    k_grad = turn_back(jnp.where(first_head, k_turned[0], k_turned[1]) * 0.125)
    v_grad = jnp.where(first_head, v_sum[0], v_sum[1]).astype(BF16)
    bias_out[...] = jnp.zeros_like(bias_out)
    for index, value in enumerate((q_grad, k_grad, v_grad)):
        bias_out[index : index + 1, :] = jnp.sum(value.astype(F32), axis=0, keepdims=True)
    together = jnp.concatenate([q_grad, k_grad, v_grad], axis=1)
    weight_grad = dot(tokens_turned[...], together).astype(BF16)
    q_grad_out[...] = weight_grad[:, :PAIR]
    k_grad_out[...] = weight_grad[:, PAIR : 2 * PAIR]
    v_grad_out[...] = weight_grad[:, 2 * PAIR :]
    weights = jnp.concatenate([wq[...], wk[...], wv[...]], axis=1)
    part = dot(together, weights, NT)

    @pl.when(step == 0)
    def _():
        accum[...] = part

    @pl.when(step > 0)
    def _():
        accum[...] += part

    @pl.when(step == pl.num_programs(0) - 1)
    def _():
        part_out[...] = accum[...].astype(BF16)


def left_contract(left_side, right_side):
    return jnp.einsum("ti,tj->ij", left_side, right_side, preferred_element_type=F32)


def exchange_stages(ctx_size, dp_size):
    def bits(axis, size):
        return [(axis, 1 << i) for i in range((size - 1).bit_length())]

    ctx, dp = bits("ctx", ctx_size), bits("dp", dp_size)
    return ctx[:1] + ctx[1:] + dp, ctx[:1] + dp + ctx[1:]


def flip(value, axis, bit):
    size = lax.axis_size(axis)
    return lax.ppermute(value, axis, [(i, i ^ bit) for i in range(size)])


def set_bit(axis, bit):
    return (lax.axis_index(axis) & bit) != 0


def sum_everywhere(value, stages):
    for axis, bit in stages:
        half = value.shape[0] // 2
        upper = set_bit(axis, bit).astype(jnp.int32)
        send = lax.dynamic_slice_in_dim(value, (1 - upper) * half, half, 0)
        keep = lax.dynamic_slice_in_dim(value, upper * half, half, 0)
        received = flip(send, axis, bit)
        value = (keep.astype(F32) + received.astype(F32)).astype(value.dtype)
    for axis, bit in reversed(stages):
        received = flip(value, axis, bit)
        upper = set_bit(axis, bit)
        value = jnp.where(
            upper,
            jnp.concatenate([received, value], axis=0),
            jnp.concatenate([value, received], axis=0),
        )
    return value


def per_device(
    tokens, out_grad, lengths, query_weight, query_bias, key_weight, key_bias, value_weight,
    value_bias, output_weight, output_bias, first_gain, first_shift, inner_weight, inner_bias,
    outer_weight, outer_bias, second_gain, second_shift,
):
    rows, width = tokens.shape
    local = query_weight.shape[1]
    pairs = local // PAIR
    hidden_width = inner_weight.shape[1]
    ctx_size, dp_size = lax.axis_size("ctx"), lax.axis_size("dp")
    me = lax.axis_index("ctx")
    mate = me ^ 1
    info = jnp.stack(
        [
            me * rows, lengths[0, 0], lengths[0, 0] + lengths[0, 1],
            jnp.int32(ctx_size * rows), mate, me - 2, mate - 2, mate, me + 2, mate + 2,
        ]
    ).astype(jnp.int32)

    frequency = 10000.0 ** (-2.0 * np.arange(HEAD_DIM // 2) / HEAD_DIM)
    lanes = np.tile(frequency, PAIR // (HEAD_DIM // 2))
    angles = np.arange(rows)[:, None] * lanes[None, :]
    base_cos = jnp.asarray(np.cos(angles), F32)
    base_sin = jnp.asarray(np.sin(angles), F32)
    bias = jnp.stack([query_bias, key_bias, value_bias])

    def shape(*dims, dtype=BF16):
        return jax.ShapeDtypeStruct(dims, dtype)

    queries, kv_own, cosine, sine = call(
        project_kernel,
        (pairs,),
        [
            whole((rows, width)), columns(width, PAIR), columns(width, PAIR), columns(width, PAIR),
            columns(3, PAIR), whole((rows, PAIR)), whole((rows, PAIR)), whole((1, PAIR)),
        ],
        [
            columns(rows, PAIR), columns(rows, 2 * PAIR), whole((rows, PAIR)), whole((rows, PAIR)),
        ],
        [
            shape(rows, local), shape(rows, 2 * local),
            shape(rows, PAIR, dtype=F32), shape(rows, PAIR, dtype=F32),
        ],
        flops=6 * rows * width * local,
        bytes_accessed=2 * (rows * width + 3 * width * local + 3 * rows * local),
        scalars=1,
    )(
        info, tokens, query_weight, key_weight, value_weight, bias, base_cos, base_sin,
        jnp.asarray(lanes[None, :], F32),
    )

    forward_pairs = [(i, i + 2) for i in range(ctx_size - 2)]
    backward_pairs = [(i + 2, i) for i in range(ctx_size - 2)]

    def spread(value, pairs_list):
        far = lax.ppermute(value, "ctx", pairs_list)
        return flip(value, "ctx", 1), far, flip(far, "ctx", 1)

    kv_mate, kv_far, kv_cross = spread(kv_own, forward_pairs)

    stat = pl.BlockSpec((1, 2, rows), lambda p, *_: (p, 0, 0))
    kv_spec = columns(rows, 2 * PAIR)
    pair_spec = columns(rows, PAIR)
    low, high, lse, attn_part = call(
        attend_kernel,
        (pairs,),
        [pair_spec, kv_spec, kv_spec, kv_spec, kv_spec, rowblock(PAIR, width)],
        [pair_spec, rowblock(PAIR, rows), stat, whole((rows, width))],
        [
            shape(rows, local), shape(local, rows, dtype=F32),
            shape(pairs, 2, rows, dtype=F32), shape(rows, width),
        ],
        scratch=[
            pltpu.VMEM((2, rows, PAIR), BF16), pltpu.VMEM((2, rows), F32),
            pltpu.VMEM((2, rows), F32), pltpu.VMEM((2, PAIR, rows), F32),
            pltpu.VMEM((rows, width), F32),
        ],
        flops=4 * rows * 2 * rows * local,
        bytes_accessed=12 * rows * local,
        scalars=1,
    )(info, queries, kv_own, kv_mate, kv_far, kv_cross, output_weight)

    q_mate, q_far, q_cross = spread(queries, backward_pairs)
    lse_mate, lse_far, lse_cross = spread(lse, backward_pairs)

    def swap(value):
        return flip(value, "tensor", 1)

    vectors = jnp.stack(
        [output_bias, first_gain, first_shift, outer_bias, second_gain, second_shift]
    )
    unit = hidden_width // 3
    row_spec = whole((rows, width))
    vec_spec = whole((6, width))
    attn_other = swap(attn_part)
    normed_first, inverse_first, first_low, hidden, slope, ffn_part = call(
        forward_kernel,
        (3,),
        [
            row_spec, row_spec, row_spec, vec_spec, columns(width, unit), columns(1, unit),
            rowblock(unit, width),
        ],
        [
            row_spec, whole((rows, 1)), row_spec, columns(rows, unit), columns(rows, unit),
            row_spec,
        ],
        [
            shape(rows, width, dtype=F32), shape(rows, 1, dtype=F32), shape(rows, width),
            shape(rows, hidden_width), shape(rows, hidden_width), shape(rows, width),
        ],
        scratch=[pltpu.VMEM((rows, width), F32)],
        flops=4 * rows * width * hidden_width,
        bytes_accessed=4 * width * hidden_width + 8 * rows * hidden_width,
    )(
        tokens, attn_part, attn_other, vectors, inner_weight, inner_bias[None, :], outer_weight
    )

    ffn_other = swap(ffn_part)
    layer_out, ffn_grad, pre_grad, first_part, res_second, second_sums, inner_sums = call(
        backward_kernel,
        (3,),
        [
            row_spec, row_spec, row_spec, row_spec, vec_spec, columns(rows, unit),
            columns(width, unit), rowblock(unit, width),
        ],
        [
            row_spec, row_spec, columns(rows, unit), row_spec, row_spec, whole((8, width)),
            columns(1, unit),
        ],
        [
            shape(rows, width), shape(rows, width), shape(rows, hidden_width),
            shape(rows, width), shape(rows, width, dtype=F32), shape(8, width, dtype=F32),
            shape(1, hidden_width, dtype=F32),
        ],
        scratch=[pltpu.VMEM((rows, width), F32)],
        flops=4 * rows * width * hidden_width,
        bytes_accessed=4 * width * hidden_width + 8 * rows * hidden_width,
    )(
        normed_first, ffn_part, ffn_other, out_grad, vectors, slope, inner_weight, outer_weight
    )

    first_other = swap(first_part)
    x_first, z_first = exchange_stages(ctx_size, dp_size)
    outer_weight_grad = sum_everywhere(left_contract(hidden, ffn_grad).astype(BF16), x_first)
    inner_weight_grad = sum_everywhere(left_contract(first_low, pre_grad).astype(BF16), z_first)

    res_first, attn_grad, head_grad, rowdot, first_sums = call(
        middle_kernel,
        (1,),
        [
            row_spec, row_spec, row_spec, row_spec, whole((rows, 1)), vec_spec,
            whole((local, width)), whole((local, rows)),
        ],
        [
            row_spec, row_spec, whole((rows, local)), whole((pairs, 2, rows)), whole((8, width)),
        ],
        [
            shape(rows, width, dtype=F32), shape(rows, width), shape(rows, local),
            shape(pairs, 2, rows, dtype=F32), shape(8, width, dtype=F32),
        ],
        flops=4 * rows * width * local,
        bytes_accessed=20 * rows * width,
    )(
        res_second, first_part, first_other, normed_first, inverse_first, vectors,
        output_weight, high,
    )

    grad_mate, grad_far, grad_cross = spread(head_grad, backward_pairs)
    rowdot_mate, rowdot_far, rowdot_cross = spread(rowdot, backward_pairs)

    q_weight_grad, k_weight_grad, v_weight_grad, bias_sums, input_part = call(
        attend_back_kernel,
        (pairs,),
        [pair_spec, pair_spec, kv_spec, stat, stat]
        + [kv_spec] * 3
        + [pair_spec] * 6
        + [stat] * 6
        + [whole((rows, width))]
        + [columns(width, PAIR)] * 3
        + [whole((rows, PAIR))] * 2,
        [columns(width, PAIR)] * 3 + [columns(8, PAIR), whole((rows, width))],
        [shape(width, local)] * 3 + [shape(8, local, dtype=F32), shape(rows, width)],
        scratch=[
            pltpu.VMEM((2, rows, PAIR), BF16), pltpu.VMEM((2, rows, PAIR), BF16),
            pltpu.VMEM((2, rows, PAIR), BF16), pltpu.VMEM((2, rows, PAIR), BF16),
            pltpu.VMEM((PAIR, rows), F32), pltpu.VMEM((2, rows, PAIR), F32),
            pltpu.VMEM((2, rows, PAIR), F32), pltpu.VMEM((width, rows), BF16),
            pltpu.VMEM((rows, width), F32),
        ],
        flops=10 * rows * 2 * rows * local,
        bytes_accessed=40 * rows * local,
        scalars=1,
    )(
        info, queries, head_grad, kv_own, lse, rowdot, kv_mate, kv_far, kv_cross,
        q_mate, q_far, q_cross, grad_mate, grad_far, grad_cross,
        lse_mate, lse_far, lse_cross, rowdot_mate, rowdot_far, rowdot_cross,
        tokens, query_weight, key_weight, value_weight, cosine, sine,
    )

    input_other = swap(input_part)
    output_weight_grad = sum_everywhere(left_contract(low, attn_grad).astype(BF16), x_first)
    qk_weight_grad = sum_everywhere(
        jnp.concatenate([q_weight_grad, k_weight_grad], axis=1), x_first
    )
    v_weight_grad = sum_everywhere(v_weight_grad, z_first)
    input_grad = (res_first + input_part.astype(F32) + input_other.astype(F32)).astype(BF16)

    packed = jnp.concatenate(
        [
            second_sums[:3], first_sums[:3], inner_sums.reshape(-1, width),
            jnp.pad(bias_sums[:3], ((0, 0), (0, width - local))),
        ],
        axis=0,
    )
    packed = jnp.pad(packed, ((0, -packed.shape[0] % 16), (0, 0)))
    for axis, bit in x_first:
        packed = packed + flip(packed, axis, bit)
    inner_rows = hidden_width // width
    last = 6 + inner_rows
    return (
        layer_out,
        input_grad,
        qk_weight_grad[:, :local].astype(F32),
        packed[last, :local],
        qk_weight_grad[:, local:].astype(F32),
        packed[last + 1, :local],
        v_weight_grad.astype(F32),
        packed[last + 2, :local],
        output_weight_grad.astype(F32),
        packed[5],
        packed[3],
        packed[4],
        inner_weight_grad.astype(F32),
        packed[6 : 6 + inner_rows].reshape(-1),
        outer_weight_grad.astype(F32),
        packed[2],
        packed[0],
        packed[1],
    )


def solution(mesh):
    rows_spec, column_spec, row_spec = P(("dp", "ctx"), None), P(None, "tensor"), P("tensor", None)
    return jax.shard_map(
        per_device,
        mesh=mesh,
        in_specs=(
            rows_spec, rows_spec, P("dp", None),
            column_spec, P("tensor"), column_spec, P("tensor"), column_spec, P("tensor"),
            row_spec, P(), P(), P(), column_spec, P("tensor"), row_spec, P(), P(), P(),
        ),
        out_specs=(
            rows_spec, rows_spec,
            column_spec, P("tensor"), column_spec, P("tensor"), column_spec, P("tensor"),
            row_spec, P(), P(), P(), column_spec, P("tensor"), row_spec, P(), P(), P(),
        ),
        check_vma=False,
    )
```

```python
import jax
import jax.numpy as jnp
import numpy as np
from jax import lax
from jax.experimental import pallas as pl
from jax.experimental.pallas import tpu as pltpu
from jax.sharding import PartitionSpec as P

HEAD_DIM = 64
PAIR = 2 * HEAD_DIM
MASKED = -1e30
EPSILON = 1e-06
TILE = 256
WIDE = 512
GRAD_ROWS = TILE + 48
F32 = jnp.float32
BF16 = jnp.bfloat16
VMEM_BYTES = 12 * 1024 * 1024
FINAL = pltpu.HBM

NN = (((1,), (0,)), ((), ()))
NT = (((1,), (1,)), ((), ()))
TN = (((0,), (0,)), ((), ()))


def dot(left, right, dims=NN):
    return lax.dot_general(left, right, dims, preferred_element_type=F32)


class Order:
    last = None


def call(kernel, inputs, outputs, scratch=(), scalars=0, hbm=0, cost=1.0, ordered=True, final=False):
    spaces = [pltpu.SMEM] * scalars + [pltpu.VMEM] * (len(inputs) - scalars - hbm)
    spaces += [pltpu.HBM] * hbm
    inputs = list(inputs)
    for index in range(len(inputs) - hbm, len(inputs)):
        inputs[index] = pltpu.with_memory_space_constraint(inputs[index], pltpu.HBM)
    body = kernel
    if ordered and Order.last is not None:
        count = len(inputs)
        inputs.append(Order.last)
        spaces.append(pl.ANY)

        def body(*refs):
            kernel(*refs[:count], *refs[count + 1 :])

    results = pl.pallas_call(
        body,
        in_specs=[pl.BlockSpec(memory_space=space) for space in spaces],
        out_specs=[pl.BlockSpec(memory_space=pltpu.VMEM)] * len(outputs),
        out_shape=[
            FINAL(dims, dtype) if final else jax.ShapeDtypeStruct(dims, dtype)
            for dims, dtype in outputs
        ],
        scratch_shapes=list(scratch),
        compiler_params=pltpu.CompilerParams(vmem_limit_bytes=VMEM_BYTES),
        cost_estimate=pl.CostEstimate(
            flops=int(cost * 3e10), bytes_accessed=int(cost * 1e13), transcendentals=0
        ),
    )(*inputs)
    if ordered:
        Order.last = results[0]
    return results


def tile(index):
    return pl.ds(index * TILE, TILE)


def sum_rows(value):
    return jnp.sum(value.astype(F32), axis=0, keepdims=True)


def mean(value):
    return jnp.mean(value, axis=-1, keepdims=True)


def normalize(rows_in):
    centered = rows_in - mean(rows_in)
    inverse = lax.rsqrt(mean(centered * centered) + EPSILON)
    return centered * inverse, inverse


def norm_back(grad, normed, inverse):
    return inverse * (grad - mean(grad) - normed * mean(grad * normed))


def swap_halves(value):
    lane = lax.broadcasted_iota(jnp.int32, value.shape, 1)
    ahead = pltpu.roll(value, PAIR - HEAD_DIM // 2, 1)
    behind = pltpu.roll(value, HEAD_DIM // 2, 1)
    return jnp.where(lane % HEAD_DIM < HEAD_DIM // 2, ahead, behind)


def head_mask(shape, head):
    lane = lax.broadcasted_iota(jnp.int32, shape, 1)
    return (lane // HEAD_DIM) == head


class Layout:
    def __init__(self, place, rows):
        self.me = place[0]
        self.rows = rows
        self.offset = self.me * rows
        self.end0 = place[3]
        self.end1 = self.end0 + place[4]

    def start(self, index):
        return jnp.where(
            index >= self.end1, self.end1, jnp.where(index >= self.end0, self.end0, 0)
        )

    def allowed(self, query_row, queries, key_row, keys):
        query = query_row + lax.broadcasted_iota(jnp.int32, (1, queries), 1)
        key = key_row + lax.broadcasted_iota(jnp.int32, (keys, 1), 0)
        return (key >= self.start(query)) & (key <= query)


def project_tables(place, table, cos_out, sin_out):
    rows = cos_out.shape[0]
    base_cos, base_sin, freq = table[:rows, :], table[rows : 2 * rows, :], table[2 * rows :, :]
    where = Layout(place, rows)
    row = where.offset + lax.broadcasted_iota(jnp.int32, (rows, 1), 0)
    turns = []
    for start in (0, where.end0, where.end1):
        angle = (where.offset - start).astype(F32) * freq
        turns.append((jnp.cos(angle)[0:1, :], jnp.sin(angle)[0:1, :]))
    late, later = row >= where.end0, row >= where.end1
    cos_turn = jnp.where(later, turns[2][0], jnp.where(late, turns[1][0], turns[0][0]))
    sin_turn = jnp.where(later, turns[2][1], jnp.where(late, turns[1][1], turns[0][1]))
    cosine = base_cos * cos_turn - base_sin * sin_turn
    sine = base_sin * cos_turn + base_cos * sin_turn
    lane = lax.broadcasted_iota(jnp.int32, (rows, PAIR), 1)
    cos_out[...] = cosine
    sin_out[...] = jnp.where(lane % HEAD_DIM < HEAD_DIM // 2, -sine, sine)


def project_pair(pair, place, tokens, wq, wk, wv, bq, bk, bv, cos, sin, own_out, far_out):
    span = slice(pair * PAIR, (pair + 1) * PAIR)
    cosine, sine = cos[...], sin[...]
    weight = jnp.concatenate([wq[:, span], wk[:, span], wv[:, span]], axis=1)
    pre = dot(tokens[...], weight)
    query = pre[:, :PAIR] + bq[span].reshape(1, PAIR)
    key = pre[:, PAIR : 2 * PAIR] + bk[span].reshape(1, PAIR)
    query = (query * cosine + swap_halves(query) * sine).astype(BF16)
    key = (key * cosine + swap_halves(key) * sine).astype(BF16)
    value = (pre[:, 2 * PAIR :] + bv[span].reshape(1, PAIR)).astype(BF16)
    own_out[:, :PAIR] = query
    own_out[:, PAIR : 2 * PAIR] = key
    own_out[:, 2 * PAIR :] = value
    onward = place[0] < place[1] // 2
    far_out[:, :PAIR] = jnp.where(onward, key, query)
    far_out[:, PAIR:] = jnp.where(onward, value, query)


def first_project_kernel(place, *refs):
    count = (len(refs) - 7) // 2
    sources, (own_out, far_out, cos_out, sin_out) = refs[:count + 1], refs[count + 1 : count + 5]
    copies, table, sems = refs[count + 5 : 2 * count + 5], refs[-2], refs[-1]
    moves = [
        pltpu.make_async_copy(source, target, sems.at[index])
        for index, (source, target) in enumerate(zip(sources, (table, *copies)))
    ]
    for move in moves:
        move.start()
    moves[0].wait()
    project_tables(place, table, cos_out, sin_out)
    for move in moves[1:]:
        move.wait()
    project_pair(0, place, *copies, cos_out, sin_out, own_out, far_out)


def project_kernel(pair):
    def kernel(place, tokens, wq, wk, wv, bq, bk, bv, cos, sin, own_out, far_out):
        project_pair(pair, place, tokens, wq, wk, wv, bq, bk, bv, cos, sin, own_out, far_out)

    return kernel


def attend_kernel(
    place, own, mate, far, cross,
    low_out, lse_out, high, q_masked, peak, total, accum,
):
    rows = own.shape[0]
    where = Layout(place, rows)
    turned_q = own[:, :PAIR].astype(F32).T * 0.125
    for head in range(2):
        other = slice(HEAD_DIM * (1 - head), HEAD_DIM * (2 - head))
        mine = slice(HEAD_DIM * head, HEAD_DIM * (head + 1))
        q_masked[head, mine, :] = turned_q[mine, :].astype(BF16)
        q_masked[head, other, :] = jnp.zeros((HEAD_DIM, rows), BF16)

    def visit(keys, values, key_row, first):
        turned = values.astype(F32).T.astype(BF16)
        for part in range(rows // WIDE):
            lanes = pl.ds(part * WIDE, WIDE)
            mask = where.allowed(where.offset + part * WIDE, WIDE, key_row, rows)
            for head in range(2):
                span = slice(HEAD_DIM * head, HEAD_DIM * (head + 1))
                scores = dot(keys, q_masked[head, :, lanes])
                scores = jnp.where(mask, scores, MASKED)
                top = jnp.max(scores, axis=0, keepdims=True)
                if not first:
                    old = peak[head : head + 1, lanes]
                    top = jnp.maximum(old, top)
                    decay = jnp.exp(old - top)
                prob = jnp.exp(scores - top)
                sums = jnp.sum(prob, axis=0, keepdims=True)
                product = dot(turned[span, :], prob.astype(BF16))
                if not first:
                    sums += total[head : head + 1, lanes] * decay
                    product += accum[span, lanes] * decay
                peak[head : head + 1, lanes] = top
                total[head : head + 1, lanes] = sums
                accum[span, lanes] = product

    visit(own[:, PAIR : 2 * PAIR], own[:, 2 * PAIR :], where.offset, True)
    first_start = where.start(where.offset)

    @pl.when(first_start < where.offset)
    def _():
        odd = (where.me & 1) == 1
        visit(
            jnp.where(odd, mate[:, PAIR : 2 * PAIR], cross[:, :PAIR]),
            jnp.where(odd, mate[:, 2 * PAIR :], cross[:, PAIR:]), where.offset - rows, False,
        )

    @pl.when(first_start < where.offset - rows)
    def _():
        visit(far[:, :PAIR], far[:, PAIR:], where.offset - 2 * rows, False)

    for head in range(2):
        sums = total[head : head + 1, :]
        lse_out[head : head + 1, :] = peak[head : head + 1, :] + jnp.log(sums)
        span = slice(HEAD_DIM * head, HEAD_DIM * (head + 1))
        high[span, :] = accum[span, :] / sums
    low_out[...] = high[...].T.astype(BF16)


def output_kernel(*refs):
    lows, wo, outs = refs[:3], refs[3], refs[4:]
    for index, out in enumerate(outs):
        low = jnp.concatenate([ref[tile(index), :] for ref in lows], axis=1)
        out[...] = dot(low, wo[...]).astype(BF16)


def forward_kernel(chunk, units):
    def kernel(
        tokens, part, other, bias, gain, shift, w_in, b_in, w_out,
        normed_out, inverse_out, first_out, hidden_out, slope_out, part_out,
    ):
        width = tokens.shape[1]
        attn = part[...].astype(F32) + other[...].astype(F32) + bias[...].reshape(1, width)
        normed, inverse = normalize(tokens[tile(chunk), :].astype(F32) + attn)
        normed_out[...] = normed.astype(BF16)
        inverse_out[...] = inverse
        first = normed * gain[...].reshape(1, width) + shift[...].reshape(1, width)
        first_low = first.astype(BF16)
        first_out[...] = first_low
        total = None
        unit = w_in.shape[1] // units
        for index in range(units):
            span = slice(index * unit, (index + 1) * unit)
            pre = dot(first_low, w_in[:, span]) + b_in[span].reshape(1, unit)
            cdf = 0.5 * (1.0 + lax.erf(pre * 0.7071067811865476))
            density = jnp.exp(-0.5 * pre * pre) * 0.3989422804014327
            hidden = (pre * cdf).astype(BF16)
            hidden_out[:, span] = hidden
            slope_out[:, span] = (cdf + pre * density).astype(BF16)
            product = dot(hidden, w_out[span, :])
            total = product if total is None else total + product
        part_out[...] = total.astype(BF16)

    return kernel


def backward_kernel(chunk, units):
    def kernel(
        normed_first, part, other, out_grad, first_gain, first_shift, bias, gain, shift,
        slope, w_in, w_out,
        layer_out, ffn_grad_out, pre_grad_out, part_out, sums_out, inner_out,
    ):
        width = part.shape[1]

        def row(ref):
            return ref[...].reshape(1, width)

        first = normed_first[...].astype(F32) * row(first_gain) + row(first_shift)
        ffn = part[...].astype(F32) + other[...].astype(F32) + row(bias)
        normed, inverse = normalize(first + ffn)
        layer_out[...] = (normed * row(gain) + row(shift)).astype(BF16)
        upstream = out_grad[tile(chunk), :].astype(F32)
        res_grad = norm_back(upstream * row(gain), normed, inverse)
        ffn_grad = res_grad.astype(BF16)
        ffn_grad_out[...] = ffn_grad
        sums_out[0:1, :] = sum_rows(upstream * normed)
        sums_out[1:2, :] = sum_rows(upstream)
        sums_out[2:3, :] = sum_rows(ffn_grad)
        total = None
        unit = w_in.shape[1] // units
        for index in range(units):
            span = slice(index * unit, (index + 1) * unit)
            hidden_grad = dot(ffn_grad, w_out[span, :], NT)
            pre_grad = (hidden_grad * slope[:, span].astype(F32)).astype(BF16)
            pre_grad_out[:, span] = pre_grad
            inner_out[0:1, span] = sum_rows(pre_grad)
            product = dot(pre_grad, w_in[:, span], NT)
            total = product if total is None else total + product
        part_out[...] = total.astype(BF16)

    return kernel


def split_three(value):
    high = value.astype(BF16)
    rest = value - high.astype(F32)
    middle = rest.astype(BF16)
    return high, middle, (rest - middle.astype(F32)).astype(BF16)


def middle_kernel(chunk):
    def kernel(
        ffn_grad, part, other, normed, inverse, gain, wo, high0, high1, high2, lse0, lse1, lse2,
        *rest,
    ):
        grad_out, head_out, sums_out, stats = rest[-4:]
        base = chunk * GRAD_ROWS
        if chunk:
            head_out[:base, :] = rest[0][...]
        width = part.shape[1]
        local = wo.shape[0]
        first_grad = (
            ffn_grad[...].astype(F32) + part[...].astype(F32) + other[...].astype(F32)
        )
        unit = normed[...].astype(F32)
        res_grad = norm_back(first_grad * gain[...].reshape(1, width), unit, inverse[...])
        attn_grad = res_grad.astype(BF16)
        grad_out[...] = attn_grad
        sums_out[0:1, :] = sum_rows(first_grad * unit)
        sums_out[1:2, :] = sum_rows(first_grad)
        sums_out[2:3, :] = sum_rows(attn_grad)
        head_grad = dot(attn_grad, wo[...], NT).astype(BF16)
        head_out[base : base + TILE, :] = head_grad
        high = jnp.concatenate([ref[:, tile(chunk)] for ref in (high0, high1, high2)], axis=0)
        turned = head_grad.astype(F32).T * high
        stats[...] = jnp.zeros_like(stats)
        for index, lse in enumerate((lse0, lse1, lse2)):
            stats[2 * index : 2 * index + 2, :] = lse[:, tile(chunk)]
        for head in range(local // HEAD_DIM):
            span = slice(HEAD_DIM * head, HEAD_DIM * (head + 1))
            stats[8 + head : 9 + head, :] = jnp.sum(turned[span, :], axis=0, keepdims=True)
        begin = base + TILE
        head_out[begin:, :] = jnp.zeros((GRAD_ROWS - TILE, local), BF16)
        for index, value in enumerate(split_three(stats[...])):
            head_out[begin + 16 * index : begin + 16 * (index + 1), :TILE] = value

    return kernel


def stat_rows(grad, chunk):
    begin = chunk * GRAD_ROWS + TILE
    pieces = [
        grad[begin + 16 * index : begin + 16 * (index + 1), :TILE].astype(F32)
        for index in range(3)
    ]
    return pieces[0] + (pieces[1] + pieces[2])


def pair_terms(keys, values, queries, grads, mask, log_row, dot_row):
    scores = jnp.where(mask, dot(keys, queries, NT), MASKED)
    prob = jnp.exp(scores - log_row)
    prob_grad = dot(values, grads, NT)
    return prob.astype(BF16), (prob * (prob_grad - dot_row)).astype(BF16)


def query_side_kernel(pair):
    pair_span = slice(pair * PAIR, (pair + 1) * PAIR)

    def kernel(
        place, own, grad, mate, far, cross, cos, sin,
        q_grad_out, k_part_out, v_part_out,
        q_masked, grad_masked, stats, q_turned,
    ):
        rows = own.shape[0]
        where = Layout(place, rows)
        for index in range(rows // TILE):
            stats[:, tile(index)] = stat_rows(grad, index)
            some = grad[index * GRAD_ROWS : index * GRAD_ROWS + TILE, pair_span]
            for head in range(2):
                mask = head_mask((TILE, PAIR), head)
                q_masked[head, tile(index), :] = jnp.where(
                    mask, own[tile(index), :PAIR] * 0.125, 0
                ).astype(BF16)
                grad_masked[head, tile(index), :] = jnp.where(mask, some, 0).astype(BF16)

        def visit(keys, values, key_row, own_keys):
            turned = keys.astype(F32).T.astype(BF16)
            key_sum = value_sum = None
            for part in range(rows // WIDE):
                lanes = pl.ds(part * WIDE, WIDE)
                mask = where.allowed(where.offset + part * WIDE, WIDE, key_row, rows)
                for head in range(2):
                    index = 2 * pair + head
                    span = slice(HEAD_DIM * head, HEAD_DIM * (head + 1))
                    prob, score_grad = pair_terms(
                        keys, values, q_masked[head, lanes, :], grad_masked[head, lanes, :],
                        mask, stats[index : index + 1, lanes],
                        stats[8 + index : 9 + index, lanes],
                    )
                    product = dot(turned[span, :], score_grad)
                    if own_keys:
                        q_turned[span, lanes] = product
                        key_part = dot(score_grad, q_masked[head, lanes, :])
                        value_part = dot(prob, grad_masked[head, lanes, :])
                        key_sum = key_part if key_sum is None else key_sum + key_part
                        value_sum = value_part if value_sum is None else value_sum + value_part
                    else:
                        q_turned[span, lanes] += product
            if own_keys:
                k_part_out[...] = key_sum
                v_part_out[...] = value_sum

        visit(own[:, PAIR : 2 * PAIR], own[:, 2 * PAIR :], where.offset, True)
        first_start = where.start(where.offset)

        @pl.when(first_start < where.offset)
        def _():
            odd = (where.me & 1) == 1
            visit(
                jnp.where(odd, mate[:, PAIR : 2 * PAIR], cross[:, :PAIR]),
                jnp.where(odd, mate[:, 2 * PAIR :], cross[:, PAIR:]), where.offset - rows,
                False,
            )

        @pl.when(first_start < where.offset - rows)
        def _():
            visit(far[:, :PAIR], far[:, PAIR:], where.offset - 2 * rows, False)

        turned = q_turned[...].T * 0.125
        q_grad_out[...] = (turned * cos[...] - swap_halves(turned) * sin[...]).astype(BF16)

    return kernel


def key_side_kernel(pair):
    pair_span = slice(pair * PAIR, (pair + 1) * PAIR)

    def kernel(
        place, own, k_part, v_part, cos, sin, mate, far, cross,
        grad_mate, grad_far, grad_cross,
        k_grad_out, v_grad_out,
        k_masked, v_masked, k_turned, v_sum,
    ):
        rows = own.shape[0]
        where = Layout(place, rows)
        span_rows = place[1] * rows
        end = where.offset + rows
        k_turned[...] = k_part[...]
        v_sum[...] = v_part[...]

        def some(ref, chunk):
            return ref[chunk * GRAD_ROWS : chunk * GRAD_ROWS + TILE, pair_span]

        near = (end < span_rows) & (where.start(end) < end)
        beyond = (end + rows < span_rows) & (where.start(end + rows) < end)

        @pl.when(near)
        def _():
            for head in range(2):
                mask = head_mask((rows, PAIR), head)
                k_masked[head] = jnp.where(mask, own[:, PAIR : 2 * PAIR] * 0.125, 0).astype(BF16)
                v_masked[head] = jnp.where(mask, own[:, 2 * PAIR :], 0).astype(BF16)

        def visit(queries, grads, stats, query_row):
            first_head = head_mask((rows, PAIR), 0)
            for index in range(rows // TILE):
                mask = where.allowed(query_row + index * TILE, TILE, where.offset, rows)
                part = queries[index * TILE : (index + 1) * TILE, :]
                key_parts, value_parts = [], []
                for head in range(2):
                    line = 2 * pair + head
                    prob, score_grad = pair_terms(
                        k_masked[head], v_masked[head], part, grads[index], mask,
                        stats[index][line : line + 1, :], stats[index][8 + line : 9 + line, :],
                    )
                    key_parts.append(dot(score_grad, part))
                    value_parts.append(dot(prob, grads[index]))
                k_turned[...] += jnp.where(first_head, *key_parts) * 0.125
                v_sum[...] += jnp.where(first_head, *value_parts)

        @pl.when(near)
        def _():
            even = (where.me & 1) == 0
            chunks = range(rows // TILE)
            visit(
                jnp.where(even, mate[:, :PAIR], cross[:, :PAIR]),
                [jnp.where(even, some(grad_mate, i), some(grad_cross, i)) for i in chunks],
                [
                    jnp.where(even, stat_rows(grad_mate, i), stat_rows(grad_cross, i))
                    for i in chunks
                ],
                end,
            )

        @pl.when(beyond)
        def _():
            chunks = range(rows // TILE)
            visit(
                far[:, :PAIR], [some(grad_far, i) for i in chunks],
                [stat_rows(grad_far, i) for i in chunks], end + rows,
            )

        turned = k_turned[...]
        k_grad_out[...] = (turned * cos[...] - swap_halves(turned) * sin[...]).astype(BF16)
        v_grad_out[...] = v_sum[...].astype(BF16)

    return kernel


def input_kernel(*refs):
    grads, weights, out = refs[:9], refs[9:12], refs[12]
    total = None
    for index, weight in enumerate(weights):
        value = jnp.concatenate([ref[...] for ref in grads[3 * index : 3 * index + 3]], axis=1)
        product = dot(value, weight[...], NT)
        total = product if total is None else total + product
    out[...] = total.astype(BF16)


def finish_input_kernel(part, other, grad0, grad1, out):
    for index, grad in enumerate((grad0, grad1)):
        rows = tile(index)
        out[rows, :] = (
            part[rows, :].astype(F32) + other[rows, :].astype(F32) + grad[...].astype(F32)
        ).astype(BF16)


def stack_kernel(*refs):
    for index, ref in enumerate(refs[:-1]):
        refs[-1][tile(index), :] = ref[...]


def finish_inner_kernel(bit_ref, own, rest, inner_out, o_out):
    upper = bit_ref[0]
    half, wide = own.shape[0], inner_out.shape[1]
    for begin, ref in ((upper, own), (1 - upper, rest)):
        span = pl.ds(pl.multiple_of(begin * half, half), half)
        inner_out[span, :] = ref[:, :wide].astype(F32)
        o_out[:, span] = ref[:, wide:].astype(F32)


def finish_attention_kernel(bit_ref, own, rest, q_out, k_out, v_out, *vector_outs):
    upper = bit_ref[0]
    half, local = own.shape[0], q_out.shape[1]
    for begin, ref in ((upper, own), (1 - upper, rest)):
        span = pl.ds(pl.multiple_of(begin * half, half), half)
        q_out[span, :] = ref[:, :local].astype(F32)
        k_out[span, :] = ref[:, local : 2 * local].astype(F32)
        v_out[span, :] = ref[:, 2 * local : 3 * local].astype(F32)

        @pl.when(begin == 0)
        def _():
            tail = ref[:128, 3 * local :].astype(F32)
            tail = tail + pltpu.roll(tail, HEAD_DIM, 1)
            lane = lax.broadcasted_iota(jnp.int32, (1, PAIR), 1)
            line = 0
            for out in vector_outs:
                for index in range(out.shape[0] // PAIR):
                    value = jnp.where(
                        lane < HEAD_DIM, tail[line : line + 1, :], tail[line + 1 : line + 2, :]
                    )
                    out[index * PAIR : (index + 1) * PAIR] = value[0, :]
                    line += 2


def halves_of(place, rows):
    half = rows // 2
    bit = place[2]
    return (
        pl.multiple_of((1 - bit) * half, half), pl.multiple_of(bit * half, half)
    )


def weight_grad_kernel(place, left0, left1, right0, right1, send_out, keep_out):
    half = left0.shape[1] // 2
    for begin, out in zip(halves_of(place, 2 * half), (send_out, keep_out)):
        span = pl.ds(begin, half)
        out[...] = (
            dot(left0[:, span], right0[...], TN) + dot(left1[:, span], right1[...], TN)
        ).astype(BF16)


def inner_weight_kernel(
    place, first0, first1, pre0, pre1, low0, low1, low2, attn0, attn1, send_out, keep_out
):
    half = first0.shape[1] // 2
    wide = pre0.shape[1]
    lows = jnp.concatenate([low0[...], low1[...], low2[...]], axis=1)
    for begin, out in zip(halves_of(place, 2 * half), (send_out, keep_out)):
        span = pl.ds(begin, half)
        out[:, :wide] = (
            dot(first0[:, span], pre0[...], TN) + dot(first1[:, span], pre1[...], TN)
        ).astype(BF16)
        out[:, wide:] = (
            dot(lows[:TILE], attn0[:, span], TN) + dot(lows[TILE:], attn1[:, span], TN)
        ).astype(BF16)


def attention_weight_kernel(*refs):
    place, tokens = refs[:2]
    grads = refs[2:11]
    second0, second1, first0, first1, inner0, inner1 = refs[11:17]
    send_out, keep_out, vectors = refs[17:]
    width = tokens.shape[1]
    half = width // 2
    vectors[...] = jnp.zeros_like(vectors)
    rows_of = []
    for left, right in ((second0, second1), (first0, first1)):
        for index in range(3):
            rows_of.append(left[index : index + 1, :] + right[index : index + 1, :])
    rows_of.append(inner0[0:1, :] + inner1[0:1, :])
    for grad in grads:
        rows_of.append(sum_rows(grad[...]))
    line = 0
    for value in rows_of:
        for index in range(value.shape[1] // PAIR):
            piece = value[:, index * PAIR : (index + 1) * PAIR]
            vectors[line : line + 1, :] = piece
            vectors[line + 1 : line + 2, :] = pltpu.roll(piece, HEAD_DIM, 1)
            line += 2
    tail = high_and_low(vectors[...], pltpu.roll)
    together = jnp.concatenate([ref[...] for ref in grads], axis=1)
    main = together.shape[1]
    for begin, out in zip(halves_of(place, width), (send_out, keep_out)):
        span = pl.ds(begin, half)
        out[:, :main] = dot(tokens[:, span], together, TN).astype(BF16)
        out[:, main:] = jnp.where(begin == 0, tail, 0).astype(BF16)


def high_and_low(value, roll):
    high = value.astype(BF16).astype(F32)
    return jnp.where(head_mask(value.shape, 0), high, roll(value - high, HEAD_DIM, 1))


def add_two(one, two, tail, roll):
    one, two = one.astype(F32), two.astype(F32)
    if not tail:
        return (one + two).astype(BF16)
    main = one.shape[1] - PAIR
    rest = one[:, main:] + two[:, main:]
    rest = high_and_low(rest + roll(rest, HEAD_DIM, 1), roll)
    return jnp.concatenate([(one[:, :main] + two[:, :main]).astype(BF16), rest.astype(BF16)], axis=1)


def fold(bit, keep, received, split, tail):
    rows, width = keep.shape
    half = rows // 2
    if not split:

        def add_kernel(one, two, out):
            out[...] = add_two(one[...], two[...], tail, pltpu.roll)

        return call(add_kernel, [keep, received], [((rows, width), BF16)], cost=0.3)[0]
    if half % 16:
        total = add_two(keep, received, tail, jnp.roll)
        return [
            lax.dynamic_slice_in_dim(total, start * half, half, 0) for start in (1 - bit, bit)
        ]

    def fold_kernel(bit_ref, one, two, send_out, keep_out):
        upper = bit_ref[0]
        for begin, out in ((1 - upper, send_out), (upper, keep_out)):
            span = pl.ds(pl.multiple_of(begin * half, half), half)
            out[...] = add_two(one[span, :], two[span, :], tail, pltpu.roll)

    return call(
        fold_kernel, [bit.reshape(1), keep, received], [((half, width), BF16)] * 2, scalars=1,
        cost=0.5,
    )


def join(bit, own, received, dtype=BF16):
    half, width = own.shape
    if half % 16:
        ordered = jnp.where(
            bit == 1,
            jnp.concatenate([received, own], axis=0),
            jnp.concatenate([own, received], axis=0),
        )
        return ordered.astype(dtype)

    def join_kernel(bit_ref, one, two, out):
        upper = bit_ref[0]
        out[pl.ds(pl.multiple_of(upper * half, half), half), :] = one[...].astype(dtype)
        out[pl.ds(pl.multiple_of((1 - upper) * half, half), half), :] = two[...].astype(dtype)

    return call(
        join_kernel, [bit.reshape(1), own, received], [((2 * half, width), dtype)], scalars=1,
        cost=0.5, final=dtype == F32,
    )[0]


def flip(value, axis, bit):
    size = lax.axis_size(axis)
    return lax.ppermute(value, axis, [(i, i ^ bit) for i in range(size)])


class Sum:
    def __init__(self, pieces, stages, bits, tail=False):
        send, self.value = pieces
        self.tail, self.stages, self.bits, self.index = tail, stages, bits, 0
        self.received = flip(send, *stages[0])

    def step(self):
        stages, index, count = self.stages, self.index, len(self.stages)
        if index == 2 * count - 2:
            return
        self.index += 1
        if index < count - 2:
            stage = stages[index + 1]
            send, self.value = fold(self.bits[stage], self.value, self.received, True, self.tail)
            self.received = flip(send, *stage)
            return
        if index < count:
            self.value = fold(None, self.value, self.received, False, self.tail)
        else:
            self.value = join(self.bits[stages[2 * count - 2 - index]], self.value, self.received)
        self.received = flip(self.value, *stages[count - 1 if index == count - 2 else 2 * count - 3 - index])

    def finish(self):
        while self.index < 2 * len(self.stages) - 2:
            self.step()
        return self.value, self.received


def per_device(
    tokens, out_grad, lengths, query_weight, query_bias, key_weight, key_bias, value_weight,
    value_bias, output_weight, output_bias, first_gain, first_shift, inner_weight, inner_bias,
    outer_weight, outer_bias, second_gain, second_shift,
):
    Order.last = None
    rows, width = tokens.shape
    local = query_weight.shape[1]
    pairs = local // PAIR
    hidden_width = inner_weight.shape[1]
    chunks = rows // TILE
    units = hidden_width // 512
    ctx_size, dp_size = lax.axis_size("ctx"), lax.axis_size("dp")
    me = lax.axis_index("ctx")
    spot = jnp.arange(8)
    place = jnp.pad(lengths[0], (3, 5 - lengths.shape[1])) + jnp.where(
        spot == 0, me, jnp.where(spot == 1, ctx_size, jnp.where(spot == 2, me & 1, 0))
    )
    stage_bits = [
        (axis, 1 << i)
        for axis, size in (("ctx", ctx_size), ("dp", dp_size))
        for i in range((size - 1).bit_length())
    ]
    bits = {
        (axis, bit): ((lax.axis_index(axis) & bit) != 0).astype(jnp.int32)
        for axis, bit in stage_bits
    }
    ctx_stages = [stage for stage in stage_bits if stage[0] == "ctx"]

    frequency = 10000.0 ** (-2.0 * np.arange(HEAD_DIM // 2) / HEAD_DIM)
    lanes = np.tile(frequency, PAIR // (HEAD_DIM // 2))
    angles = np.arange(rows)[:, None] * lanes[None, :]
    trig = jnp.asarray(
        np.concatenate([np.cos(angles), np.sin(angles), np.tile(lanes, (8, 1))]), F32
    )

    weights = [query_weight, key_weight, value_weight, query_bias, key_bias, value_bias]
    owns, fars, mates, crosses = [], [], [], []
    reach = ctx_size // 2
    around = [(i, (i + reach) % ctx_size) for i in range(ctx_size)]
    table = ((rows, PAIR), F32)
    for pair in range(pairs):
        shapes = [((rows, 3 * PAIR), BF16), ((rows, 2 * PAIR), BF16)]
        if pair == 0:
            sources = [tokens, *weights]
            own, sent, cosine, sine, *copied = call(
                first_project_kernel, [place, trig, *sources],
                shapes + [table, table] + [(value.shape, value.dtype) for value in sources],
                scratch=[
                    pltpu.VMEM(trig.shape, F32), pltpu.SemaphoreType.DMA((1 + len(sources),)),
                ],
                scalars=1, hbm=1 + len(sources), cost=3.0,
            )
            tokens, weights = copied[0], copied[1:]
        else:
            own, sent = call(
                project_kernel(pair), [place, tokens, *weights, cosine, sine], shapes,
                scalars=1, cost=1.0,
            )
        far = lax.ppermute(sent, "ctx", around)
        owns.append(own)
        fars.append(far)
        mates.append(flip(own, "ctx", 1))
        crosses.append(flip(far, "ctx", 1))

    lows, logs, highs = [], [], []
    for pair in range(pairs):
        low, lse, high = call(
            attend_kernel,
            [place, owns[pair], mates[pair], fars[pair], crosses[pair]],
            [((rows, PAIR), BF16), ((2, rows), F32), ((PAIR, rows), F32)],
            scratch=[
                pltpu.VMEM((2, PAIR, rows), BF16), pltpu.VMEM((2, rows), F32),
                pltpu.VMEM((2, rows), F32), pltpu.VMEM((PAIR, rows), F32),
            ],
            scalars=1, cost=4.0,
        )
        lows.append(low)
        logs.append(lse)
        highs.append(high)
    attn_parts = call(
        output_kernel, [*lows, output_weight], [((TILE, width), BF16)] * chunks, cost=1.0
    )

    def swap(value):
        return flip(value, "tensor", 1)

    block = ((TILE, width), BF16)
    wide = ((TILE, hidden_width), BF16)
    attn_others = [swap(part) for part in attn_parts]
    forward = []
    for chunk in range(chunks):
        forward.append(
            call(
                forward_kernel(chunk, units),
                [
                    tokens, attn_parts[chunk], attn_others[chunk], output_bias, first_gain,
                    first_shift, inner_weight, inner_bias, outer_weight,
                ],
                [block, ((TILE, 1), F32), block, wide, wide, block],
                cost=3.5,
            )
        )
    normed, inverse, first_low, hidden, slope, ffn_parts = zip(*forward)
    ffn_others = [swap(part) for part in ffn_parts]
    backward = []
    for chunk in range(chunks):
        backward.append(
            call(
                backward_kernel(chunk, units),
                [
                    normed[chunk], ffn_parts[chunk], ffn_others[chunk], out_grad, first_gain,
                    first_shift, outer_bias, second_gain, second_shift, slope[chunk],
                    inner_weight, outer_weight,
                ],
                [
                    block, block, wide, block, ((8, width), F32), ((8, hidden_width), F32),
                ],
                cost=3.0,
            )
        )
    layer_out, ffn_grad, pre_grad, first_parts, second_sums, inner_sums = zip(*backward)
    first_others = [swap(part) for part in first_parts]

    outer_half = ((hidden_width // 2, width), BF16)
    outer_pieces = call(
        weight_grad_kernel, [place, *hidden, *ffn_grad], [outer_half] * 2, scalars=1, cost=2.0
    )
    outer_sum = Sum(outer_pieces, stage_bits, bits)
    layer_out = call(
        stack_kernel, layer_out, [((rows, width), BF16)], cost=0.3, final=True
    )[0]

    back_reach = [(i + reach, i) for i in range(ctx_size - reach)]
    attn_grad, first_sums, head_grad = [], [], []
    for chunk in range(chunks):
        grad, head_part, sums = call(
            middle_kernel(chunk),
            [
                ffn_grad[chunk], first_parts[chunk], first_others[chunk], normed[chunk],
                inverse[chunk], first_gain, output_weight, *highs, *logs, *head_grad[-1:],
            ],
            [block, (((chunk + 1) * GRAD_ROWS, local), BF16), ((8, width), F32)],
            scratch=[pltpu.VMEM((16, TILE), F32)],
            cost=1.5,
        )
        attn_grad.append(grad)
        first_sums.append(sums)
        head_grad.append(head_part)
        if chunk == 0:
            outer_sum.step()
    head_grad = head_grad[-1]
    grad_far = lax.ppermute(head_grad, "ctx", back_reach)
    grad_mate = flip(head_grad, "ctx", 1)
    grad_cross = flip(grad_far, "ctx", 1)
    inner_half = ((width // 2, hidden_width + local), BF16)
    inner_pieces = call(
        inner_weight_kernel, [place, *first_low, *pre_grad, *lows, *attn_grad],
        [inner_half] * 2, scalars=1, cost=2.0,
    )
    inner_sum = Sum(inner_pieces, stage_bits, bits)

    q_grads, k_grads, v_grads, key_parts = [], [], [], []
    double = pltpu.VMEM((2, rows, PAIR), BF16)
    single = pltpu.VMEM((rows, PAIR), F32)

    def query_side(pair):
        q_grad, k_part, v_part = call(
            query_side_kernel(pair),
            [
                place, owns[pair], head_grad, mates[pair], fars[pair], crosses[pair],
                cosine, sine,
            ],
            [((rows, PAIR), BF16), table, table],
            scratch=[
                double, double, pltpu.VMEM((16, rows), F32), pltpu.VMEM((PAIR, rows), F32),
            ],
            scalars=1, cost=4.0,
        )
        q_grads.append(q_grad)
        key_parts.append((k_part, v_part))

    def key_side(pair):
        k_grad, v_grad = call(
            key_side_kernel(pair),
            [
                place, owns[pair], *key_parts[pair], cosine, sine, mates[pair],
                fars[pair], crosses[pair], grad_mate, grad_far, grad_cross,
            ],
            [((rows, PAIR), BF16)] * 2,
            scratch=[double, double, single, single],
            scalars=1, cost=4.0,
        )
        k_grads.append(k_grad)
        v_grads.append(v_grad)

    query_side(0)
    inner_sum.step()
    query_side(1)
    outer_sum.step()
    query_side(2)
    outer_sum.step()
    key_side(0)
    key_side(1)
    key_side(2)
    all_grads = [*q_grads, *k_grads, *v_grads]
    attention_half = ((width // 2, 3 * local + PAIR), BF16)
    attention_sum = Sum(
        call(
            attention_weight_kernel,
            [place, tokens, *all_grads, *second_sums, *first_sums, *inner_sums],
            [attention_half] * 2,
            scratch=[pltpu.VMEM((width // 2, PAIR), F32)],
            scalars=1, cost=2.5,
        ),
        stage_bits, bits, True,
    )
    input_part = call(
        input_kernel, [*all_grads, *weights[:3]], [((rows, width), BF16)], cost=1.5
    )[0]
    attention_sum.step()
    input_other = swap(input_part)
    outer_sum.step()
    inner_sum.step()
    outer_sum.step()
    inner_sum.step()
    attention_sum.step()
    outer_own, outer_rest = outer_sum.finish()
    inner_sum.step()
    attention_sum.step()
    input_grad = call(
        finish_input_kernel, [input_part, input_other, *attn_grad], [((rows, width), BF16)],
        cost=0.5, final=True,
    )[0]
    core = bits[ctx_stages[0]]
    outer_grad = join(core, outer_own, outer_rest, F32)
    inner_sum.step()
    attention_sum.step()
    inner_own, inner_rest = inner_sum.finish()
    attention_sum.step()
    inner_grad, o_weight_grad = call(
        finish_inner_kernel, [core.reshape(1), inner_own, inner_rest],
        [((width, hidden_width), F32), ((local, width), F32)], scalars=1, cost=2.0, final=True,
    )
    attention_own, attention_rest = attention_sum.finish()
    vector_sizes = [width] * 6 + [hidden_width] + [local] * 3
    (
        q_weight_grad, k_weight_grad, v_weight_grad,
        second_gain_grad, second_shift_grad, outer_bias_grad,
        first_gain_grad, first_shift_grad, output_bias_grad, inner_bias_grad,
        q_bias_grad, k_bias_grad, v_bias_grad,
    ) = call(
        finish_attention_kernel,
        [core.reshape(1), attention_own, attention_rest],
        [((width, local), F32)] * 3 + [((size,), F32) for size in vector_sizes],
        scalars=1, cost=2.0, final=True,
    )
    return (
        layer_out, input_grad,
        q_weight_grad, q_bias_grad, k_weight_grad, k_bias_grad, v_weight_grad, v_bias_grad,
        o_weight_grad, output_bias_grad, first_gain_grad, first_shift_grad,
        inner_grad, inner_bias_grad, outer_grad, outer_bias_grad,
        second_gain_grad, second_shift_grad,
    )


def solution(mesh):
    rows_spec, column_spec, row_spec = P(("dp", "ctx"), None), P(None, "tensor"), P("tensor", None)
    return jax.shard_map(
        per_device,
        mesh=mesh,
        in_specs=(
            rows_spec, rows_spec, P("dp", None),
            column_spec, P("tensor"), column_spec, P("tensor"), column_spec, P("tensor"),
            row_spec, P(), P(), P(), column_spec, P("tensor"), row_spec, P(), P(), P(),
        ),
        out_specs=(
            rows_spec, rows_spec,
            column_spec, P("tensor"), column_spec, P("tensor"), column_spec, P("tensor"),
            row_spec, P(), P(), P(), column_spec, P("tensor"), row_spec, P(), P(), P(),
        ),
        check_vma=False,
    )
```

```python
import jax
import jax.numpy as jnp
import numpy as np
from jax import lax
from jax.experimental import pallas as pl
from jax.experimental.pallas import tpu as pltpu
from jax.sharding import PartitionSpec as P

HEAD_DIM = 64
PAIR = 2 * HEAD_DIM
MASKED = -1e30
EPSILON = 1e-06
TILE = 256
WIDE = 512
GRAD_ROWS = TILE + 48
GROUPS = ((0, 1), (2,))
F32 = jnp.float32
BF16 = jnp.bfloat16
VMEM_BYTES = 12 * 1024 * 1024
FINAL = pltpu.HBM

NN = (((1,), (0,)), ((), ()))
NT = (((1,), (1,)), ((), ()))
TN = (((0,), (0,)), ((), ()))


def dot(left, right, dims=NN):
    return lax.dot_general(left, right, dims, preferred_element_type=F32)


class Order:
    last = None


def call(kernel, inputs, outputs, scratch=(), scalars=0, hbm=0, cost=1.0, ordered=True, final=False):
    spaces = [pltpu.SMEM] * scalars + [pltpu.VMEM] * (len(inputs) - scalars - hbm)
    spaces += [pltpu.HBM] * hbm
    inputs = list(inputs)
    for index in range(len(inputs) - hbm, len(inputs)):
        inputs[index] = pltpu.with_memory_space_constraint(inputs[index], pltpu.HBM)
    body = kernel
    if ordered and Order.last is not None:
        count = len(inputs)
        inputs.append(Order.last)
        spaces.append(pl.ANY)

        def body(*refs):
            kernel(*refs[:count], *refs[count + 1 :])

    results = pl.pallas_call(
        body,
        in_specs=[pl.BlockSpec(memory_space=space) for space in spaces],
        out_specs=[pl.BlockSpec(memory_space=pltpu.VMEM)] * len(outputs),
        out_shape=[
            FINAL(dims, dtype) if final else jax.ShapeDtypeStruct(dims, dtype)
            for dims, dtype in outputs
        ],
        scratch_shapes=list(scratch),
        compiler_params=pltpu.CompilerParams(vmem_limit_bytes=VMEM_BYTES),
        cost_estimate=pl.CostEstimate(
            flops=int(cost * 1e10), bytes_accessed=int(cost * 1e13), transcendentals=0
        ),
    )(*inputs)
    if ordered:
        Order.last = min(results, key=lambda value: value.size * value.dtype.itemsize)
        if final:
            Order.last = pltpu.with_memory_space_constraint(Order.last, pltpu.HBM)
    return results


def tile(index):
    return pl.ds(index * TILE, TILE)


def sum_rows(value):
    return jnp.sum(value.astype(F32), axis=0, keepdims=True)


def mean(value):
    return jnp.mean(value, axis=-1, keepdims=True)


def normalize(rows_in):
    centered = rows_in - mean(rows_in)
    inverse = lax.rsqrt(mean(centered * centered) + EPSILON)
    return centered * inverse, inverse


def norm_back(grad, normed, inverse):
    return inverse * (grad - mean(grad) - normed * mean(grad * normed))


def swap_halves(value):
    lane = lax.broadcasted_iota(jnp.int32, value.shape, 1)
    ahead = pltpu.roll(value, PAIR - HEAD_DIM // 2, 1)
    behind = pltpu.roll(value, HEAD_DIM // 2, 1)
    return jnp.where(lane % HEAD_DIM < HEAD_DIM // 2, ahead, behind)


def window(ref, slot, parts):
    return ref.at[:, slot * parts * PAIR : (slot + 1) * parts * PAIR]


def head_mask(shape, head):
    lane = lax.broadcasted_iota(jnp.int32, shape, 1)
    return (lane // HEAD_DIM) == head


class Layout:
    def __init__(self, place, rows):
        self.me = place[0]
        self.rows = rows
        self.offset = self.me * rows
        self.end0 = place[3]
        self.end1 = self.end0 + place[4]

    def start(self, index):
        return jnp.where(
            index >= self.end1, self.end1, jnp.where(index >= self.end0, self.end0, 0)
        )

    def allowed(self, query_row, queries, key_row, keys):
        query = query_row + lax.broadcasted_iota(jnp.int32, (1, queries), 1)
        key = key_row + lax.broadcasted_iota(jnp.int32, (keys, 1), 0)
        return (key >= self.start(query)) & (key <= query)


def project_tables(place, table, cos_out, sin_out):
    rows = cos_out.shape[0]
    base_cos, base_sin, freq = table[:rows, :], table[rows : 2 * rows, :], table[2 * rows :, :]
    where = Layout(place, rows)
    row = where.offset + lax.broadcasted_iota(jnp.int32, (rows, 1), 0)
    turns = []
    for start in (0, where.end0, where.end1):
        angle = (where.offset - start).astype(F32) * freq
        turns.append((jnp.cos(angle)[0:1, :], jnp.sin(angle)[0:1, :]))
    late, later = row >= where.end0, row >= where.end1
    cos_turn = jnp.where(later, turns[2][0], jnp.where(late, turns[1][0], turns[0][0]))
    sin_turn = jnp.where(later, turns[2][1], jnp.where(late, turns[1][1], turns[0][1]))
    cosine = base_cos * cos_turn - base_sin * sin_turn
    sine = base_sin * cos_turn + base_cos * sin_turn
    lane = lax.broadcasted_iota(jnp.int32, (rows, PAIR), 1)
    cos_out[...] = cosine
    sin_out[...] = jnp.where(lane % HEAD_DIM < HEAD_DIM // 2, -sine, sine)


def project_group(group, place, tokens, wq, wk, wv, bq, bk, bv, cos, sin, own_out, far_out):
    cosine, sine = cos[...], sin[...]
    onward = place[0] < place[1] // 2
    for slot, pair in enumerate(group):
        span = slice(pair * PAIR, (pair + 1) * PAIR)
        weight = jnp.concatenate([wq[:, span], wk[:, span], wv[:, span]], axis=1)
        pre = dot(tokens[...], weight)
        query = pre[:, :PAIR] + bq[span].reshape(1, PAIR)
        key = pre[:, PAIR : 2 * PAIR] + bk[span].reshape(1, PAIR)
        query = (query * cosine + swap_halves(query) * sine).astype(BF16)
        key = (key * cosine + swap_halves(key) * sine).astype(BF16)
        value = (pre[:, 2 * PAIR :] + bv[span].reshape(1, PAIR)).astype(BF16)
        own, far = window(own_out, slot, 3), window(far_out, slot, 2)
        own[:, :PAIR] = query
        own[:, PAIR : 2 * PAIR] = key
        own[:, 2 * PAIR :] = value
        far[:, :PAIR] = jnp.where(onward, key, query)
        far[:, PAIR:] = jnp.where(onward, value, query)


def first_project_kernel(place, *refs):
    count = (len(refs) - 7) // 2
    sources, (own_out, far_out, cos_out, sin_out) = refs[:count + 1], refs[count + 1 : count + 5]
    copies, table, sems = refs[count + 5 : 2 * count + 5], refs[-2], refs[-1]
    moves = [
        pltpu.make_async_copy(source, target, sems.at[index])
        for index, (source, target) in enumerate(zip(sources, (table, *copies)))
    ]
    for move in moves:
        move.start()
    moves[0].wait()
    project_tables(place, table, cos_out, sin_out)
    for move in moves[1:]:
        move.wait()
    project_group(GROUPS[0], place, *copies, cos_out, sin_out, own_out, far_out)


def load_kernel(*refs):
    count = len(refs) // 2
    moves = [
        pltpu.make_async_copy(refs[index], refs[count + index], refs[-1].at[index])
        for index in range(count)
    ]
    for move in moves:
        move.start()
    for move in moves:
        move.wait()


def project_kernel(group):
    def kernel(*refs):
        project_group(group, *refs)

    return kernel


def attend_kernel(slot):
    def kernel(
        place, own, mate, far, cross,
        low_out, lse_out, high, q_masked, peak, total, accum,
    ):
        own, mate = window(own, slot, 3), window(mate, slot, 3)
        far, cross = window(far, slot, 2), window(cross, slot, 2)
        rows = own.shape[0]
        where = Layout(place, rows)
        turned_q = own[:, :PAIR].astype(F32).T * 0.125
        for head in range(2):
            other = slice(HEAD_DIM * (1 - head), HEAD_DIM * (2 - head))
            mine = slice(HEAD_DIM * head, HEAD_DIM * (head + 1))
            q_masked[head, mine, :] = turned_q[mine, :].astype(BF16)
            q_masked[head, other, :] = jnp.zeros((HEAD_DIM, rows), BF16)

        def visit(keys, values, key_row, first):
            turned = values.astype(F32).T.astype(BF16)
            for part in range(rows // WIDE):
                lanes = pl.ds(part * WIDE, WIDE)
                mask = where.allowed(where.offset + part * WIDE, WIDE, key_row, rows)
                for head in range(2):
                    span = slice(HEAD_DIM * head, HEAD_DIM * (head + 1))
                    scores = dot(keys, q_masked[head, :, lanes])
                    scores = jnp.where(mask, scores, MASKED)
                    top = jnp.max(scores, axis=0, keepdims=True)
                    if not first:
                        old = peak[head : head + 1, lanes]
                        top = jnp.maximum(old, top)
                        decay = jnp.exp(old - top)
                    prob = jnp.exp(scores - top)
                    sums = jnp.sum(prob, axis=0, keepdims=True)
                    product = dot(turned[span, :], prob.astype(BF16))
                    if not first:
                        sums += total[head : head + 1, lanes] * decay
                        product += accum[span, lanes] * decay
                    peak[head : head + 1, lanes] = top
                    total[head : head + 1, lanes] = sums
                    accum[span, lanes] = product

        visit(own[:, PAIR : 2 * PAIR], own[:, 2 * PAIR :], where.offset, True)
        first_start = where.start(where.offset)

        @pl.when(first_start < where.offset)
        def _():
            odd = (where.me & 1) == 1
            visit(
                jnp.where(odd, mate[:, PAIR : 2 * PAIR], cross[:, :PAIR]),
                jnp.where(odd, mate[:, 2 * PAIR :], cross[:, PAIR:]), where.offset - rows, False,
            )

        @pl.when(first_start < where.offset - rows)
        def _():
            visit(far[:, :PAIR], far[:, PAIR:], where.offset - 2 * rows, False)

        for head in range(2):
            sums = total[head : head + 1, :]
            lse_out[head : head + 1, :] = peak[head : head + 1, :] + jnp.log(sums)
            span = slice(HEAD_DIM * head, HEAD_DIM * (head + 1))
            high[span, :] = accum[span, :] / sums
        low_out[...] = high[...].T.astype(BF16)

    return kernel


def output_kernel(*refs):
    lows, wo, outs = refs[:3], refs[3], refs[4:]
    for index, out in enumerate(outs):
        low = jnp.concatenate([ref[tile(index), :] for ref in lows], axis=1)
        out[...] = dot(low, wo[...]).astype(BF16)


def forward_kernel(chunk, units):
    def kernel(
        tokens, part, other, bias, gain, shift, w_in, b_in, w_out,
        normed_out, inverse_out, first_out, hidden_out, slope_out, part_out,
    ):
        width = tokens.shape[1]
        attn = part[...].astype(F32) + other[...].astype(F32) + bias[...].reshape(1, width)
        normed, inverse = normalize(tokens[tile(chunk), :].astype(F32) + attn)
        normed_out[...] = normed.astype(BF16)
        inverse_out[...] = inverse
        first = normed * gain[...].reshape(1, width) + shift[...].reshape(1, width)
        first_low = first.astype(BF16)
        first_out[...] = first_low
        total = None
        unit = w_in.shape[1] // units
        for index in range(units):
            span = slice(index * unit, (index + 1) * unit)
            pre = dot(first_low, w_in[:, span]) + b_in[span].reshape(1, unit)
            cdf = 0.5 * (1.0 + lax.erf(pre * 0.7071067811865476))
            density = jnp.exp(-0.5 * pre * pre) * 0.3989422804014327
            hidden = (pre * cdf).astype(BF16)
            hidden_out[:, span] = hidden
            slope_out[:, span] = (cdf + pre * density).astype(BF16)
            product = dot(hidden, w_out[span, :])
            total = product if total is None else total + product
        part_out[...] = total.astype(BF16)

    return kernel


def backward_kernel(chunk, units):
    def kernel(
        normed_first, part, other, out_grad, first_gain, first_shift, bias, gain, shift,
        slope, w_in, w_out,
        layer_out, ffn_grad_out, pre_grad_out, part_out, sums_out, inner_out,
    ):
        width = part.shape[1]

        def row(ref):
            return ref[...].reshape(1, width)

        first = normed_first[...].astype(F32) * row(first_gain) + row(first_shift)
        ffn = part[...].astype(F32) + other[...].astype(F32) + row(bias)
        normed, inverse = normalize(first + ffn)
        layer_out[...] = (normed * row(gain) + row(shift)).astype(BF16)
        upstream = out_grad[tile(chunk), :].astype(F32)
        res_grad = norm_back(upstream * row(gain), normed, inverse)
        ffn_grad = res_grad.astype(BF16)
        ffn_grad_out[...] = ffn_grad
        sums_out[0:1, :] = sum_rows(upstream * normed)
        sums_out[1:2, :] = sum_rows(upstream)
        sums_out[2:3, :] = sum_rows(ffn_grad)
        total = None
        unit = w_in.shape[1] // units
        for index in range(units):
            span = slice(index * unit, (index + 1) * unit)
            hidden_grad = dot(ffn_grad, w_out[span, :], NT)
            pre_grad = (hidden_grad * slope[:, span].astype(F32)).astype(BF16)
            pre_grad_out[:, span] = pre_grad
            inner_out[0:1, span] = sum_rows(pre_grad)
            product = dot(pre_grad, w_in[:, span], NT)
            total = product if total is None else total + product
        part_out[...] = total.astype(BF16)

    return kernel


def split_three(value):
    high = value.astype(BF16)
    rest = value - high.astype(F32)
    middle = rest.astype(BF16)
    return high, middle, (rest - middle.astype(F32)).astype(BF16)


def middle_kernel(chunk):
    def kernel(
        ffn_grad, part, other, normed, inverse, gain, wo, high0, high1, high2, lse0, lse1, lse2,
        *rest,
    ):
        grad_out, head_out, sums_out, stats = rest[-4:]
        base = chunk * GRAD_ROWS
        if chunk:
            head_out[:base, :] = rest[0][...]
        width = part.shape[1]
        local = wo.shape[0]
        first_grad = (
            ffn_grad[...].astype(F32) + part[...].astype(F32) + other[...].astype(F32)
        )
        unit = normed[...].astype(F32)
        res_grad = norm_back(first_grad * gain[...].reshape(1, width), unit, inverse[...])
        attn_grad = res_grad.astype(BF16)
        grad_out[...] = attn_grad
        sums_out[0:1, :] = sum_rows(first_grad * unit)
        sums_out[1:2, :] = sum_rows(first_grad)
        sums_out[2:3, :] = sum_rows(attn_grad)
        head_grad = dot(attn_grad, wo[...], NT).astype(BF16)
        head_out[base : base + TILE, :] = head_grad
        high = jnp.concatenate([ref[:, tile(chunk)] for ref in (high0, high1, high2)], axis=0)
        turned = head_grad.astype(F32).T * high
        stats[...] = jnp.zeros_like(stats)
        for index, lse in enumerate((lse0, lse1, lse2)):
            stats[2 * index : 2 * index + 2, :] = lse[:, tile(chunk)]
        for head in range(local // HEAD_DIM):
            span = slice(HEAD_DIM * head, HEAD_DIM * (head + 1))
            stats[8 + head : 9 + head, :] = jnp.sum(turned[span, :], axis=0, keepdims=True)
        begin = base + TILE
        head_out[begin:, :] = jnp.zeros((GRAD_ROWS - TILE, local), BF16)
        for index, value in enumerate(split_three(stats[...])):
            head_out[begin + 16 * index : begin + 16 * (index + 1), :TILE] = value

    return kernel


def stat_rows(grad, chunk):
    begin = chunk * GRAD_ROWS + TILE
    pieces = [
        grad[begin + 16 * index : begin + 16 * (index + 1), :TILE].astype(F32)
        for index in range(3)
    ]
    return pieces[0] + (pieces[1] + pieces[2])


def pair_terms(keys, values, queries, grads, mask, log_row, dot_row):
    scores = jnp.where(mask, dot(keys, queries, NT), MASKED)
    prob = jnp.exp(scores - log_row)
    prob_grad = dot(values, grads, NT)
    return prob.astype(BF16), (prob * (prob_grad - dot_row)).astype(BF16)


def query_side_kernel(pair, slot):
    pair_span = slice(pair * PAIR, (pair + 1) * PAIR)

    def kernel(
        place, own, grad, mate, far, cross, cos, sin,
        q_grad_out, k_part_out, v_part_out,
        q_masked, grad_masked, stats, q_turned,
    ):
        own, mate = window(own, slot, 3), window(mate, slot, 3)
        far, cross = window(far, slot, 2), window(cross, slot, 2)
        rows = own.shape[0]
        where = Layout(place, rows)
        for index in range(rows // TILE):
            stats[:, tile(index)] = stat_rows(grad, index)
            some = grad[index * GRAD_ROWS : index * GRAD_ROWS + TILE, pair_span]
            for head in range(2):
                mask = head_mask((TILE, PAIR), head)
                q_masked[head, tile(index), :] = jnp.where(
                    mask, own[tile(index), :PAIR] * 0.125, 0
                ).astype(BF16)
                grad_masked[head, tile(index), :] = jnp.where(mask, some, 0).astype(BF16)

        def visit(keys, values, key_row, own_keys):
            turned = keys.astype(F32).T.astype(BF16)
            key_sum = value_sum = None
            for part in range(rows // WIDE):
                lanes = pl.ds(part * WIDE, WIDE)
                mask = where.allowed(where.offset + part * WIDE, WIDE, key_row, rows)
                for head in range(2):
                    index = 2 * pair + head
                    span = slice(HEAD_DIM * head, HEAD_DIM * (head + 1))
                    prob, score_grad = pair_terms(
                        keys, values, q_masked[head, lanes, :], grad_masked[head, lanes, :],
                        mask, stats[index : index + 1, lanes],
                        stats[8 + index : 9 + index, lanes],
                    )
                    product = dot(turned[span, :], score_grad)
                    if own_keys:
                        q_turned[span, lanes] = product
                        key_part = dot(score_grad, q_masked[head, lanes, :])
                        value_part = dot(prob, grad_masked[head, lanes, :])
                        key_sum = key_part if key_sum is None else key_sum + key_part
                        value_sum = value_part if value_sum is None else value_sum + value_part
                    else:
                        q_turned[span, lanes] += product
            if own_keys:
                k_part_out[...] = key_sum
                v_part_out[...] = value_sum

        visit(own[:, PAIR : 2 * PAIR], own[:, 2 * PAIR :], where.offset, True)
        first_start = where.start(where.offset)

        @pl.when(first_start < where.offset)
        def _():
            odd = (where.me & 1) == 1
            visit(
                jnp.where(odd, mate[:, PAIR : 2 * PAIR], cross[:, :PAIR]),
                jnp.where(odd, mate[:, 2 * PAIR :], cross[:, PAIR:]), where.offset - rows,
                False,
            )

        @pl.when(first_start < where.offset - rows)
        def _():
            visit(far[:, :PAIR], far[:, PAIR:], where.offset - 2 * rows, False)

        turned = q_turned[...].T * 0.125
        q_grad_out[...] = (turned * cos[...] - swap_halves(turned) * sin[...]).astype(BF16)

    return kernel


def key_side_kernel(pair, slot):
    pair_span = slice(pair * PAIR, (pair + 1) * PAIR)

    def kernel(
        place, own, k_part, v_part, cos, sin, mate, far, cross,
        grad_mate, grad_far, grad_cross,
        k_grad_out, v_grad_out,
        k_masked, v_masked, k_turned, v_sum,
    ):
        own, mate = window(own, slot, 3), window(mate, slot, 3)
        far, cross = window(far, slot, 2), window(cross, slot, 2)
        rows = own.shape[0]
        where = Layout(place, rows)
        span_rows = place[1] * rows
        end = where.offset + rows
        k_turned[...] = k_part[...]
        v_sum[...] = v_part[...]

        def some(ref, chunk):
            return ref[chunk * GRAD_ROWS : chunk * GRAD_ROWS + TILE, pair_span]

        near = (end < span_rows) & (where.start(end) < end)
        beyond = (end + rows < span_rows) & (where.start(end + rows) < end)

        @pl.when(near)
        def _():
            for head in range(2):
                mask = head_mask((rows, PAIR), head)
                k_masked[head] = jnp.where(mask, own[:, PAIR : 2 * PAIR] * 0.125, 0).astype(BF16)
                v_masked[head] = jnp.where(mask, own[:, 2 * PAIR :], 0).astype(BF16)

        def visit(queries, grads, stats, query_row):
            first_head = head_mask((rows, PAIR), 0)
            for index in range(rows // TILE):
                mask = where.allowed(query_row + index * TILE, TILE, where.offset, rows)
                part = queries[index * TILE : (index + 1) * TILE, :]
                key_parts, value_parts = [], []
                for head in range(2):
                    line = 2 * pair + head
                    prob, score_grad = pair_terms(
                        k_masked[head], v_masked[head], part, grads[index], mask,
                        stats[index][line : line + 1, :], stats[index][8 + line : 9 + line, :],
                    )
                    key_parts.append(dot(score_grad, part))
                    value_parts.append(dot(prob, grads[index]))
                k_turned[...] += jnp.where(first_head, *key_parts) * 0.125
                v_sum[...] += jnp.where(first_head, *value_parts)

        @pl.when(near)
        def _():
            even = (where.me & 1) == 0
            chunks = range(rows // TILE)
            visit(
                jnp.where(even, mate[:, :PAIR], cross[:, :PAIR]),
                [jnp.where(even, some(grad_mate, i), some(grad_cross, i)) for i in chunks],
                [
                    jnp.where(even, stat_rows(grad_mate, i), stat_rows(grad_cross, i))
                    for i in chunks
                ],
                end,
            )

        @pl.when(beyond)
        def _():
            chunks = range(rows // TILE)
            visit(
                far[:, :PAIR], [some(grad_far, i) for i in chunks],
                [stat_rows(grad_far, i) for i in chunks], end + rows,
            )

        turned = k_turned[...]
        k_grad_out[...] = (turned * cos[...] - swap_halves(turned) * sin[...]).astype(BF16)
        v_grad_out[...] = v_sum[...].astype(BF16)

    return kernel


def input_kernel(*refs):
    grads, weights, out = refs[:9], refs[9:12], refs[12]
    total = None
    for index, weight in enumerate(weights):
        value = jnp.concatenate([ref[...] for ref in grads[3 * index : 3 * index + 3]], axis=1)
        product = dot(value, weight[...], NT)
        total = product if total is None else total + product
    out[...] = total.astype(BF16)


def finish_input_kernel(part, other, grad0, grad1, out):
    for index, grad in enumerate((grad0, grad1)):
        rows = tile(index)
        out[rows, :] = (
            part[rows, :].astype(F32) + other[rows, :].astype(F32) + grad[...].astype(F32)
        ).astype(BF16)


def stack_kernel(*refs):
    for index, ref in enumerate(refs[:-1]):
        refs[-1][tile(index), :] = ref[...]


def finish_inner_kernel(bit_ref, own, rest, inner_out, o_out):
    upper = bit_ref[0]
    half, wide = own.shape[0], inner_out.shape[1]
    for begin, ref in ((upper, own), (1 - upper, rest)):
        span = pl.ds(pl.multiple_of(begin * half, half), half)
        inner_out[span, :] = ref[:, :wide].astype(F32)
        o_out[:, span] = ref[:, wide:].astype(F32)


def finish_attention_kernel(bit_ref, own, rest, q_out, k_out, v_out, *vector_outs):
    upper = bit_ref[0]
    half, local = own.shape[0], q_out.shape[1]
    for begin, ref in ((upper, own), (1 - upper, rest)):
        span = pl.ds(pl.multiple_of(begin * half, half), half)
        q_out[span, :] = ref[:, :local].astype(F32)
        k_out[span, :] = ref[:, local : 2 * local].astype(F32)
        v_out[span, :] = ref[:, 2 * local : 3 * local].astype(F32)

        @pl.when(begin == 0)
        def _():
            tail = ref[:128, 3 * local :].astype(F32)
            tail = tail + pltpu.roll(tail, HEAD_DIM, 1)
            lane = lax.broadcasted_iota(jnp.int32, (1, PAIR), 1)
            line = 0
            for out in vector_outs:
                for index in range(out.shape[0] // PAIR):
                    value = jnp.where(
                        lane < HEAD_DIM, tail[line : line + 1, :], tail[line + 1 : line + 2, :]
                    )
                    out[index * PAIR : (index + 1) * PAIR] = value[0, :]
                    line += 2


def halves_of(place, rows):
    half = rows // 2
    bit = place[2]
    return (
        pl.multiple_of((1 - bit) * half, half), pl.multiple_of(bit * half, half)
    )


def weight_grad_kernel(place, left0, left1, right0, right1, send_out, keep_out):
    half = left0.shape[1] // 2
    for begin, out in zip(halves_of(place, 2 * half), (send_out, keep_out)):
        span = pl.ds(begin, half)
        out[...] = (
            dot(left0[:, span], right0[...], TN) + dot(left1[:, span], right1[...], TN)
        ).astype(BF16)


def inner_weight_kernel(
    place, first0, first1, pre0, pre1, low0, low1, low2, attn0, attn1, send_out, keep_out
):
    half = first0.shape[1] // 2
    wide = pre0.shape[1]
    lows = jnp.concatenate([low0[...], low1[...], low2[...]], axis=1)
    for begin, out in zip(halves_of(place, 2 * half), (send_out, keep_out)):
        span = pl.ds(begin, half)
        out[:, :wide] = (
            dot(first0[:, span], pre0[...], TN) + dot(first1[:, span], pre1[...], TN)
        ).astype(BF16)
        out[:, wide:] = (
            dot(lows[:TILE], attn0[:, span], TN) + dot(lows[TILE:], attn1[:, span], TN)
        ).astype(BF16)


def attention_weight_kernel(*refs):
    place, tokens = refs[:2]
    grads = refs[2:11]
    second0, second1, first0, first1, inner0, inner1 = refs[11:17]
    send_out, keep_out, vectors = refs[17:]
    width = tokens.shape[1]
    half = width // 2
    vectors[...] = jnp.zeros_like(vectors)
    rows_of = []
    for left, right in ((second0, second1), (first0, first1)):
        for index in range(3):
            rows_of.append(left[index : index + 1, :] + right[index : index + 1, :])
    rows_of.append(inner0[0:1, :] + inner1[0:1, :])
    for grad in grads:
        rows_of.append(sum_rows(grad[...]))
    line = 0
    for value in rows_of:
        for index in range(value.shape[1] // PAIR):
            piece = value[:, index * PAIR : (index + 1) * PAIR]
            vectors[line : line + 1, :] = piece
            vectors[line + 1 : line + 2, :] = pltpu.roll(piece, HEAD_DIM, 1)
            line += 2
    tail = high_and_low(vectors[...], pltpu.roll)
    together = jnp.concatenate([ref[...] for ref in grads], axis=1)
    main = together.shape[1]
    for begin, out in zip(halves_of(place, width), (send_out, keep_out)):
        span = pl.ds(begin, half)
        out[:, :main] = dot(tokens[:, span], together, TN).astype(BF16)
        out[:, main:] = jnp.where(begin == 0, tail, 0).astype(BF16)


def high_and_low(value, roll):
    high = value.astype(BF16).astype(F32)
    return jnp.where(head_mask(value.shape, 0), high, roll(value - high, HEAD_DIM, 1))


def add_two(one, two, tail, roll):
    one, two = one.astype(F32), two.astype(F32)
    if not tail:
        return (one + two).astype(BF16)
    main = one.shape[1] - PAIR
    rest = one[:, main:] + two[:, main:]
    rest = high_and_low(rest + roll(rest, HEAD_DIM, 1), roll)
    return jnp.concatenate([(one[:, :main] + two[:, :main]).astype(BF16), rest.astype(BF16)], axis=1)


def fold(bit, keep, received, split, tail):
    rows, width = keep.shape
    half = rows // 2
    if not split:

        def add_kernel(one, two, out):
            out[...] = add_two(one[...], two[...], tail, pltpu.roll)

        return call(add_kernel, [keep, received], [((rows, width), BF16)], cost=2.0)[0]
    if half % 16:
        total = add_two(keep, received, tail, jnp.roll)
        return [
            lax.dynamic_slice_in_dim(total, start * half, half, 0) for start in (1 - bit, bit)
        ]

    def fold_kernel(bit_ref, one, two, send_out, keep_out):
        upper = bit_ref[0]
        for begin, out in ((1 - upper, send_out), (upper, keep_out)):
            span = pl.ds(pl.multiple_of(begin * half, half), half)
            out[...] = add_two(one[span, :], two[span, :], tail, pltpu.roll)

    return call(
        fold_kernel, [bit.reshape(1), keep, received], [((half, width), BF16)] * 2, scalars=1,
        cost=2.0,
    )


def join(bit, own, received, dtype=BF16):
    half, width = own.shape
    if half % 16:
        ordered = jnp.where(
            bit == 1,
            jnp.concatenate([received, own], axis=0),
            jnp.concatenate([own, received], axis=0),
        )
        return ordered.astype(dtype)

    def join_kernel(bit_ref, one, two, out):
        upper = bit_ref[0]
        out[pl.ds(pl.multiple_of(upper * half, half), half), :] = one[...].astype(dtype)
        out[pl.ds(pl.multiple_of((1 - upper) * half, half), half), :] = two[...].astype(dtype)

    return call(
        join_kernel, [bit.reshape(1), own, received], [((2 * half, width), dtype)], scalars=1,
        cost=2.0, final=dtype == F32,
    )[0]


def flip(value, axis, bit):
    size = lax.axis_size(axis)
    return lax.ppermute(value, axis, [(i, i ^ bit) for i in range(size)])


class Sum:
    def __init__(self, pieces, stages, bits, tail=False):
        send, self.value = pieces
        self.tail, self.stages, self.bits, self.index = tail, stages, bits, 0
        self.received = flip(send, *stages[0])

    def step(self):
        stages, index, count = self.stages, self.index, len(self.stages)
        if index == 2 * count - 2:
            return
        self.index += 1
        if index < count - 2:
            stage = stages[index + 1]
            send, self.value = fold(self.bits[stage], self.value, self.received, True, self.tail)
            self.received = flip(send, *stage)
            return
        if index < count:
            self.value = fold(None, self.value, self.received, False, self.tail)
        else:
            self.value = join(self.bits[stages[2 * count - 2 - index]], self.value, self.received)
        self.received = flip(self.value, *stages[count - 1 if index == count - 2 else 2 * count - 3 - index])

    def finish(self):
        while self.index < 2 * len(self.stages) - 2:
            self.step()
        return self.value, self.received


def per_device(
    tokens, out_grad, lengths, query_weight, query_bias, key_weight, key_bias, value_weight,
    value_bias, output_weight, output_bias, first_gain, first_shift, inner_weight, inner_bias,
    outer_weight, outer_bias, second_gain, second_shift,
):
    Order.last = None
    rows, width = tokens.shape
    local = query_weight.shape[1]
    pairs = local // PAIR
    hidden_width = inner_weight.shape[1]
    chunks = rows // TILE
    units = hidden_width // 512
    ctx_size, dp_size = lax.axis_size("ctx"), lax.axis_size("dp")
    me = lax.axis_index("ctx")
    spot = jnp.arange(8)
    place = jnp.pad(lengths[0], (3, 5 - lengths.shape[1])) + jnp.where(
        spot == 0, me, jnp.where(spot == 1, ctx_size, jnp.where(spot == 2, me & 1, 0))
    )
    stage_bits = [
        (axis, 1 << i)
        for axis, size in (("ctx", ctx_size), ("dp", dp_size))
        for i in range((size - 1).bit_length())
    ]
    bits = {
        (axis, bit): ((lax.axis_index(axis) & bit) != 0).astype(jnp.int32)
        for axis, bit in stage_bits
    }
    ctx_stages = [stage for stage in stage_bits if stage[0] == "ctx"]

    frequency = 10000.0 ** (-2.0 * np.arange(HEAD_DIM // 2) / HEAD_DIM)
    lanes = np.tile(frequency, PAIR // (HEAD_DIM // 2))
    angles = np.arange(rows)[:, None] * lanes[None, :]
    trig = jnp.asarray(
        np.concatenate([np.cos(angles), np.sin(angles), np.tile(lanes, (8, 1))]), F32
    )

    weights = [query_weight, key_weight, value_weight, query_bias, key_bias, value_bias]
    owns, fars, mates = [], [], []
    reach = ctx_size // 2
    around = [(i, (i + reach) % ctx_size) for i in range(ctx_size)]
    table = ((rows, PAIR), F32)
    places = [(group, slot) for group, pair_list in enumerate(GROUPS) for slot in range(len(pair_list))]
    for index, group in enumerate(GROUPS):
        shapes = [
            ((rows, 3 * PAIR * len(group)), BF16), ((rows, 2 * PAIR * len(group)), BF16),
        ]
        if index == 0:
            sources = [tokens, *weights]
            own, sent, cosine, sine, *copied = call(
                first_project_kernel, [place, trig, *sources],
                shapes + [table, table] + [(value.shape, value.dtype) for value in sources],
                scratch=[
                    pltpu.VMEM(trig.shape, F32), pltpu.SemaphoreType.DMA((1 + len(sources),)),
                ],
                scalars=1, hbm=1 + len(sources), cost=3.0,
            )
            tokens, weights = copied[0], copied[1:]
        else:
            own, sent = call(
                project_kernel(group), [place, tokens, *weights, cosine, sine], shapes,
                scalars=1, cost=1.0,
            )
        owns.append(own)
        fars.append(lax.ppermute(sent, "ctx", around))

    lows, logs, highs, crosses = [], [], [], []

    def load(*values):
        return call(
            load_kernel, values, [(value.shape, value.dtype) for value in values],
            scratch=[pltpu.SemaphoreType.DMA((len(values),))], hbm=len(values), cost=2.0,
        )

    def exchange(index):
        if index:
            owns[index], fars[index], _ = lax.optimization_barrier(
                (owns[index], fars[index], lows[0])
            )
        else:
            fars[0], _ = lax.optimization_barrier((fars[0], owns[-1]))
        mates.append(flip(owns[index], "ctx", 1))
        crosses.append(flip(fars[index], "ctx", 1))

    exchange(0)
    output_bias = load(output_bias)[0]
    for index, slot in places:
        low, lse, high = call(
            attend_kernel(slot),
            [place, owns[index], mates[index], fars[index], crosses[index]],
            [((rows, PAIR), BF16), ((2, rows), F32), ((PAIR, rows), F32)],
            scratch=[
                pltpu.VMEM((2, PAIR, rows), BF16), pltpu.VMEM((2, rows), F32),
                pltpu.VMEM((2, rows), F32), pltpu.VMEM((PAIR, rows), F32),
            ],
            scalars=1, cost=4.0,
        )
        lows.append(low)
        logs.append(lse)
        highs.append(high)
        if len(lows) == 1:
            for later in range(1, len(GROUPS)):
                exchange(later)
    attn_parts = call(
        output_kernel, [*lows, output_weight], [((TILE, width), BF16)] * chunks, cost=1.0
    )

    def swap(value):
        return flip(value, "tensor", 1)

    inner_weight, outer_weight = load(inner_weight, outer_weight)
    attn_parts = list(attn_parts)
    attn_parts[1:] = lax.optimization_barrier((attn_parts[1:], inner_weight))[0]

    block = ((TILE, width), BF16)
    wide = ((TILE, hidden_width), BF16)
    attn_others = [swap(part) for part in attn_parts]
    forward = []
    for chunk in range(chunks):
        forward.append(
            call(
                forward_kernel(chunk, units),
                [
                    tokens, attn_parts[chunk], attn_others[chunk], output_bias, first_gain,
                    first_shift, inner_weight, inner_bias, outer_weight,
                ],
                [block, ((TILE, 1), F32), block, wide, wide, block],
                cost=3.5,
            )
        )
    normed, inverse, first_low, hidden, slope, ffn_parts = zip(*forward)
    ffn_others = [swap(part) for part in ffn_parts]
    backward = []
    for chunk in range(chunks):
        backward.append(
            call(
                backward_kernel(chunk, units),
                [
                    normed[chunk], ffn_parts[chunk], ffn_others[chunk], out_grad, first_gain,
                    first_shift, outer_bias, second_gain, second_shift, slope[chunk],
                    inner_weight, outer_weight,
                ],
                [
                    block, block, wide, block, ((8, width), F32), ((8, hidden_width), F32),
                ],
                cost=3.0,
            )
        )
    layer_out, ffn_grad, pre_grad, first_parts, second_sums, inner_sums = zip(*backward)
    first_others = [swap(part) for part in first_parts]

    back_reach = [(i + reach, i) for i in range(ctx_size - reach)]
    attn_grad, first_sums, head_grad = [], [], []
    for chunk in range(chunks):
        grad, head_part, sums = call(
            middle_kernel(chunk),
            [
                ffn_grad[chunk], first_parts[chunk], first_others[chunk], normed[chunk],
                inverse[chunk], first_gain, output_weight, *highs, *logs, *head_grad[-1:],
            ],
            [block, (((chunk + 1) * GRAD_ROWS, local), BF16), ((8, width), F32)],
            scratch=[pltpu.VMEM((16, TILE), F32)],
            cost=1.5,
        )
        attn_grad.append(grad)
        first_sums.append(sums)
        head_grad.append(head_part)
        if chunk == 0:
            outer_half = ((hidden_width // 2, width), BF16)
            outer_pieces = call(
                weight_grad_kernel, [place, *hidden, *ffn_grad], [outer_half] * 2, scalars=1, cost=2.0
            )
            outer_sum = Sum(outer_pieces, stage_bits, bits)
    head_grad = head_grad[-1]
    grad_far = lax.ppermute(head_grad, "ctx", back_reach)
    grad_mate = flip(head_grad, "ctx", 1)
    outer_sum.step()
    inner_half = ((width // 2, hidden_width + local), BF16)
    inner_pieces = call(
        inner_weight_kernel, [place, *first_low, *pre_grad, *lows, *attn_grad],
        [inner_half] * 2, scalars=1, cost=2.0,
    )
    inner_sum = Sum(inner_pieces, stage_bits, bits)

    q_grads, k_grads, v_grads, key_parts = [], [], [], []
    double = pltpu.VMEM((2, rows, PAIR), BF16)
    single = pltpu.VMEM((rows, PAIR), F32)

    def query_side(pair):
        index, slot = places[pair]
        q_grad, k_part, v_part = call(
            query_side_kernel(pair, slot),
            [
                place, owns[index], head_grad, mates[index], fars[index], crosses[index],
                cosine, sine,
            ],
            [((rows, PAIR), BF16), table, table],
            scratch=[
                double, double, pltpu.VMEM((16, rows), F32), pltpu.VMEM((PAIR, rows), F32),
            ],
            scalars=1, cost=4.0,
        )
        q_grads.append(q_grad)
        key_parts.append((k_part, v_part))

    def key_side(pair):
        index, slot = places[pair]
        k_grad, v_grad = call(
            key_side_kernel(pair, slot),
            [
                place, owns[index], *key_parts[pair], cosine, sine, mates[index],
                fars[index], crosses[index], grad_mate, grad_far, grad_cross,
            ],
            [((rows, PAIR), BF16)] * 2,
            scratch=[double, double, single, single],
            scalars=1, cost=4.0,
        )
        k_grads.append(k_grad)
        v_grads.append(v_grad)

    query_side(0)
    inner_sum.step()
    query_side(1)
    query_side(2)
    outer_sum.step()
    grad_far, _ = lax.optimization_barrier((grad_far, q_grads[1]))
    grad_cross = flip(grad_far, "ctx", 1)
    key_side(0)
    key_side(1)
    outer_sum.step()
    key_side(2)
    inner_sum.step()
    all_grads = [*q_grads, *k_grads, *v_grads]
    attention_half = ((width // 2, 3 * local + PAIR), BF16)
    attention_sum = Sum(
        call(
            attention_weight_kernel,
            [place, tokens, *all_grads, *second_sums, *first_sums, *inner_sums],
            [attention_half] * 2,
            scratch=[pltpu.VMEM((width // 2, PAIR), F32)],
            scalars=1, cost=2.5,
        ),
        stage_bits, bits, True,
    )
    inner_sum.step()
    attention_sum.step()
    input_part = call(
        input_kernel, [*all_grads, *weights[:3]], [((rows, width), BF16)], cost=1.5
    )[0]
    input_other = swap(input_part)
    outer_sum.step()
    layer_out = call(
        stack_kernel, layer_out, [((rows, width), BF16)], cost=0.3, final=True
    )[0]

    attention_sum.step()
    outer_sum.step()
    inner_sum.step()
    attention_sum.step()
    outer_own, outer_rest = outer_sum.finish()
    inner_sum.step()
    attention_sum.step()
    input_grad = call(
        finish_input_kernel, [input_part, input_other, *attn_grad], [((rows, width), BF16)],
        cost=0.5, final=True,
    )[0]
    core = bits[ctx_stages[0]]
    outer_grad = join(core, outer_own, outer_rest, F32)
    attention_sum.step()
    inner_own, inner_rest = inner_sum.finish()
    inner_grad, o_weight_grad = call(
        finish_inner_kernel, [core.reshape(1), inner_own, inner_rest],
        [((width, hidden_width), F32), ((local, width), F32)], scalars=1, cost=2.0, final=True,
    )
    attention_own, attention_rest = attention_sum.finish()
    vector_sizes = [width] * 6 + [hidden_width] + [local] * 3
    (
        q_weight_grad, k_weight_grad, v_weight_grad,
        second_gain_grad, second_shift_grad, outer_bias_grad,
        first_gain_grad, first_shift_grad, output_bias_grad, inner_bias_grad,
        q_bias_grad, k_bias_grad, v_bias_grad,
    ) = call(
        finish_attention_kernel,
        [core.reshape(1), attention_own, attention_rest],
        [((width, local), F32)] * 3 + [((size,), F32) for size in vector_sizes],
        scalars=1, cost=2.0, final=True,
    )
    return (
        layer_out, input_grad,
        q_weight_grad, q_bias_grad, k_weight_grad, k_bias_grad, v_weight_grad, v_bias_grad,
        o_weight_grad, output_bias_grad, first_gain_grad, first_shift_grad,
        inner_grad, inner_bias_grad, outer_grad, outer_bias_grad,
        second_gain_grad, second_shift_grad,
    )


def solution(mesh):
    rows_spec, column_spec, row_spec = P(("dp", "ctx"), None), P(None, "tensor"), P("tensor", None)
    return jax.shard_map(
        per_device,
        mesh=mesh,
        in_specs=(
            rows_spec, rows_spec, P("dp", None),
            column_spec, P("tensor"), column_spec, P("tensor"), column_spec, P("tensor"),
            row_spec, P(), P(), P(), column_spec, P("tensor"), row_spec, P(), P(), P(),
        ),
        out_specs=(
            rows_spec, rows_spec,
            column_spec, P("tensor"), column_spec, P("tensor"), column_spec, P("tensor"),
            row_spec, P(), P(), P(), column_spec, P("tensor"), row_spec, P(), P(), P(),
        ),
        check_vma=False,
    )
```

```python
import jax
import jax.numpy as jnp
import numpy as np
from jax import lax
from jax.experimental import pallas as pl
from jax.experimental.pallas import tpu as pltpu
from jax.sharding import PartitionSpec as P

HEAD_DIM = 64
PAIR = 2 * HEAD_DIM
MASKED = -1e30
EPSILON = 1e-06
TILE = 256
GRAD_ROWS = TILE + 48
GROUPS = ((0, 1), (2,))
F32 = jnp.float32
BF16 = jnp.bfloat16
VMEM_BYTES = 12 * 1024 * 1024
FINAL = pltpu.HBM

NN = (((1,), (0,)), ((), ()))
NT = (((1,), (1,)), ((), ()))
TN = (((0,), (0,)), ((), ()))


def dot(left, right, dims=NN):
    return lax.dot_general(left, right, dims, preferred_element_type=F32)


class Order:
    last = None


def call(kernel, inputs, outputs, scratch=(), scalars=0, hbm=0, cost=1.0, ordered=True, final=False, after=()):
    spaces = [pltpu.SMEM] * scalars + [pltpu.VMEM] * (len(inputs) - scalars - hbm)
    spaces += [pltpu.HBM] * hbm
    inputs = list(inputs)
    for index in range(len(inputs) - hbm, len(inputs)):
        inputs[index] = pltpu.with_memory_space_constraint(inputs[index], pltpu.HBM)
    body = kernel
    extra = list(after)
    if ordered and Order.last is not None:
        extra.append(Order.last)
    if extra:
        count = len(inputs)
        inputs += extra
        spaces += [pl.ANY] * len(extra)

        def body(*refs):
            kernel(*refs[:count], *refs[count + len(extra) :])

    results = pl.pallas_call(
        body,
        in_specs=[pl.BlockSpec(memory_space=space) for space in spaces],
        out_specs=[pl.BlockSpec(memory_space=pltpu.VMEM)] * len(outputs),
        out_shape=[
            FINAL(dims, dtype) if final else jax.ShapeDtypeStruct(dims, dtype)
            for dims, dtype in outputs
        ],
        scratch_shapes=list(scratch),
        compiler_params=pltpu.CompilerParams(vmem_limit_bytes=VMEM_BYTES),
        cost_estimate=pl.CostEstimate(
            flops=int(cost * 1e10), bytes_accessed=int(cost * 1e13), transcendentals=0
        ),
    )(*inputs)
    if ordered:
        Order.last = min(results, key=lambda value: value.size * value.dtype.itemsize)
        if final:
            Order.last = pltpu.with_memory_space_constraint(Order.last, pltpu.HBM)
    return results


def tile(index):
    return pl.ds(index * TILE, TILE)


def sum_rows(value):
    return jnp.sum(value.astype(F32), axis=0, keepdims=True)


def mean(value):
    return jnp.mean(value, axis=-1, keepdims=True)


def normalize(rows_in):
    centered = rows_in - mean(rows_in)
    inverse = lax.rsqrt(mean(centered * centered) + EPSILON)
    return centered * inverse, inverse


def norm_back(grad, normed, inverse):
    return inverse * (grad - mean(grad) - normed * mean(grad * normed))


def swap_halves(value):
    lane = lax.broadcasted_iota(jnp.int32, value.shape, 1)
    ahead = pltpu.roll(value, PAIR - HEAD_DIM // 2, 1)
    behind = pltpu.roll(value, HEAD_DIM // 2, 1)
    return jnp.where(lane % HEAD_DIM < HEAD_DIM // 2, ahead, behind)


def window(ref, slot, parts):
    return ref.at[:, slot * parts * PAIR : (slot + 1) * parts * PAIR]


def head_mask(shape, head):
    lane = lax.broadcasted_iota(jnp.int32, shape, 1)
    return (lane // HEAD_DIM) == head


class Layout:
    def __init__(self, place, rows):
        self.me = place[0]
        self.rows = rows
        self.offset = self.me * rows
        self.end0 = place[3]
        self.end1 = self.end0 + place[4]

    def start(self, index):
        return jnp.where(
            index >= self.end1, self.end1, jnp.where(index >= self.end0, self.end0, 0)
        )

    def allowed(self, query_row, queries, key_row, keys):
        query = query_row + lax.broadcasted_iota(jnp.int32, (1, queries), 1)
        key = key_row + lax.broadcasted_iota(jnp.int32, (keys, 1), 0)
        return (key >= self.start(query)) & (key <= query)


def project_tables(place, table, cos_out, sin_out):
    rows = cos_out.shape[0]
    base_cos, base_sin, freq = table[:rows, :], table[rows : 2 * rows, :], table[2 * rows :, :]
    where = Layout(place, rows)
    row = where.offset + lax.broadcasted_iota(jnp.int32, (rows, 1), 0)
    turns = []
    for start in (0, where.end0, where.end1):
        angle = (where.offset - start).astype(F32) * freq
        turns.append((jnp.cos(angle)[0:1, :], jnp.sin(angle)[0:1, :]))
    late, later = row >= where.end0, row >= where.end1
    cos_turn = jnp.where(later, turns[2][0], jnp.where(late, turns[1][0], turns[0][0]))
    sin_turn = jnp.where(later, turns[2][1], jnp.where(late, turns[1][1], turns[0][1]))
    cosine = base_cos * cos_turn - base_sin * sin_turn
    sine = base_sin * cos_turn + base_cos * sin_turn
    lane = lax.broadcasted_iota(jnp.int32, (rows, PAIR), 1)
    cos_out[...] = cosine
    sin_out[...] = jnp.where(lane % HEAD_DIM < HEAD_DIM // 2, -sine, sine)


def project_group(group, place, tokens, wq, wk, wv, bq, bk, bv, cos, sin, own_out, far_out):
    cosine, sine = cos[...], sin[...]
    onward = place[0] < place[1] // 2
    for slot, pair in enumerate(group):
        span = slice(pair * PAIR, (pair + 1) * PAIR)
        weight = jnp.concatenate([wq[:, span], wk[:, span], wv[:, span]], axis=1)
        pre = dot(tokens[...], weight)
        query = pre[:, :PAIR] + bq[span].reshape(1, PAIR)
        key = pre[:, PAIR : 2 * PAIR] + bk[span].reshape(1, PAIR)
        query = (query * cosine + swap_halves(query) * sine).astype(BF16)
        key = (key * cosine + swap_halves(key) * sine).astype(BF16)
        value = (pre[:, 2 * PAIR :] + bv[span].reshape(1, PAIR)).astype(BF16)
        own, far = window(own_out, slot, 3), window(far_out, slot, 2)
        own[:, :PAIR] = query
        own[:, PAIR : 2 * PAIR] = key
        own[:, 2 * PAIR :] = value
        far[:, :PAIR] = jnp.where(onward, key, query)
        far[:, PAIR:] = jnp.where(onward, value, query)


def first_project_kernel(place, *refs):
    count = (len(refs) - 7) // 2
    sources, (own_out, far_out, cos_out, sin_out) = refs[:count + 1], refs[count + 1 : count + 5]
    copies, table, sems = refs[count + 5 : 2 * count + 5], refs[-2], refs[-1]
    moves = [
        pltpu.make_async_copy(source, target, sems.at[index])
        for index, (source, target) in enumerate(zip(sources, (table, *copies)))
    ]
    for move in moves:
        move.start()
    moves[0].wait()
    project_tables(place, table, cos_out, sin_out)
    for move in moves[1:]:
        move.wait()
    project_group(GROUPS[0], place, *copies, cos_out, sin_out, own_out, far_out)


def load_kernel(*refs):
    count = len(refs) // 2
    moves = [
        pltpu.make_async_copy(refs[index], refs[count + index], refs[-1].at[index])
        for index in range(count)
    ]
    for move in moves:
        move.start()
    for move in moves:
        move.wait()


def output_kernel(
    low0, low1, low2, other0, other1, wo, wo_other, w_in, w_out,
    attn_out, w_in_out, w_out_out, sems,
):
    moves = [
        pltpu.make_async_copy(source, target, sems.at[index])
        for index, (source, target) in enumerate(((w_in, w_in_out), (w_out, w_out_out)))
    ]
    for move in moves:
        move.start()
    low = jnp.concatenate([low0[...], low1[...], low2[...]], axis=1)
    other = jnp.concatenate([other0[...], other1[...]], axis=1)
    attn_out[...] = dot(low, wo[...]) + dot(other, wo_other[: 2 * PAIR, :])
    for move in moves:
        move.wait()


def project_kernel(group):
    def kernel(*refs):
        project_group(group, *refs)

    return kernel


def attend_kernel(slot):
    def kernel(
        place, own, mate, far, cross,
        low_out, lse_out, high, q_masked, peak, total, accum,
    ):
        own, mate = window(own, slot, 3), window(mate, slot, 3)
        far, cross = window(far, slot, 2), window(cross, slot, 2)
        rows = own.shape[0]
        where = Layout(place, rows)
        turned_q = own[:, :PAIR].astype(F32).T * 0.125
        for head in range(2):
            other = slice(HEAD_DIM * (1 - head), HEAD_DIM * (2 - head))
            mine = slice(HEAD_DIM * head, HEAD_DIM * (head + 1))
            q_masked[head, mine, :] = turned_q[mine, :].astype(BF16)
            q_masked[head, other, :] = jnp.zeros((HEAD_DIM, rows), BF16)

        def visit(keys, values, key_row, query, width, first):
            turned = values.astype(F32).T.astype(BF16)
            lanes = pl.ds(query, width)
            mask = where.allowed(where.offset + query, width, key_row, keys.shape[0])
            for head in range(2):
                span = slice(HEAD_DIM * head, HEAD_DIM * (head + 1))
                scores = dot(keys, q_masked[head, :, lanes])
                scores = jnp.where(mask, scores, MASKED)
                top = jnp.max(scores, axis=0, keepdims=True)
                if not first:
                    old = peak[head : head + 1, lanes]
                    top = jnp.maximum(old, top)
                    decay = jnp.exp(old - top)
                prob = jnp.exp(scores - top)
                sums = jnp.sum(prob, axis=0, keepdims=True)
                product = dot(turned[span, :], prob.astype(BF16))
                if not first:
                    sums += total[head : head + 1, lanes] * decay
                    product += accum[span, lanes] * decay
                peak[head : head + 1, lanes] = top
                total[head : head + 1, lanes] = sums
                accum[span, lanes] = product

        half = rows // 2
        visit(
            own[:half, PAIR : 2 * PAIR], own[:half, 2 * PAIR :], where.offset, 0, rows, True
        )
        visit(
            own[half:, PAIR : 2 * PAIR], own[half:, 2 * PAIR :], where.offset + half, half, half,
            False,
        )
        first_start = where.start(where.offset)

        @pl.when(first_start < where.offset)
        def _():
            odd = (where.me & 1) == 1
            visit(
                jnp.where(odd, mate[:, PAIR : 2 * PAIR], cross[:, :PAIR]),
                jnp.where(odd, mate[:, 2 * PAIR :], cross[:, PAIR:]), where.offset - rows,
                0, rows, False,
            )

        @pl.when(first_start < where.offset - rows)
        def _():
            base = where.offset - 2 * rows
            visit(far[half:, :PAIR], far[half:, PAIR:], base + half, 0, rows, False)
            visit(far[:half, :PAIR], far[:half, PAIR:], base, 0, half, False)

        for head in range(2):
            sums = total[head : head + 1, :]
            lse_out[head : head + 1, :] = peak[head : head + 1, :] + jnp.log(sums)
            span = slice(HEAD_DIM * head, HEAD_DIM * (head + 1))
            high[span, :] = accum[span, :] / sums
        low_out[...] = high[...].T.astype(BF16)

    return kernel


def forward_kernel(chunk, units):
    def kernel(
        tokens, attn_part, other, wo_other, bias, gain, shift, w_in, b_in, w_out,
        normed_out, inverse_out, first_out, hidden_out, slope_out, part_out,
    ):
        width = tokens.shape[1]
        last = wo_other.shape[0] - PAIR
        attn = attn_part[tile(chunk), :] + dot(other[tile(chunk), :], wo_other[last:, :])
        attn += bias[...].reshape(1, width)
        normed, inverse = normalize(tokens[tile(chunk), :].astype(F32) + attn)
        normed_out[...] = normed.astype(BF16)
        inverse_out[...] = inverse
        first = normed * gain[...].reshape(1, width) + shift[...].reshape(1, width)
        first_low = first.astype(BF16)
        first_out[...] = first_low
        total = None
        unit = w_in.shape[1] // units
        for index in range(units):
            span = slice(index * unit, (index + 1) * unit)
            pre = dot(first_low, w_in[:, span]) + b_in[span].reshape(1, unit)
            cdf = 0.5 * (1.0 + lax.erf(pre * 0.7071067811865476))
            density = jnp.exp(-0.5 * pre * pre) * 0.3989422804014327
            hidden = (pre * cdf).astype(BF16)
            hidden_out[:, span] = hidden
            slope_out[:, span] = (cdf + pre * density).astype(BF16)
            product = dot(hidden, w_out[span, :])
            total = product if total is None else total + product
        part_out[...] = total.astype(BF16)

    return kernel


def backward_kernel(chunk, units):
    def kernel(
        normed_first, part, other, out_grad, first_gain, first_shift, bias, gain, shift,
        slope, w_in, w_out,
        layer_out, ffn_grad_out, pre_grad_out, part_out, sums_out, inner_out,
    ):
        width = part.shape[1]

        def row(ref):
            return ref[...].reshape(1, width)

        first = normed_first[...].astype(F32) * row(first_gain) + row(first_shift)
        ffn = part[...].astype(F32) + other[...].astype(F32) + row(bias)
        normed, inverse = normalize(first + ffn)
        layer_out[...] = (normed * row(gain) + row(shift)).astype(BF16)
        upstream = out_grad[tile(chunk), :].astype(F32)
        res_grad = norm_back(upstream * row(gain), normed, inverse)
        ffn_grad = res_grad.astype(BF16)
        ffn_grad_out[...] = ffn_grad
        sums_out[0:1, :] = sum_rows(upstream * normed)
        sums_out[1:2, :] = sum_rows(upstream)
        sums_out[2:3, :] = sum_rows(ffn_grad)
        total = None
        unit = w_in.shape[1] // units
        for index in range(units):
            span = slice(index * unit, (index + 1) * unit)
            hidden_grad = dot(ffn_grad, w_out[span, :], NT)
            pre_grad = (hidden_grad * slope[:, span].astype(F32)).astype(BF16)
            pre_grad_out[:, span] = pre_grad
            inner_out[0:1, span] = sum_rows(pre_grad)
            product = dot(pre_grad, w_in[:, span], NT)
            total = product if total is None else total + product
        part_out[...] = total.astype(BF16)

    return kernel


def split_three(value):
    high = value.astype(BF16)
    rest = value - high.astype(F32)
    middle = rest.astype(BF16)
    return high, middle, (rest - middle.astype(F32)).astype(BF16)


def middle_kernel(chunk):
    def kernel(
        ffn_grad, part, other, normed, inverse, gain, wo, high0, high1, high2, lse0, lse1, lse2,
        *rest,
    ):
        grad_out, head_out, sums_out, stats = rest[-4:]
        base = chunk * GRAD_ROWS
        if chunk:
            head_out[:base, :] = rest[0][...]
        width = part.shape[1]
        local = wo.shape[0]
        first_grad = (
            ffn_grad[...].astype(F32) + part[...].astype(F32) + other[...].astype(F32)
        )
        unit = normed[...].astype(F32)
        res_grad = norm_back(first_grad * gain[...].reshape(1, width), unit, inverse[...])
        attn_grad = res_grad.astype(BF16)
        grad_out[...] = attn_grad
        sums_out[0:1, :] = sum_rows(first_grad * unit)
        sums_out[1:2, :] = sum_rows(first_grad)
        sums_out[2:3, :] = sum_rows(attn_grad)
        head_grad = dot(attn_grad, wo[...], NT).astype(BF16)
        head_out[base : base + TILE, :] = head_grad
        high = jnp.concatenate([ref[:, tile(chunk)] for ref in (high0, high1, high2)], axis=0)
        turned = head_grad.astype(F32).T * high
        stats[...] = jnp.zeros_like(stats)
        for index, lse in enumerate((lse0, lse1, lse2)):
            stats[2 * index : 2 * index + 2, :] = lse[:, tile(chunk)]
        for head in range(local // HEAD_DIM):
            span = slice(HEAD_DIM * head, HEAD_DIM * (head + 1))
            stats[8 + head : 9 + head, :] = jnp.sum(turned[span, :], axis=0, keepdims=True)
        begin = base + TILE
        head_out[begin:, :] = jnp.zeros((GRAD_ROWS - TILE, local), BF16)
        for index, value in enumerate(split_three(stats[...])):
            head_out[begin + 16 * index : begin + 16 * (index + 1), :TILE] = value

    return kernel


def stat_rows(grad, chunk):
    begin = chunk * GRAD_ROWS + TILE
    pieces = [
        grad[begin + 16 * index : begin + 16 * (index + 1), :TILE].astype(F32)
        for index in range(3)
    ]
    return pieces[0] + (pieces[1] + pieces[2])


def pair_terms(keys, values, queries, grads, mask, log_row, dot_row):
    scores = jnp.where(mask, dot(keys, queries, NT), MASKED)
    prob = jnp.exp(scores - log_row)
    prob_grad = dot(values, grads, NT)
    return prob.astype(BF16), (prob * (prob_grad - dot_row)).astype(BF16)


def query_side_kernel(pair, slot):
    pair_span = slice(pair * PAIR, (pair + 1) * PAIR)

    def kernel(
        place, own, grad, mate, far, cross, cos, sin,
        q_grad_out, k_part_out, v_part_out,
        q_masked, grad_masked, stats, q_turned,
    ):
        own, mate = window(own, slot, 3), window(mate, slot, 3)
        far, cross = window(far, slot, 2), window(cross, slot, 2)
        rows = own.shape[0]
        where = Layout(place, rows)
        for index in range(rows // TILE):
            stats[:, tile(index)] = stat_rows(grad, index)
            some = grad[index * GRAD_ROWS : index * GRAD_ROWS + TILE, pair_span]
            for head in range(2):
                mask = head_mask((TILE, PAIR), head)
                q_masked[head, tile(index), :] = jnp.where(
                    mask, own[tile(index), :PAIR] * 0.125, 0
                ).astype(BF16)
                grad_masked[head, tile(index), :] = jnp.where(mask, some, 0).astype(BF16)

        def visit(keys, values, key_row, query, width, own_rows=None, fresh=False):
            turned = keys.astype(F32).T.astype(BF16)
            lanes = pl.ds(query, width)
            mask = where.allowed(where.offset + query, width, key_row, keys.shape[0])
            key_sum = value_sum = None
            for head in range(2):
                index = 2 * pair + head
                span = slice(HEAD_DIM * head, HEAD_DIM * (head + 1))
                prob, score_grad = pair_terms(
                    keys, values, q_masked[head, lanes, :], grad_masked[head, lanes, :],
                    mask, stats[index : index + 1, lanes], stats[8 + index : 9 + index, lanes],
                )
                product = dot(turned[span, :], score_grad)
                if fresh:
                    q_turned[span, lanes] = product
                else:
                    q_turned[span, lanes] += product
                if own_rows is not None:
                    key_part = dot(score_grad, q_masked[head, lanes, :])
                    value_part = dot(prob, grad_masked[head, lanes, :])
                    key_sum = key_part if key_sum is None else key_sum + key_part
                    value_sum = value_part if value_sum is None else value_sum + value_part
            if own_rows is not None:
                k_part_out[own_rows, :] = key_sum
                v_part_out[own_rows, :] = value_sum

        half = rows // 2
        low, high = slice(0, half), slice(half, rows)
        visit(
            own[low, PAIR : 2 * PAIR], own[low, 2 * PAIR :], where.offset, 0, rows, low, True
        )
        visit(
            own[high, PAIR : 2 * PAIR], own[high, 2 * PAIR :], where.offset + half, half, half,
            high,
        )
        first_start = where.start(where.offset)

        @pl.when(first_start < where.offset)
        def _():
            odd = (where.me & 1) == 1
            visit(
                jnp.where(odd, mate[:, PAIR : 2 * PAIR], cross[:, :PAIR]),
                jnp.where(odd, mate[:, 2 * PAIR :], cross[:, PAIR:]), where.offset - rows,
                0, rows,
            )

        @pl.when(first_start < where.offset - rows)
        def _():
            base = where.offset - 2 * rows
            visit(far[high, :PAIR], far[high, PAIR:], base + half, 0, rows)
            visit(far[low, :PAIR], far[low, PAIR:], base, 0, half)

        turned = q_turned[...].T * 0.125
        q_grad_out[...] = (turned * cos[...] - swap_halves(turned) * sin[...]).astype(BF16)

    return kernel


def key_side_kernel(pair, slot):
    pair_span = slice(pair * PAIR, (pair + 1) * PAIR)

    def kernel(
        place, own, k_part, v_part, cos, sin, mate, far, cross,
        grad_mate, grad_far, grad_cross,
        k_grad_out, v_grad_out,
        k_masked, v_masked, k_turned, v_sum,
    ):
        own, mate = window(own, slot, 3), window(mate, slot, 3)
        far, cross = window(far, slot, 2), window(cross, slot, 2)
        rows = own.shape[0]
        where = Layout(place, rows)
        span_rows = place[1] * rows
        end = where.offset + rows
        k_turned[...] = k_part[...]
        v_sum[...] = v_part[...]

        def some(ref, chunk):
            return ref[chunk * GRAD_ROWS : chunk * GRAD_ROWS + TILE, pair_span]

        near = (end < span_rows) & (where.start(end) < end)
        beyond = (end + rows < span_rows) & (where.start(end + rows) < end)

        @pl.when(near)
        def _():
            for head in range(2):
                mask = head_mask((rows, PAIR), head)
                k_masked[head] = jnp.where(mask, own[:, PAIR : 2 * PAIR] * 0.125, 0).astype(BF16)
                v_masked[head] = jnp.where(mask, own[:, 2 * PAIR :], 0).astype(BF16)

        def visit(queries, grads, stats, query_row):
            first_head = head_mask((rows, PAIR), 0)
            for index in range(rows // TILE):
                mask = where.allowed(query_row + index * TILE, TILE, where.offset, rows)
                part = queries[index * TILE : (index + 1) * TILE, :]
                key_parts, value_parts = [], []
                for head in range(2):
                    line = 2 * pair + head
                    prob, score_grad = pair_terms(
                        k_masked[head], v_masked[head], part, grads[index], mask,
                        stats[index][line : line + 1, :], stats[index][8 + line : 9 + line, :],
                    )
                    key_parts.append(dot(score_grad, part))
                    value_parts.append(dot(prob, grads[index]))
                k_turned[...] += jnp.where(first_head, *key_parts) * 0.125
                v_sum[...] += jnp.where(first_head, *value_parts)

        @pl.when(near)
        def _():
            even = (where.me & 1) == 0
            chunks = range(rows // TILE)
            visit(
                jnp.where(even, mate[:, :PAIR], cross[:, :PAIR]),
                [jnp.where(even, some(grad_mate, i), some(grad_cross, i)) for i in chunks],
                [
                    jnp.where(even, stat_rows(grad_mate, i), stat_rows(grad_cross, i))
                    for i in chunks
                ],
                end,
            )

        @pl.when(beyond)
        def _():
            chunks = range(rows // TILE)
            visit(
                far[:, :PAIR], [some(grad_far, i) for i in chunks],
                [stat_rows(grad_far, i) for i in chunks], end + rows,
            )

        turned = k_turned[...]
        k_grad_out[...] = (turned * cos[...] - swap_halves(turned) * sin[...]).astype(BF16)
        v_grad_out[...] = v_sum[...].astype(BF16)

    return kernel


def input_kernel(*refs):
    grads, weights, out = refs[:9], refs[9:12], refs[12]
    total = None
    for index, weight in enumerate(weights):
        value = jnp.concatenate([ref[...] for ref in grads[3 * index : 3 * index + 3]], axis=1)
        product = dot(value, weight[...], NT)
        total = product if total is None else total + product
    out[...] = total.astype(BF16)


def finish_input_kernel(part, other, grad0, grad1, out):
    for index, grad in enumerate((grad0, grad1)):
        rows = tile(index)
        out[rows, :] = (
            part[rows, :].astype(F32) + other[rows, :].astype(F32) + grad[...].astype(F32)
        ).astype(BF16)


def stack_kernel(*refs):
    for index, ref in enumerate(refs[:-1]):
        refs[-1][tile(index), :] = ref[...]


def finish_inner_kernel(bit_ref, own, rest, inner_out, o_out):
    upper = bit_ref[0]
    half, wide = own.shape[0], inner_out.shape[1]
    for begin, ref in ((upper, own), (1 - upper, rest)):
        span = pl.ds(pl.multiple_of(begin * half, half), half)
        inner_out[span, :] = ref[:, :wide].astype(F32)
        o_out[:, span] = ref[:, wide:].astype(F32)


def finish_attention_kernel(bit_ref, own, rest, q_out, k_out, v_out, *vector_outs):
    upper = bit_ref[0]
    half, local = own.shape[0], q_out.shape[1]
    for begin, ref in ((upper, own), (1 - upper, rest)):
        span = pl.ds(pl.multiple_of(begin * half, half), half)
        q_out[span, :] = ref[:, :local].astype(F32)
        k_out[span, :] = ref[:, local : 2 * local].astype(F32)
        v_out[span, :] = ref[:, 2 * local : 3 * local].astype(F32)

        @pl.when(begin == 0)
        def _():
            tail = ref[:128, 3 * local :].astype(F32)
            tail = tail + pltpu.roll(tail, HEAD_DIM, 1)
            lane = lax.broadcasted_iota(jnp.int32, (1, PAIR), 1)
            line = 0
            for out in vector_outs:
                for index in range(out.shape[0] // PAIR):
                    value = jnp.where(
                        lane < HEAD_DIM, tail[line : line + 1, :], tail[line + 1 : line + 2, :]
                    )
                    out[index * PAIR : (index + 1) * PAIR] = value[0, :]
                    line += 2


def halves_of(place, rows):
    half = rows // 2
    bit = place[2]
    return (
        pl.multiple_of((1 - bit) * half, half), pl.multiple_of(bit * half, half)
    )


def weight_grad_kernel(place, left0, left1, right0, right1, send_out, keep_out):
    half = left0.shape[1] // 2
    for begin, out in zip(halves_of(place, 2 * half), (send_out, keep_out)):
        span = pl.ds(begin, half)
        out[...] = (
            dot(left0[:, span], right0[...], TN) + dot(left1[:, span], right1[...], TN)
        ).astype(BF16)


def inner_weight_kernel(
    place, first0, first1, pre0, pre1, low0, low1, low2, attn0, attn1, send_out, keep_out
):
    half = first0.shape[1] // 2
    wide = pre0.shape[1]
    lows = jnp.concatenate([low0[...], low1[...], low2[...]], axis=1)
    for begin, out in zip(halves_of(place, 2 * half), (send_out, keep_out)):
        span = pl.ds(begin, half)
        out[:, :wide] = (
            dot(first0[:, span], pre0[...], TN) + dot(first1[:, span], pre1[...], TN)
        ).astype(BF16)
        out[:, wide:] = (
            dot(lows[:TILE], attn0[:, span], TN) + dot(lows[TILE:], attn1[:, span], TN)
        ).astype(BF16)


def attention_weight_kernel(*refs):
    place, tokens = refs[:2]
    grads = refs[2:11]
    second0, second1, first0, first1, inner0, inner1 = refs[11:17]
    send_out, keep_out, vectors = refs[17:]
    width = tokens.shape[1]
    half = width // 2
    vectors[...] = jnp.zeros_like(vectors)
    rows_of = []
    for left, right in ((second0, second1), (first0, first1)):
        for index in range(3):
            rows_of.append(left[index : index + 1, :] + right[index : index + 1, :])
    rows_of.append(inner0[0:1, :] + inner1[0:1, :])
    for grad in grads:
        rows_of.append(sum_rows(grad[...]))
    line = 0
    for value in rows_of:
        for index in range(value.shape[1] // PAIR):
            piece = value[:, index * PAIR : (index + 1) * PAIR]
            vectors[line : line + 1, :] = piece
            vectors[line + 1 : line + 2, :] = pltpu.roll(piece, HEAD_DIM, 1)
            line += 2
    tail = high_and_low(vectors[...], pltpu.roll)
    together = jnp.concatenate([ref[...] for ref in grads], axis=1)
    main = together.shape[1]
    for begin, out in zip(halves_of(place, width), (send_out, keep_out)):
        span = pl.ds(begin, half)
        out[:, :main] = dot(tokens[:, span], together, TN).astype(BF16)
        out[:, main:] = jnp.where(begin == 0, tail, 0).astype(BF16)


def high_and_low(value, roll):
    high = value.astype(BF16).astype(F32)
    return jnp.where(head_mask(value.shape, 0), high, roll(value - high, HEAD_DIM, 1))


def add_two(one, two, tail, roll):
    one, two = one.astype(F32), two.astype(F32)
    if not tail:
        return (one + two).astype(BF16)
    main = one.shape[1] - PAIR
    rest = one[:, main:] + two[:, main:]
    rest = high_and_low(rest + roll(rest, HEAD_DIM, 1), roll)
    return jnp.concatenate([(one[:, :main] + two[:, :main]).astype(BF16), rest.astype(BF16)], axis=1)


def fold(bit, keep, received, split, tail):
    rows, width = keep.shape
    half = rows // 2
    if not split:

        def add_kernel(one, two, out):
            out[...] = add_two(one[...], two[...], tail, pltpu.roll)

        return call(add_kernel, [keep, received], [((rows, width), BF16)], cost=2.0)[0]
    if half % 16:
        total = add_two(keep, received, tail, jnp.roll)
        return [
            lax.dynamic_slice_in_dim(total, start * half, half, 0) for start in (1 - bit, bit)
        ]

    def fold_kernel(bit_ref, one, two, send_out, keep_out):
        upper = bit_ref[0]
        for begin, out in ((1 - upper, send_out), (upper, keep_out)):
            span = pl.ds(pl.multiple_of(begin * half, half), half)
            out[...] = add_two(one[span, :], two[span, :], tail, pltpu.roll)

    return call(
        fold_kernel, [bit.reshape(1), keep, received], [((half, width), BF16)] * 2, scalars=1,
        cost=2.0,
    )


def join(bit, own, received, dtype=BF16):
    half, width = own.shape
    if half % 16:
        ordered = jnp.where(
            bit == 1,
            jnp.concatenate([received, own], axis=0),
            jnp.concatenate([own, received], axis=0),
        )
        return ordered.astype(dtype)

    def join_kernel(bit_ref, one, two, out):
        upper = bit_ref[0]
        out[pl.ds(pl.multiple_of(upper * half, half), half), :] = one[...].astype(dtype)
        out[pl.ds(pl.multiple_of((1 - upper) * half, half), half), :] = two[...].astype(dtype)

    return call(
        join_kernel, [bit.reshape(1), own, received], [((2 * half, width), dtype)], scalars=1,
        cost=2.0, final=dtype == F32,
    )[0]


def flip(value, axis, bit):
    size = lax.axis_size(axis)
    return lax.ppermute(value, axis, [(i, i ^ bit) for i in range(size)])


class Sum:
    def __init__(self, pieces, stages, bits, tail=False):
        send, self.value = pieces
        self.tail, self.stages, self.bits, self.index = tail, stages, bits, 0
        self.received = flip(send, *stages[0])

    def step(self):
        stages, index, count = self.stages, self.index, len(self.stages)
        if index == 2 * count - 2:
            return
        self.index += 1
        if index < count - 2:
            stage = stages[index + 1]
            send, self.value = fold(self.bits[stage], self.value, self.received, True, self.tail)
            self.received = flip(send, *stage)
            return
        if index < count:
            self.value = fold(None, self.value, self.received, False, self.tail)
        else:
            self.value = join(self.bits[stages[2 * count - 2 - index]], self.value, self.received)
        self.received = flip(self.value, *stages[count - 1 if index == count - 2 else 2 * count - 3 - index])

    def finish(self):
        while self.index < 2 * len(self.stages) - 2:
            self.step()
        return self.value, self.received


def per_device(
    tokens, out_grad, lengths, query_weight, query_bias, key_weight, key_bias, value_weight,
    value_bias, output_weight, output_bias, first_gain, first_shift, inner_weight, inner_bias,
    outer_weight, outer_bias, second_gain, second_shift,
):
    Order.last = None
    rows, width = tokens.shape
    local = query_weight.shape[1]
    pairs = local // PAIR
    hidden_width = inner_weight.shape[1]
    chunks = rows // TILE
    units = hidden_width // 512
    ctx_size, dp_size = lax.axis_size("ctx"), lax.axis_size("dp")
    me = lax.axis_index("ctx")
    spot = jnp.arange(8)
    place = jnp.pad(lengths[0], (3, 5 - lengths.shape[1])) + jnp.where(
        spot == 0, me, jnp.where(spot == 1, ctx_size, jnp.where(spot == 2, me & 1, 0))
    )
    stage_bits = [
        (axis, 1 << i)
        for axis, size in (("ctx", ctx_size), ("dp", dp_size))
        for i in range((size - 1).bit_length())
    ]
    bits = {
        (axis, bit): ((lax.axis_index(axis) & bit) != 0).astype(jnp.int32)
        for axis, bit in stage_bits
    }
    ctx_stages = [stage for stage in stage_bits if stage[0] == "ctx"]

    frequency = 10000.0 ** (-2.0 * np.arange(HEAD_DIM // 2) / HEAD_DIM)
    lanes = np.tile(frequency, PAIR // (HEAD_DIM // 2))
    angles = np.arange(rows)[:, None] * lanes[None, :]
    trig = jnp.asarray(
        np.concatenate([np.cos(angles), np.sin(angles), np.tile(lanes, (8, 1))]), F32
    )

    weights = [query_weight, key_weight, value_weight, query_bias, key_bias, value_bias]
    owns, fars, mates = [], [], []
    reach = ctx_size // 2
    around = [(i, (i + reach) % ctx_size) for i in range(ctx_size)]
    table = ((rows, PAIR), F32)
    def swap(value):
        return flip(value, "tensor", 1)

    weight_other = swap(output_weight)
    places = [(group, slot) for group, pair_list in enumerate(GROUPS) for slot in range(len(pair_list))]
    for index, group in enumerate(GROUPS):
        shapes = [
            ((rows, 3 * PAIR * len(group)), BF16), ((rows, 2 * PAIR * len(group)), BF16),
        ]
        if index == 0:
            sources = [tokens, *weights]
            own, sent, cosine, sine, *copied = call(
                first_project_kernel, [place, trig, *sources],
                shapes + [table, table] + [(value.shape, value.dtype) for value in sources],
                scratch=[
                    pltpu.VMEM(trig.shape, F32), pltpu.SemaphoreType.DMA((1 + len(sources),)),
                ],
                scalars=1, hbm=1 + len(sources), cost=3.0,
            )
            tokens, weights = copied[0], copied[1:]
        else:
            own, sent = call(
                project_kernel(group), [place, tokens, *weights, cosine, sine], shapes,
                scalars=1, cost=1.0,
            )
        owns.append(own)
        fars.append(lax.ppermute(sent, "ctx", around))

    lows, logs, highs, crosses, low_others = [], [], [], [], []

    def load(*values, after=()):
        return call(
            load_kernel, values, [(value.shape, value.dtype) for value in values],
            scratch=[pltpu.SemaphoreType.DMA((len(values),))], hbm=len(values), cost=2.0, after=after,
        )

    def exchange(index):
        if index:
            owns[index], fars[index], _ = lax.optimization_barrier(
                (owns[index], fars[index], lows[0])
            )
        else:
            fars[0], _ = lax.optimization_barrier((fars[0], owns[-1]))
        mates.append(flip(owns[index], "ctx", 1))
        crosses.append(flip(fars[index], "ctx", 1))

    exchange(0)
    output_bias = load(output_bias)[0]
    for index, slot in places:
        low, lse, high = call(
            attend_kernel(slot),
            [place, owns[index], mates[index], fars[index], crosses[index]],
            [((rows, PAIR), BF16), ((2, rows), F32), ((PAIR, rows), F32)],
            scratch=[
                pltpu.VMEM((2, PAIR, rows), BF16), pltpu.VMEM((2, rows), F32),
                pltpu.VMEM((2, rows), F32), pltpu.VMEM((PAIR, rows), F32),
            ],
            scalars=1, cost=4.0, after=low_others[:1] if len(lows) == 2 else (),
        )
        lows.append(low)
        low_others.append(swap(low))
        logs.append(lse)
        highs.append(high)
        if len(lows) == 1:
            for later in range(1, len(GROUPS)):
                exchange(later)
    attn_part, inner_weight, outer_weight = call(
        output_kernel,
        [
            *lows, *low_others[: pairs - 1], output_weight, weight_other, inner_weight,
            outer_weight,
        ],
        [((rows, width), F32)]
        + [(value.shape, value.dtype) for value in (inner_weight, outer_weight)],
        scratch=[pltpu.SemaphoreType.DMA((2,))], hbm=2, cost=2.0,
    )
    block = ((TILE, width), BF16)
    wide = ((TILE, hidden_width), BF16)
    forward = []
    for chunk in range(chunks):
        forward.append(
            call(
                forward_kernel(chunk, units),
                [
                    tokens, attn_part, low_others[-1], weight_other, output_bias, first_gain,
                    first_shift, inner_weight, inner_bias, outer_weight,
                ],
                [block, ((TILE, 1), F32), block, wide, wide, block],
                cost=3.5,
            )
        )
    normed, inverse, first_low, hidden, slope, ffn_parts = zip(*forward)
    ffn_others = [swap(part) for part in ffn_parts]
    backward = []
    for chunk in range(chunks):
        backward.append(
            call(
                backward_kernel(chunk, units),
                [
                    normed[chunk], ffn_parts[chunk], ffn_others[chunk], out_grad, first_gain,
                    first_shift, outer_bias, second_gain, second_shift, slope[chunk],
                    inner_weight, outer_weight,
                ],
                [
                    block, block, wide, block, ((8, width), F32), ((8, hidden_width), F32),
                ],
                cost=3.0,
            )
        )
    layer_out, ffn_grad, pre_grad, first_parts, second_sums, inner_sums = zip(*backward)
    first_others = [swap(part) for part in first_parts]

    back_reach = [(i + reach, i) for i in range(ctx_size - reach)]
    attn_grad, first_sums, head_grad = [], [], []
    for chunk in range(chunks):
        grad, head_part, sums = call(
            middle_kernel(chunk),
            [
                ffn_grad[chunk], first_parts[chunk], first_others[chunk], normed[chunk],
                inverse[chunk], first_gain, output_weight, *highs, *logs, *head_grad[-1:],
            ],
            [block, (((chunk + 1) * GRAD_ROWS, local), BF16), ((8, width), F32)],
            scratch=[pltpu.VMEM((16, TILE), F32)],
            cost=1.5,
        )
        attn_grad.append(grad)
        first_sums.append(sums)
        head_grad.append(head_part)
        if chunk == 0:
            outer_half = ((hidden_width // 2, width), BF16)
            outer_pieces = call(
                weight_grad_kernel, [place, *hidden, *ffn_grad], [outer_half] * 2, scalars=1, cost=2.0
            )
            outer_sum = Sum(outer_pieces, stage_bits, bits)
    head_grad = head_grad[-1]
    grad_far = lax.ppermute(head_grad, "ctx", back_reach)
    grad_mate = flip(head_grad, "ctx", 1)
    outer_sum.step()
    inner_half = ((width // 2, hidden_width + local), BF16)
    inner_pieces = call(
        inner_weight_kernel, [place, *first_low, *pre_grad, *lows, *attn_grad],
        [inner_half] * 2, scalars=1, cost=2.0,
    )
    inner_sum = Sum(inner_pieces, stage_bits, bits)

    q_grads, k_grads, v_grads, key_parts = [], [], [], []
    double = pltpu.VMEM((2, rows, PAIR), BF16)
    single = pltpu.VMEM((rows, PAIR), F32)

    def query_side(pair):
        index, slot = places[pair]
        q_grad, k_part, v_part = call(
            query_side_kernel(pair, slot),
            [
                place, owns[index], head_grad, mates[index], fars[index], crosses[index],
                cosine, sine,
            ],
            [((rows, PAIR), BF16), table, table],
            scratch=[
                double, double, pltpu.VMEM((16, rows), F32), pltpu.VMEM((PAIR, rows), F32),
            ],
            scalars=1, cost=4.0,
        )
        q_grads.append(q_grad)
        key_parts.append((k_part, v_part))

    def key_side(pair):
        index, slot = places[pair]
        k_grad, v_grad = call(
            key_side_kernel(pair, slot),
            [
                place, owns[index], *key_parts[pair], cosine, sine, mates[index],
                fars[index], crosses[index], grad_mate, grad_far, grad_cross,
            ],
            [((rows, PAIR), BF16)] * 2,
            scratch=[double, double, single, single],
            scalars=1, cost=4.0,
        )
        k_grads.append(k_grad)
        v_grads.append(v_grad)

    query_side(0)
    inner_sum.step()
    query_side(1)
    query_side(2)
    outer_sum.step()
    grad_far, _ = lax.optimization_barrier((grad_far, q_grads[1]))
    grad_cross = flip(grad_far, "ctx", 1)
    key_side(0)
    key_side(1)
    outer_sum.step()
    key_side(2)
    inner_sum.step()
    all_grads = [*q_grads, *k_grads, *v_grads]
    attention_half = ((width // 2, 3 * local + PAIR), BF16)
    attention_sum = Sum(
        call(
            attention_weight_kernel,
            [place, tokens, *all_grads, *second_sums, *first_sums, *inner_sums],
            [attention_half] * 2,
            scratch=[pltpu.VMEM((width // 2, PAIR), F32)],
            scalars=1, cost=2.5,
        ),
        stage_bits, bits, True,
    )
    outer_sum.step()
    attention_sum.step()
    input_part = call(
        input_kernel, [*all_grads, *weights[:3]], [((rows, width), BF16)], cost=1.5
    )[0]
    input_other = swap(input_part)
    inner_sum.step()
    layer_out = call(
        stack_kernel, layer_out, [((rows, width), BF16)], cost=0.3, final=True
    )[0]

    attention_sum.step()
    outer_sum.step()
    inner_sum.step()
    attention_sum.step()
    outer_own, outer_rest = outer_sum.finish()
    inner_sum.step()
    attention_sum.step()
    input_grad = call(
        finish_input_kernel, [input_part, input_other, *attn_grad], [((rows, width), BF16)],
        cost=0.5, final=True,
    )[0]
    core = bits[ctx_stages[0]]
    outer_grad = join(core, outer_own, outer_rest, F32)
    attention_sum.step()
    inner_own, inner_rest = inner_sum.finish()
    inner_grad, o_weight_grad = call(
        finish_inner_kernel, [core.reshape(1), inner_own, inner_rest],
        [((width, hidden_width), F32), ((local, width), F32)], scalars=1, cost=2.0, final=True,
    )
    attention_own, attention_rest = attention_sum.finish()
    vector_sizes = [width] * 6 + [hidden_width] + [local] * 3
    (
        q_weight_grad, k_weight_grad, v_weight_grad,
        second_gain_grad, second_shift_grad, outer_bias_grad,
        first_gain_grad, first_shift_grad, output_bias_grad, inner_bias_grad,
        q_bias_grad, k_bias_grad, v_bias_grad,
    ) = call(
        finish_attention_kernel,
        [core.reshape(1), attention_own, attention_rest],
        [((width, local), F32)] * 3 + [((size,), F32) for size in vector_sizes],
        scalars=1, cost=2.0, final=True,
    )
    return (
        layer_out, input_grad,
        q_weight_grad, q_bias_grad, k_weight_grad, k_bias_grad, v_weight_grad, v_bias_grad,
        o_weight_grad, output_bias_grad, first_gain_grad, first_shift_grad,
        inner_grad, inner_bias_grad, outer_grad, outer_bias_grad,
        second_gain_grad, second_shift_grad,
    )


def solution(mesh):
    rows_spec, column_spec, row_spec = P(("dp", "ctx"), None), P(None, "tensor"), P("tensor", None)
    return jax.shard_map(
        per_device,
        mesh=mesh,
        in_specs=(
            rows_spec, rows_spec, P("dp", None),
            column_spec, P("tensor"), column_spec, P("tensor"), column_spec, P("tensor"),
            row_spec, P(), P(), P(), column_spec, P("tensor"), row_spec, P(), P(), P(),
        ),
        out_specs=(
            rows_spec, rows_spec,
            column_spec, P("tensor"), column_spec, P("tensor"), column_spec, P("tensor"),
            row_spec, P(), P(), P(), column_spec, P("tensor"), row_spec, P(), P(), P(),
        ),
        check_vma=False,
    )
```

```python
import jax
import jax.numpy as jnp
import numpy as np
from jax import lax
from jax.experimental import pallas as pl
from jax.experimental.pallas import tpu as pltpu
from jax.sharding import PartitionSpec as P

HEAD_DIM = 64
PAIR = 2 * HEAD_DIM
MASKED = -1e30
EPSILON = 1e-06
TILE = 256
GRAD_ROWS = TILE + 48
GROUPS = ((0,), (1,), (2,))
F32 = jnp.float32
BF16 = jnp.bfloat16
VMEM_BYTES = 12 * 1024 * 1024
FINAL = pltpu.HBM

NN = (((1,), (0,)), ((), ()))
NT = (((1,), (1,)), ((), ()))
TN = (((0,), (0,)), ((), ()))


def dot(left, right, dims=NN):
    return lax.dot_general(left, right, dims, preferred_element_type=F32)


class Order:
    last = None


def call(kernel, inputs, outputs, scratch=(), scalars=0, hbm=0, cost=1.0, ordered=True, final=False, after=()):
    spaces = [pltpu.SMEM] * scalars + [pltpu.VMEM] * (len(inputs) - scalars - hbm)
    spaces += [pltpu.HBM] * hbm
    inputs = list(inputs)
    for index in range(len(inputs) - hbm, len(inputs)):
        inputs[index] = pltpu.with_memory_space_constraint(inputs[index], pltpu.HBM)
    body = kernel
    extra = list(after)
    if ordered and Order.last is not None:
        extra.append(Order.last)
    if extra:
        count = len(inputs)
        inputs += extra
        spaces += [pl.ANY] * len(extra)

        def body(*refs):
            kernel(*refs[:count], *refs[count + len(extra) :])

    results = pl.pallas_call(
        body,
        in_specs=[pl.BlockSpec(memory_space=space) for space in spaces],
        out_specs=[pl.BlockSpec(memory_space=pltpu.VMEM)] * len(outputs),
        out_shape=[
            FINAL(dims, dtype) if final else jax.ShapeDtypeStruct(dims, dtype)
            for dims, dtype in outputs
        ],
        scratch_shapes=list(scratch),
        compiler_params=pltpu.CompilerParams(vmem_limit_bytes=VMEM_BYTES),
        cost_estimate=pl.CostEstimate(
            flops=int(cost * 1e10), bytes_accessed=int(cost * 1e13), transcendentals=0
        ),
    )(*inputs)
    if ordered:
        Order.last = min(results, key=lambda value: value.size * value.dtype.itemsize)
        if final:
            Order.last = pltpu.with_memory_space_constraint(Order.last, pltpu.HBM)
    return results


def tile(index):
    return pl.ds(index * TILE, TILE)


def sum_rows(value):
    return jnp.sum(value.astype(F32), axis=0, keepdims=True)


def mean(value):
    return jnp.mean(value, axis=-1, keepdims=True)


def normalize(rows_in):
    centered = rows_in - mean(rows_in)
    inverse = lax.rsqrt(mean(centered * centered) + EPSILON)
    return centered * inverse, inverse


def norm_back(grad, normed, inverse):
    return inverse * (grad - mean(grad) - normed * mean(grad * normed))


def swap_halves(value):
    lane = lax.broadcasted_iota(jnp.int32, value.shape, 1)
    ahead = pltpu.roll(value, PAIR - HEAD_DIM // 2, 1)
    behind = pltpu.roll(value, HEAD_DIM // 2, 1)
    return jnp.where(lane % HEAD_DIM < HEAD_DIM // 2, ahead, behind)


def window(ref, slot, parts):
    return ref.at[:, slot * parts * PAIR : (slot + 1) * parts * PAIR]


def head_mask(shape, head):
    lane = lax.broadcasted_iota(jnp.int32, shape, 1)
    return (lane // HEAD_DIM) == head


class Layout:
    def __init__(self, place, rows):
        self.me = place[0]
        self.rows = rows
        self.offset = self.me * rows
        self.end0 = place[3]
        self.end1 = self.end0 + place[4]

    def start(self, index):
        return jnp.where(
            index >= self.end1, self.end1, jnp.where(index >= self.end0, self.end0, 0)
        )

    def allowed(self, query_row, queries, key_row, keys):
        query = query_row + lax.broadcasted_iota(jnp.int32, (1, queries), 1)
        key = key_row + lax.broadcasted_iota(jnp.int32, (keys, 1), 0)
        return (key >= self.start(query)) & (key <= query)


def project_tables(place, table, cos_out, sin_out):
    rows = cos_out.shape[0]
    base_cos, base_sin, freq = table[:rows, :], table[rows : 2 * rows, :], table[2 * rows :, :]
    where = Layout(place, rows)
    row = where.offset + lax.broadcasted_iota(jnp.int32, (rows, 1), 0)
    turns = []
    for start in (0, where.end0, where.end1):
        angle = (where.offset - start).astype(F32) * freq
        turns.append((jnp.cos(angle)[0:1, :], jnp.sin(angle)[0:1, :]))
    late, later = row >= where.end0, row >= where.end1
    cos_turn = jnp.where(later, turns[2][0], jnp.where(late, turns[1][0], turns[0][0]))
    sin_turn = jnp.where(later, turns[2][1], jnp.where(late, turns[1][1], turns[0][1]))
    cosine = base_cos * cos_turn - base_sin * sin_turn
    sine = base_sin * cos_turn + base_cos * sin_turn
    lane = lax.broadcasted_iota(jnp.int32, (rows, PAIR), 1)
    cos_out[...] = cosine
    sin_out[...] = jnp.where(lane % HEAD_DIM < HEAD_DIM // 2, -sine, sine)


def project_group(group, place, tokens, wq, wk, wv, bq, bk, bv, cos, sin, own_out, far_out):
    cosine, sine = cos[...], sin[...]
    onward = place[0] < place[1] // 2
    for slot, pair in enumerate(group):
        span = slice(pair * PAIR, (pair + 1) * PAIR)
        weight = jnp.concatenate([wq[:, span], wk[:, span], wv[:, span]], axis=1)
        pre = dot(tokens[...], weight)
        query = pre[:, :PAIR] + bq[span].reshape(1, PAIR)
        key = pre[:, PAIR : 2 * PAIR] + bk[span].reshape(1, PAIR)
        query = (query * cosine + swap_halves(query) * sine).astype(BF16)
        key = (key * cosine + swap_halves(key) * sine).astype(BF16)
        value = (pre[:, 2 * PAIR :] + bv[span].reshape(1, PAIR)).astype(BF16)
        own, far = window(own_out, slot, 3), window(far_out, slot, 2)
        own[:, :PAIR] = query
        own[:, PAIR : 2 * PAIR] = key
        own[:, 2 * PAIR :] = value
        far[:, :PAIR] = jnp.where(onward, key, query)
        far[:, PAIR:] = jnp.where(onward, value, query)


def first_project_kernel(place, *refs):
    count = (len(refs) - 7) // 2
    sources, (own_out, far_out, cos_out, sin_out) = refs[:count + 1], refs[count + 1 : count + 5]
    copies, table, sems = refs[count + 5 : 2 * count + 5], refs[-2], refs[-1]
    moves = [
        pltpu.make_async_copy(source, target, sems.at[index])
        for index, (source, target) in enumerate(zip(sources, (table, *copies)))
    ]
    for move in moves:
        move.start()
    moves[0].wait()
    project_tables(place, table, cos_out, sin_out)
    for move in moves[1:]:
        move.wait()
    project_group(GROUPS[0], place, *copies, cos_out, sin_out, own_out, far_out)


def load_kernel(*refs):
    count = len(refs) // 2
    moves = [
        pltpu.make_async_copy(refs[index], refs[count + index], refs[-1].at[index])
        for index in range(count)
    ]
    for move in moves:
        move.start()
    for move in moves:
        move.wait()


def output_kernel(
    low0, low1, low2, other0, other1, wo, wo_other, w_in, w_out,
    attn_out, w_in_out, w_out_out, sems,
):
    moves = [
        pltpu.make_async_copy(source, target, sems.at[index])
        for index, (source, target) in enumerate(((w_in, w_in_out), (w_out, w_out_out)))
    ]
    for move in moves:
        move.start()
    low = jnp.concatenate([low0[...], low1[...], low2[...]], axis=1)
    other = jnp.concatenate([other0[...], other1[...]], axis=1)
    attn_out[...] = dot(low, wo[...]) + dot(other, wo_other[: 2 * PAIR, :])
    for move in moves:
        move.wait()


def project_kernel(group):
    def kernel(*refs):
        project_group(group, *refs)

    return kernel


def attend_kernel(slot):
    def kernel(
        place, own, mate, far, cross,
        low_out, lse_out, high, q_masked, peak, total, accum,
    ):
        own, mate = window(own, slot, 3), window(mate, slot, 3)
        far, cross = window(far, slot, 2), window(cross, slot, 2)
        rows = own.shape[0]
        where = Layout(place, rows)
        turned_q = own[:, :PAIR].astype(F32).T * 0.125
        for head in range(2):
            other = slice(HEAD_DIM * (1 - head), HEAD_DIM * (2 - head))
            mine = slice(HEAD_DIM * head, HEAD_DIM * (head + 1))
            q_masked[head, mine, :] = turned_q[mine, :].astype(BF16)
            q_masked[head, other, :] = jnp.zeros((HEAD_DIM, rows), BF16)

        def visit(keys, values, key_row, query, width, first):
            turned = values.astype(F32).T.astype(BF16)
            lanes = pl.ds(query, width)
            mask = where.allowed(where.offset + query, width, key_row, keys.shape[0])
            for head in range(2):
                span = slice(HEAD_DIM * head, HEAD_DIM * (head + 1))
                scores = dot(keys, q_masked[head, :, lanes])
                scores = jnp.where(mask, scores, MASKED)
                top = jnp.max(scores, axis=0, keepdims=True)
                if not first:
                    old = peak[head : head + 1, lanes]
                    top = jnp.maximum(old, top)
                    decay = jnp.exp(old - top)
                prob = jnp.exp(scores - top)
                sums = jnp.sum(prob, axis=0, keepdims=True)
                product = dot(turned[span, :], prob.astype(BF16))
                if not first:
                    sums += total[head : head + 1, lanes] * decay
                    product += accum[span, lanes] * decay
                peak[head : head + 1, lanes] = top
                total[head : head + 1, lanes] = sums
                accum[span, lanes] = product

        half = rows // 2
        visit(
            own[:half, PAIR : 2 * PAIR], own[:half, 2 * PAIR :], where.offset, 0, rows, True
        )
        visit(
            own[half:, PAIR : 2 * PAIR], own[half:, 2 * PAIR :], where.offset + half, half, half,
            False,
        )
        first_start = where.start(where.offset)

        @pl.when(first_start < where.offset)
        def _():
            odd = (where.me & 1) == 1
            visit(
                jnp.where(odd, mate[:, PAIR : 2 * PAIR], cross[:, :PAIR]),
                jnp.where(odd, mate[:, 2 * PAIR :], cross[:, PAIR:]), where.offset - rows,
                0, rows, False,
            )

        @pl.when(first_start < where.offset - rows)
        def _():
            base = where.offset - 2 * rows
            visit(far[half:, :PAIR], far[half:, PAIR:], base + half, 0, rows, False)
            visit(far[:half, :PAIR], far[:half, PAIR:], base, 0, half, False)

        for head in range(2):
            sums = total[head : head + 1, :]
            lse_out[head : head + 1, :] = peak[head : head + 1, :] + jnp.log(sums)
            span = slice(HEAD_DIM * head, HEAD_DIM * (head + 1))
            high[span, :] = accum[span, :] / sums
        low_out[...] = high[...].T.astype(BF16)

    return kernel


def forward_kernel(chunk, units):
    def kernel(
        tokens, attn_part, other, wo_other, bias, gain, shift, w_in, b_in, w_out,
        normed_out, inverse_out, first_out, hidden_out, slope_out, part_out,
    ):
        width = tokens.shape[1]
        last = wo_other.shape[0] - PAIR
        attn = attn_part[tile(chunk), :] + dot(other[tile(chunk), :], wo_other[last:, :])
        attn += bias[...].reshape(1, width)
        normed, inverse = normalize(tokens[tile(chunk), :].astype(F32) + attn)
        normed_out[...] = normed.astype(BF16)
        inverse_out[...] = inverse
        first = normed * gain[...].reshape(1, width) + shift[...].reshape(1, width)
        first_low = first.astype(BF16)
        first_out[...] = first_low
        total = None
        unit = w_in.shape[1] // units
        for index in range(units):
            span = slice(index * unit, (index + 1) * unit)
            pre = dot(first_low, w_in[:, span]) + b_in[span].reshape(1, unit)
            cdf = 0.5 * (1.0 + lax.erf(pre * 0.7071067811865476))
            density = jnp.exp(-0.5 * pre * pre) * 0.3989422804014327
            hidden = (pre * cdf).astype(BF16)
            hidden_out[:, span] = hidden
            slope_out[:, span] = (cdf + pre * density).astype(BF16)
            product = dot(hidden, w_out[span, :])
            total = product if total is None else total + product
        part_out[...] = total.astype(BF16)

    return kernel


def backward_kernel(chunk, units):
    def kernel(
        normed_first, part, other, out_grad, first_gain, first_shift, bias, gain, shift,
        slope, w_in, w_out,
        layer_out, ffn_grad_out, pre_grad_out, part_out, sums_out, inner_out,
    ):
        width = part.shape[1]

        def row(ref):
            return ref[...].reshape(1, width)

        first = normed_first[...].astype(F32) * row(first_gain) + row(first_shift)
        ffn = part[...].astype(F32) + other[...].astype(F32) + row(bias)
        normed, inverse = normalize(first + ffn)
        layer_out[...] = (normed * row(gain) + row(shift)).astype(BF16)
        upstream = out_grad[tile(chunk), :].astype(F32)
        res_grad = norm_back(upstream * row(gain), normed, inverse)
        ffn_grad = res_grad.astype(BF16)
        ffn_grad_out[...] = ffn_grad
        sums_out[0:1, :] = sum_rows(upstream * normed)
        sums_out[1:2, :] = sum_rows(upstream)
        sums_out[2:3, :] = sum_rows(ffn_grad)
        total = None
        unit = w_in.shape[1] // units
        for index in range(units):
            span = slice(index * unit, (index + 1) * unit)
            hidden_grad = dot(ffn_grad, w_out[span, :], NT)
            pre_grad = (hidden_grad * slope[:, span].astype(F32)).astype(BF16)
            pre_grad_out[:, span] = pre_grad
            inner_out[0:1, span] = sum_rows(pre_grad)
            product = dot(pre_grad, w_in[:, span], NT)
            total = product if total is None else total + product
        part_out[...] = total.astype(BF16)

    return kernel


def split_three(value):
    high = value.astype(BF16)
    rest = value - high.astype(F32)
    middle = rest.astype(BF16)
    return high, middle, (rest - middle.astype(F32)).astype(BF16)


def middle_kernel(chunk):
    def kernel(
        ffn_grad, part, other, normed, inverse, gain, wo, high0, high1, high2, lse0, lse1, lse2,
        *rest,
    ):
        grad_out, head_out, sums_out, stats = rest[-4:]
        base = chunk * GRAD_ROWS
        if chunk:
            head_out[:base, :] = rest[0][...]
        width = part.shape[1]
        local = wo.shape[0]
        first_grad = (
            ffn_grad[...].astype(F32) + part[...].astype(F32) + other[...].astype(F32)
        )
        unit = normed[...].astype(F32)
        res_grad = norm_back(first_grad * gain[...].reshape(1, width), unit, inverse[...])
        attn_grad = res_grad.astype(BF16)
        grad_out[...] = attn_grad
        sums_out[0:1, :] = sum_rows(first_grad * unit)
        sums_out[1:2, :] = sum_rows(first_grad)
        sums_out[2:3, :] = sum_rows(attn_grad)
        head_grad = dot(attn_grad, wo[...], NT).astype(BF16)
        head_out[base : base + TILE, :] = head_grad
        high = jnp.concatenate([ref[:, tile(chunk)] for ref in (high0, high1, high2)], axis=0)
        turned = head_grad.astype(F32).T * high
        stats[...] = jnp.zeros_like(stats)
        for index, lse in enumerate((lse0, lse1, lse2)):
            stats[2 * index : 2 * index + 2, :] = lse[:, tile(chunk)]
        for head in range(local // HEAD_DIM):
            span = slice(HEAD_DIM * head, HEAD_DIM * (head + 1))
            stats[8 + head : 9 + head, :] = jnp.sum(turned[span, :], axis=0, keepdims=True)
        begin = base + TILE
        head_out[begin:, :] = jnp.zeros((GRAD_ROWS - TILE, local), BF16)
        for index, value in enumerate(split_three(stats[...])):
            head_out[begin + 16 * index : begin + 16 * (index + 1), :TILE] = value

    return kernel


def stat_rows(grad, chunk):
    begin = chunk * GRAD_ROWS + TILE
    pieces = [
        grad[begin + 16 * index : begin + 16 * (index + 1), :TILE].astype(F32)
        for index in range(3)
    ]
    return pieces[0] + (pieces[1] + pieces[2])


def pair_terms(keys, values, queries, grads, mask, log_row, dot_row):
    scores = jnp.where(mask, dot(keys, queries, NT), MASKED)
    prob = jnp.exp(scores - log_row)
    prob_grad = dot(values, grads, NT)
    return prob.astype(BF16), (prob * (prob_grad - dot_row)).astype(BF16)


def query_side_kernel(pair, slot):
    pair_span = slice(pair * PAIR, (pair + 1) * PAIR)

    def kernel(
        place, own, grad, mate, far, cross, cos, sin,
        q_grad_out, k_part_out, v_part_out,
        q_masked, grad_masked, stats, q_turned,
    ):
        own, mate = window(own, slot, 3), window(mate, slot, 3)
        far, cross = window(far, slot, 2), window(cross, slot, 2)
        rows = own.shape[0]
        where = Layout(place, rows)
        for index in range(rows // TILE):
            stats[:, tile(index)] = stat_rows(grad, index)
            some = grad[index * GRAD_ROWS : index * GRAD_ROWS + TILE, pair_span]
            for head in range(2):
                mask = head_mask((TILE, PAIR), head)
                q_masked[head, tile(index), :] = jnp.where(
                    mask, own[tile(index), :PAIR] * 0.125, 0
                ).astype(BF16)
                grad_masked[head, tile(index), :] = jnp.where(mask, some, 0).astype(BF16)

        def visit(keys, values, key_row, query, width, own_rows=None, fresh=False):
            turned = keys.astype(F32).T.astype(BF16)
            lanes = pl.ds(query, width)
            mask = where.allowed(where.offset + query, width, key_row, keys.shape[0])
            key_sum = value_sum = None
            for head in range(2):
                index = 2 * pair + head
                span = slice(HEAD_DIM * head, HEAD_DIM * (head + 1))
                prob, score_grad = pair_terms(
                    keys, values, q_masked[head, lanes, :], grad_masked[head, lanes, :],
                    mask, stats[index : index + 1, lanes], stats[8 + index : 9 + index, lanes],
                )
                product = dot(turned[span, :], score_grad)
                if fresh:
                    q_turned[span, lanes] = product
                else:
                    q_turned[span, lanes] += product
                if own_rows is not None:
                    key_part = dot(score_grad, q_masked[head, lanes, :])
                    value_part = dot(prob, grad_masked[head, lanes, :])
                    key_sum = key_part if key_sum is None else key_sum + key_part
                    value_sum = value_part if value_sum is None else value_sum + value_part
            if own_rows is not None:
                k_part_out[own_rows, :] = key_sum
                v_part_out[own_rows, :] = value_sum

        half = rows // 2
        low, high = slice(0, half), slice(half, rows)
        visit(
            own[low, PAIR : 2 * PAIR], own[low, 2 * PAIR :], where.offset, 0, rows, low, True
        )
        visit(
            own[high, PAIR : 2 * PAIR], own[high, 2 * PAIR :], where.offset + half, half, half,
            high,
        )
        first_start = where.start(where.offset)

        @pl.when(first_start < where.offset)
        def _():
            odd = (where.me & 1) == 1
            visit(
                jnp.where(odd, mate[:, PAIR : 2 * PAIR], cross[:, :PAIR]),
                jnp.where(odd, mate[:, 2 * PAIR :], cross[:, PAIR:]), where.offset - rows,
                0, rows,
            )

        @pl.when(first_start < where.offset - rows)
        def _():
            base = where.offset - 2 * rows
            visit(far[high, :PAIR], far[high, PAIR:], base + half, 0, rows)
            visit(far[low, :PAIR], far[low, PAIR:], base, 0, half)

        turned = q_turned[...].T * 0.125
        q_grad_out[...] = (turned * cos[...] - swap_halves(turned) * sin[...]).astype(BF16)

    return kernel


def key_side_kernel(pair, slot):
    pair_span = slice(pair * PAIR, (pair + 1) * PAIR)

    def kernel(
        place, own, k_part, v_part, cos, sin, mate, far, cross,
        grad_mate, grad_far, grad_cross,
        k_grad_out, v_grad_out,
        k_masked, v_masked, k_turned, v_sum,
    ):
        own, mate = window(own, slot, 3), window(mate, slot, 3)
        far, cross = window(far, slot, 2), window(cross, slot, 2)
        rows = own.shape[0]
        where = Layout(place, rows)
        span_rows = place[1] * rows
        end = where.offset + rows
        k_turned[...] = k_part[...]
        v_sum[...] = v_part[...]

        def some(ref, chunk):
            return ref[chunk * GRAD_ROWS : chunk * GRAD_ROWS + TILE, pair_span]

        near = (end < span_rows) & (where.start(end) < end)
        beyond = (end + rows < span_rows) & (where.start(end + rows) < end)

        @pl.when(near)
        def _():
            for head in range(2):
                mask = head_mask((rows, PAIR), head)
                k_masked[head] = jnp.where(mask, own[:, PAIR : 2 * PAIR] * 0.125, 0).astype(BF16)
                v_masked[head] = jnp.where(mask, own[:, 2 * PAIR :], 0).astype(BF16)

        def visit(queries, grads, stats, query_row):
            first_head = head_mask((rows, PAIR), 0)
            for index in range(rows // TILE):
                mask = where.allowed(query_row + index * TILE, TILE, where.offset, rows)
                part = queries[index * TILE : (index + 1) * TILE, :]
                key_parts, value_parts = [], []
                for head in range(2):
                    line = 2 * pair + head
                    prob, score_grad = pair_terms(
                        k_masked[head], v_masked[head], part, grads[index], mask,
                        stats[index][line : line + 1, :], stats[index][8 + line : 9 + line, :],
                    )
                    key_parts.append(dot(score_grad, part))
                    value_parts.append(dot(prob, grads[index]))
                k_turned[...] += jnp.where(first_head, *key_parts) * 0.125
                v_sum[...] += jnp.where(first_head, *value_parts)

        @pl.when(near)
        def _():
            even = (where.me & 1) == 0
            chunks = range(rows // TILE)
            visit(
                jnp.where(even, mate[:, :PAIR], cross[:, :PAIR]),
                [jnp.where(even, some(grad_mate, i), some(grad_cross, i)) for i in chunks],
                [
                    jnp.where(even, stat_rows(grad_mate, i), stat_rows(grad_cross, i))
                    for i in chunks
                ],
                end,
            )

        @pl.when(beyond)
        def _():
            chunks = range(rows // TILE)
            visit(
                far[:, :PAIR], [some(grad_far, i) for i in chunks],
                [stat_rows(grad_far, i) for i in chunks], end + rows,
            )

        turned = k_turned[...]
        k_grad_out[...] = (turned * cos[...] - swap_halves(turned) * sin[...]).astype(BF16)
        v_grad_out[...] = v_sum[...].astype(BF16)

    return kernel


def input_kernel(*refs):
    grads, weights, out = refs[:9], refs[9:12], refs[12]
    total = None
    for index, weight in enumerate(weights):
        value = jnp.concatenate([ref[...] for ref in grads[3 * index : 3 * index + 3]], axis=1)
        product = dot(value, weight[...], NT)
        total = product if total is None else total + product
    out[...] = total.astype(BF16)


def finish_input_kernel(part, other, grad0, grad1, out):
    for index, grad in enumerate((grad0, grad1)):
        rows = tile(index)
        out[rows, :] = (
            part[rows, :].astype(F32) + other[rows, :].astype(F32) + grad[...].astype(F32)
        ).astype(BF16)


def stack_kernel(*refs):
    for index, ref in enumerate(refs[:-1]):
        refs[-1][tile(index), :] = ref[...]


def finish_inner_kernel(bit_ref, own, rest, inner_out, o_out):
    upper = bit_ref[0]
    half, wide = own.shape[0], inner_out.shape[1]
    for begin, ref in ((upper, own), (1 - upper, rest)):
        span = pl.ds(pl.multiple_of(begin * half, half), half)
        inner_out[span, :] = ref[:, :wide].astype(F32)
        o_out[:, span] = ref[:, wide:].astype(F32)


def finish_attention_kernel(bit_ref, own, rest, q_out, k_out, v_out, *vector_outs):
    upper = bit_ref[0]
    half, local = own.shape[0], q_out.shape[1]
    for begin, ref in ((upper, own), (1 - upper, rest)):
        span = pl.ds(pl.multiple_of(begin * half, half), half)
        q_out[span, :] = ref[:, :local].astype(F32)
        k_out[span, :] = ref[:, local : 2 * local].astype(F32)
        v_out[span, :] = ref[:, 2 * local : 3 * local].astype(F32)

        @pl.when(begin == 0)
        def _():
            tail = ref[:128, 3 * local :].astype(F32)
            tail = tail + pltpu.roll(tail, HEAD_DIM, 1)
            lane = lax.broadcasted_iota(jnp.int32, (1, PAIR), 1)
            line = 0
            for out in vector_outs:
                for index in range(out.shape[0] // PAIR):
                    value = jnp.where(
                        lane < HEAD_DIM, tail[line : line + 1, :], tail[line + 1 : line + 2, :]
                    )
                    out[index * PAIR : (index + 1) * PAIR] = value[0, :]
                    line += 2


def halves_of(place, rows):
    half = rows // 2
    bit = place[2]
    return (
        pl.multiple_of((1 - bit) * half, half), pl.multiple_of(bit * half, half)
    )


def weight_grad_kernel(place, left0, left1, right0, right1, send_out, keep_out):
    half = left0.shape[1] // 2
    for begin, out in zip(halves_of(place, 2 * half), (send_out, keep_out)):
        span = pl.ds(begin, half)
        out[...] = (
            dot(left0[:, span], right0[...], TN) + dot(left1[:, span], right1[...], TN)
        ).astype(BF16)


def inner_weight_kernel(
    place, first0, first1, pre0, pre1, low0, low1, low2, attn0, attn1, send_out, keep_out
):
    half = first0.shape[1] // 2
    wide = pre0.shape[1]
    lows = jnp.concatenate([low0[...], low1[...], low2[...]], axis=1)
    for begin, out in zip(halves_of(place, 2 * half), (send_out, keep_out)):
        span = pl.ds(begin, half)
        out[:, :wide] = (
            dot(first0[:, span], pre0[...], TN) + dot(first1[:, span], pre1[...], TN)
        ).astype(BF16)
        out[:, wide:] = (
            dot(lows[:TILE], attn0[:, span], TN) + dot(lows[TILE:], attn1[:, span], TN)
        ).astype(BF16)


def attention_weight_kernel(*refs):
    place, tokens = refs[:2]
    grads = refs[2:11]
    second0, second1, first0, first1, inner0, inner1 = refs[11:17]
    send_out, keep_out, vectors = refs[17:]
    width = tokens.shape[1]
    half = width // 2
    vectors[...] = jnp.zeros_like(vectors)
    rows_of = []
    for left, right in ((second0, second1), (first0, first1)):
        for index in range(3):
            rows_of.append(left[index : index + 1, :] + right[index : index + 1, :])
    rows_of.append(inner0[0:1, :] + inner1[0:1, :])
    for grad in grads:
        rows_of.append(sum_rows(grad[...]))
    line = 0
    for value in rows_of:
        for index in range(value.shape[1] // PAIR):
            piece = value[:, index * PAIR : (index + 1) * PAIR]
            vectors[line : line + 1, :] = piece
            vectors[line + 1 : line + 2, :] = pltpu.roll(piece, HEAD_DIM, 1)
            line += 2
    tail = high_and_low(vectors[...], pltpu.roll)
    together = jnp.concatenate([ref[...] for ref in grads], axis=1)
    main = together.shape[1]
    for begin, out in zip(halves_of(place, width), (send_out, keep_out)):
        span = pl.ds(begin, half)
        out[:, :main] = dot(tokens[:, span], together, TN).astype(BF16)
        out[:, main:] = jnp.where(begin == 0, tail, 0).astype(BF16)


def high_and_low(value, roll):
    high = value.astype(BF16).astype(F32)
    return jnp.where(head_mask(value.shape, 0), high, roll(value - high, HEAD_DIM, 1))


def add_two(one, two, tail, roll):
    one, two = one.astype(F32), two.astype(F32)
    if not tail:
        return (one + two).astype(BF16)
    main = one.shape[1] - PAIR
    rest = one[:, main:] + two[:, main:]
    rest = high_and_low(rest + roll(rest, HEAD_DIM, 1), roll)
    return jnp.concatenate([(one[:, :main] + two[:, :main]).astype(BF16), rest.astype(BF16)], axis=1)


def fold(bit, keep, received, split, tail):
    rows, width = keep.shape
    half = rows // 2
    if not split:

        def add_kernel(one, two, out):
            out[...] = add_two(one[...], two[...], tail, pltpu.roll)

        return call(add_kernel, [keep, received], [((rows, width), BF16)], cost=2.0)[0]
    if half % 16:
        total = add_two(keep, received, tail, jnp.roll)
        return [
            lax.dynamic_slice_in_dim(total, start * half, half, 0) for start in (1 - bit, bit)
        ]

    def fold_kernel(bit_ref, one, two, send_out, keep_out):
        upper = bit_ref[0]
        for begin, out in ((1 - upper, send_out), (upper, keep_out)):
            span = pl.ds(pl.multiple_of(begin * half, half), half)
            out[...] = add_two(one[span, :], two[span, :], tail, pltpu.roll)

    return call(
        fold_kernel, [bit.reshape(1), keep, received], [((half, width), BF16)] * 2, scalars=1,
        cost=2.0,
    )


def join(bit, own, received, dtype=BF16):
    half, width = own.shape
    if half % 16:
        ordered = jnp.where(
            bit == 1,
            jnp.concatenate([received, own], axis=0),
            jnp.concatenate([own, received], axis=0),
        )
        return ordered.astype(dtype)

    def join_kernel(bit_ref, one, two, out):
        upper = bit_ref[0]
        out[pl.ds(pl.multiple_of(upper * half, half), half), :] = one[...].astype(dtype)
        out[pl.ds(pl.multiple_of((1 - upper) * half, half), half), :] = two[...].astype(dtype)

    return call(
        join_kernel, [bit.reshape(1), own, received], [((2 * half, width), dtype)], scalars=1,
        cost=2.0, final=dtype == F32,
    )[0]


def flip(value, axis, bit):
    size = lax.axis_size(axis)
    return lax.ppermute(value, axis, [(i, i ^ bit) for i in range(size)])


class Sum:
    def __init__(self, pieces, stages, bits, tail=False):
        send, self.value = pieces
        self.tail, self.stages, self.bits, self.index = tail, stages, bits, 0
        self.received = flip(send, *stages[0])

    def step(self):
        stages, index, count = self.stages, self.index, len(self.stages)
        if index == 2 * count - 2:
            return
        self.index += 1
        if index < count - 2:
            stage = stages[index + 1]
            send, self.value = fold(self.bits[stage], self.value, self.received, True, self.tail)
            self.received = flip(send, *stage)
            return
        if index < count:
            self.value = fold(None, self.value, self.received, False, self.tail)
        else:
            self.value = join(self.bits[stages[2 * count - 2 - index]], self.value, self.received)
        self.received = flip(self.value, *stages[count - 1 if index == count - 2 else 2 * count - 3 - index])

    def finish(self):
        while self.index < 2 * len(self.stages) - 2:
            self.step()
        return self.value, self.received


def per_device(
    tokens, out_grad, lengths, query_weight, query_bias, key_weight, key_bias, value_weight,
    value_bias, output_weight, output_bias, first_gain, first_shift, inner_weight, inner_bias,
    outer_weight, outer_bias, second_gain, second_shift,
):
    Order.last = None
    rows, width = tokens.shape
    local = query_weight.shape[1]
    pairs = local // PAIR
    hidden_width = inner_weight.shape[1]
    chunks = rows // TILE
    units = hidden_width // 512
    ctx_size, dp_size = lax.axis_size("ctx"), lax.axis_size("dp")
    me = lax.axis_index("ctx")
    spot = jnp.arange(8)
    place = jnp.pad(lengths[0], (3, 5 - lengths.shape[1])) + jnp.where(
        spot == 0, me, jnp.where(spot == 1, ctx_size, jnp.where(spot == 2, me & 1, 0))
    )
    stage_bits = [
        (axis, 1 << i)
        for axis, size in (("ctx", ctx_size), ("dp", dp_size))
        for i in range((size - 1).bit_length())
    ]
    bits = {
        (axis, bit): ((lax.axis_index(axis) & bit) != 0).astype(jnp.int32)
        for axis, bit in stage_bits
    }
    ctx_stages = [stage for stage in stage_bits if stage[0] == "ctx"]

    frequency = 10000.0 ** (-2.0 * np.arange(HEAD_DIM // 2) / HEAD_DIM)
    lanes = np.tile(frequency, PAIR // (HEAD_DIM // 2))
    angles = np.arange(rows)[:, None] * lanes[None, :]
    trig = jnp.asarray(
        np.concatenate([np.cos(angles), np.sin(angles), np.tile(lanes, (8, 1))]), F32
    )

    weights = [query_weight, key_weight, value_weight, query_bias, key_bias, value_bias]
    owns, fars, mates = [], [], []
    reach = ctx_size // 2
    around = [(i, (i + reach) % ctx_size) for i in range(ctx_size)]
    table = ((rows, PAIR), F32)
    def swap(value):
        return flip(value, "tensor", 1)

    weight_other = swap(output_weight)
    places = [(group, slot) for group, pair_list in enumerate(GROUPS) for slot in range(len(pair_list))]
    for index, group in enumerate(GROUPS):
        shapes = [
            ((rows, 3 * PAIR * len(group)), BF16), ((rows, 2 * PAIR * len(group)), BF16),
        ]
        if index == 0:
            sources = [tokens, *weights]
            own, sent, cosine, sine, *copied = call(
                first_project_kernel, [place, trig, *sources],
                shapes + [table, table] + [(value.shape, value.dtype) for value in sources],
                scratch=[
                    pltpu.VMEM(trig.shape, F32), pltpu.SemaphoreType.DMA((1 + len(sources),)),
                ],
                scalars=1, hbm=1 + len(sources), cost=3.0,
            )
            tokens, weights = copied[0], copied[1:]
        else:
            own, sent = call(
                project_kernel(group), [place, tokens, *weights, cosine, sine], shapes,
                scalars=1, cost=1.0,
            )
        owns.append(own)
        fars.append(lax.ppermute(sent, "ctx", around))

    lows, logs, highs, crosses, low_others = [], [], [], [], []

    def load(*values, after=()):
        return call(
            load_kernel, values, [(value.shape, value.dtype) for value in values],
            scratch=[pltpu.SemaphoreType.DMA((len(values),))], hbm=len(values), cost=2.0, after=after,
        )

    def exchange(index):
        if index:
            owns[index], fars[index], _ = lax.optimization_barrier(
                (owns[index], fars[index], lows[-1])
            )
        else:
            fars[0], _ = lax.optimization_barrier((fars[0], owns[-1]))
        mates.append(flip(owns[index], "ctx", 1))
        crosses.append(flip(fars[index], "ctx", 1))

    exchange(0)
    output_bias = load(output_bias)[0]
    for index, slot in places:
        low, lse, high = call(
            attend_kernel(slot),
            [place, owns[index], mates[index], fars[index], crosses[index]],
            [((rows, PAIR), BF16), ((2, rows), F32), ((PAIR, rows), F32)],
            scratch=[
                pltpu.VMEM((2, PAIR, rows), BF16), pltpu.VMEM((2, rows), F32),
                pltpu.VMEM((2, rows), F32), pltpu.VMEM((PAIR, rows), F32),
            ],
            scalars=1, cost=4.0, after=(weight_other,) if len(lows) == 1 else (),
        )
        lows.append(low)
        low_others.append(swap(low))
        logs.append(lse)
        highs.append(high)
        if len(lows) < len(GROUPS):
            exchange(len(lows))
    attn_part, inner_weight, outer_weight = call(
        output_kernel,
        [
            *lows, *low_others[: pairs - 1], output_weight, weight_other, inner_weight,
            outer_weight,
        ],
        [((rows, width), F32)]
        + [(value.shape, value.dtype) for value in (inner_weight, outer_weight)],
        scratch=[pltpu.SemaphoreType.DMA((2,))], hbm=2, cost=2.0,
    )
    block = ((TILE, width), BF16)
    wide = ((TILE, hidden_width), BF16)
    forward = []
    for chunk in range(chunks):
        forward.append(
            call(
                forward_kernel(chunk, units),
                [
                    tokens, attn_part, low_others[-1], weight_other, output_bias, first_gain,
                    first_shift, inner_weight, inner_bias, outer_weight,
                ],
                [block, ((TILE, 1), F32), block, wide, wide, block],
                cost=3.5,
            )
        )
    normed, inverse, first_low, hidden, slope, ffn_parts = zip(*forward)
    ffn_others = [swap(part) for part in ffn_parts]
    backward = []
    for chunk in range(chunks):
        backward.append(
            call(
                backward_kernel(chunk, units),
                [
                    normed[chunk], ffn_parts[chunk], ffn_others[chunk], out_grad, first_gain,
                    first_shift, outer_bias, second_gain, second_shift, slope[chunk],
                    inner_weight, outer_weight,
                ],
                [
                    block, block, wide, block, ((8, width), F32), ((8, hidden_width), F32),
                ],
                cost=3.0,
            )
        )
    layer_out, ffn_grad, pre_grad, first_parts, second_sums, inner_sums = zip(*backward)
    first_others = [swap(part) for part in first_parts]

    back_reach = [(i + reach, i) for i in range(ctx_size - reach)]
    attn_grad, first_sums, head_grad = [], [], []
    for chunk in range(chunks):
        grad, head_part, sums = call(
            middle_kernel(chunk),
            [
                ffn_grad[chunk], first_parts[chunk], first_others[chunk], normed[chunk],
                inverse[chunk], first_gain, output_weight, *highs, *logs, *head_grad[-1:],
            ],
            [block, (((chunk + 1) * GRAD_ROWS, local), BF16), ((8, width), F32)],
            scratch=[pltpu.VMEM((16, TILE), F32)],
            cost=1.5,
        )
        attn_grad.append(grad)
        first_sums.append(sums)
        head_grad.append(head_part)
        if chunk == 0:
            outer_half = ((hidden_width // 2, width), BF16)
            outer_pieces = call(
                weight_grad_kernel, [place, *hidden, *ffn_grad], [outer_half] * 2, scalars=1, cost=2.0
            )
            outer_sum = Sum(outer_pieces, stage_bits, bits)
    head_grad = head_grad[-1]
    grad_far = lax.ppermute(head_grad, "ctx", back_reach)
    grad_mate = flip(head_grad, "ctx", 1)
    outer_sum.step()
    inner_half = ((width // 2, hidden_width + local), BF16)
    inner_pieces = call(
        inner_weight_kernel, [place, *first_low, *pre_grad, *lows, *attn_grad],
        [inner_half] * 2, scalars=1, cost=2.0,
    )
    inner_sum = Sum(inner_pieces, stage_bits, bits)

    q_grads, k_grads, v_grads, key_parts = [], [], [], []
    double = pltpu.VMEM((2, rows, PAIR), BF16)
    single = pltpu.VMEM((rows, PAIR), F32)

    def query_side(pair):
        index, slot = places[pair]
        q_grad, k_part, v_part = call(
            query_side_kernel(pair, slot),
            [
                place, owns[index], head_grad, mates[index], fars[index], crosses[index],
                cosine, sine,
            ],
            [((rows, PAIR), BF16), table, table],
            scratch=[
                double, double, pltpu.VMEM((16, rows), F32), pltpu.VMEM((PAIR, rows), F32),
            ],
            scalars=1, cost=4.0,
        )
        q_grads.append(q_grad)
        key_parts.append((k_part, v_part))

    def key_side(pair):
        index, slot = places[pair]
        k_grad, v_grad = call(
            key_side_kernel(pair, slot),
            [
                place, owns[index], *key_parts[pair], cosine, sine, mates[index],
                fars[index], crosses[index], grad_mate, grad_far, grad_cross,
            ],
            [((rows, PAIR), BF16)] * 2,
            scratch=[double, double, single, single],
            scalars=1, cost=4.0,
        )
        k_grads.append(k_grad)
        v_grads.append(v_grad)

    query_side(0)
    query_side(1)
    inner_sum.step()
    query_side(2)
    outer_sum.step()
    grad_far, _ = lax.optimization_barrier((grad_far, q_grads[1]))
    grad_cross = flip(grad_far, "ctx", 1)
    key_side(0)
    key_side(1)
    outer_sum.step()
    key_side(2)
    inner_sum.step()
    all_grads = [*q_grads, *k_grads, *v_grads]
    attention_half = ((width // 2, 3 * local + PAIR), BF16)
    attention_sum = Sum(
        call(
            attention_weight_kernel,
            [place, tokens, *all_grads, *second_sums, *first_sums, *inner_sums],
            [attention_half] * 2,
            scratch=[pltpu.VMEM((width // 2, PAIR), F32)],
            scalars=1, cost=2.5,
        ),
        stage_bits, bits, True,
    )
    outer_sum.step()
    attention_sum.step()
    input_part = call(
        input_kernel, [*all_grads, *weights[:3]], [((rows, width), BF16)], cost=1.5
    )[0]
    input_other = swap(input_part)
    inner_sum.step()
    layer_out = call(
        stack_kernel, layer_out, [((rows, width), BF16)], cost=0.3, final=True
    )[0]

    attention_sum.step()
    outer_sum.step()
    inner_sum.step()
    attention_sum.step()
    outer_own, outer_rest = outer_sum.finish()
    inner_sum.step()
    attention_sum.step()
    input_grad = call(
        finish_input_kernel, [input_part, input_other, *attn_grad], [((rows, width), BF16)],
        cost=0.5, final=True,
    )[0]
    core = bits[ctx_stages[0]]
    outer_grad = join(core, outer_own, outer_rest, F32)
    attention_sum.step()
    inner_own, inner_rest = inner_sum.finish()
    inner_grad, o_weight_grad = call(
        finish_inner_kernel, [core.reshape(1), inner_own, inner_rest],
        [((width, hidden_width), F32), ((local, width), F32)], scalars=1, cost=2.0, final=True,
    )
    attention_own, attention_rest = attention_sum.finish()
    vector_sizes = [width] * 6 + [hidden_width] + [local] * 3
    (
        q_weight_grad, k_weight_grad, v_weight_grad,
        second_gain_grad, second_shift_grad, outer_bias_grad,
        first_gain_grad, first_shift_grad, output_bias_grad, inner_bias_grad,
        q_bias_grad, k_bias_grad, v_bias_grad,
    ) = call(
        finish_attention_kernel,
        [core.reshape(1), attention_own, attention_rest],
        [((width, local), F32)] * 3 + [((size,), F32) for size in vector_sizes],
        scalars=1, cost=2.0, final=True,
    )
    return (
        layer_out, input_grad,
        q_weight_grad, q_bias_grad, k_weight_grad, k_bias_grad, v_weight_grad, v_bias_grad,
        o_weight_grad, output_bias_grad, first_gain_grad, first_shift_grad,
        inner_grad, inner_bias_grad, outer_grad, outer_bias_grad,
        second_gain_grad, second_shift_grad,
    )


def solution(mesh):
    rows_spec, column_spec, row_spec = P(("dp", "ctx"), None), P(None, "tensor"), P("tensor", None)
    return jax.shard_map(
        per_device,
        mesh=mesh,
        in_specs=(
            rows_spec, rows_spec, P("dp", None),
            column_spec, P("tensor"), column_spec, P("tensor"), column_spec, P("tensor"),
            row_spec, P(), P(), P(), column_spec, P("tensor"), row_spec, P(), P(), P(),
        ),
        out_specs=(
            rows_spec, rows_spec,
            column_spec, P("tensor"), column_spec, P("tensor"), column_spec, P("tensor"),
            row_spec, P(), P(), P(), column_spec, P("tensor"), row_spec, P(), P(), P(),
        ),
        check_vma=False,
    )
```

```python
import jax
import jax.numpy as jnp
import numpy as np
from jax import lax
from jax.experimental import pallas as pl
from jax.experimental.pallas import tpu as pltpu
from jax.sharding import PartitionSpec as P

HEAD_DIM = 64
PAIR = 2 * HEAD_DIM
MASKED = -1e30
EPSILON = 1e-06
TILE = 256
GRAD_ROWS = TILE + 48
GROUPS = ((0,), (1,), (2,))
F32 = jnp.float32
BF16 = jnp.bfloat16
VMEM_BYTES = 12 * 1024 * 1024
FINAL = pltpu.HBM

NN = (((1,), (0,)), ((), ()))
NT = (((1,), (1,)), ((), ()))
TN = (((0,), (0,)), ((), ()))


def dot(left, right, dims=NN):
    return lax.dot_general(left, right, dims, preferred_element_type=F32)


class Order:
    last = None


def call(kernel, inputs, outputs, scratch=(), scalars=0, hbm=0, cost=1.0, ordered=True, final=False, after=()):
    spaces = [pltpu.SMEM] * scalars + [pltpu.VMEM] * (len(inputs) - scalars - hbm)
    spaces += [pltpu.HBM] * hbm
    inputs = list(inputs)
    for index in range(len(inputs) - hbm, len(inputs)):
        inputs[index] = pltpu.with_memory_space_constraint(inputs[index], pltpu.HBM)
    body = kernel
    extra = list(after)
    if ordered and Order.last is not None:
        extra.append(Order.last)
    if extra:
        count = len(inputs)
        inputs += extra
        spaces += [pl.ANY] * len(extra)

        def body(*refs):
            kernel(*refs[:count], *refs[count + len(extra) :])

    results = pl.pallas_call(
        body,
        in_specs=[pl.BlockSpec(memory_space=space) for space in spaces],
        out_specs=[pl.BlockSpec(memory_space=pltpu.VMEM)] * len(outputs),
        out_shape=[
            FINAL(dims, dtype) if final else jax.ShapeDtypeStruct(dims, dtype)
            for dims, dtype in outputs
        ],
        scratch_shapes=list(scratch),
        compiler_params=pltpu.CompilerParams(vmem_limit_bytes=VMEM_BYTES),
        cost_estimate=pl.CostEstimate(
            flops=int(cost * 1e10), bytes_accessed=int(cost * 1e13), transcendentals=0
        ),
    )(*inputs)
    if ordered:
        Order.last = min(results, key=lambda value: value.size * value.dtype.itemsize)
        if final:
            Order.last = pltpu.with_memory_space_constraint(Order.last, pltpu.HBM)
    return results


def tile(index):
    return pl.ds(index * TILE, TILE)


def sum_rows(value):
    return jnp.sum(value.astype(F32), axis=0, keepdims=True)


def mean(value):
    return jnp.mean(value, axis=-1, keepdims=True)


def normalize(rows_in):
    centered = rows_in - mean(rows_in)
    inverse = lax.rsqrt(mean(centered * centered) + EPSILON)
    return centered * inverse, inverse


def norm_back(grad, normed, inverse):
    return inverse * (grad - mean(grad) - normed * mean(grad * normed))


def swap_halves(value):
    lane = lax.broadcasted_iota(jnp.int32, value.shape, 1)
    ahead = pltpu.roll(value, PAIR - HEAD_DIM // 2, 1)
    behind = pltpu.roll(value, HEAD_DIM // 2, 1)
    return jnp.where(lane % HEAD_DIM < HEAD_DIM // 2, ahead, behind)


def window(ref, slot, parts):
    return ref.at[:, slot * parts * PAIR : (slot + 1) * parts * PAIR]


def head_mask(shape, head):
    lane = lax.broadcasted_iota(jnp.int32, shape, 1)
    return (lane // HEAD_DIM) == head


class Layout:
    def __init__(self, place, rows):
        self.me = place[0]
        self.rows = rows
        self.offset = self.me * rows
        self.end0 = place[3]
        self.end1 = self.end0 + place[4]

    def start(self, index):
        return jnp.where(
            index >= self.end1, self.end1, jnp.where(index >= self.end0, self.end0, 0)
        )

    def allowed(self, query_row, queries, key_row, keys):
        query = query_row + lax.broadcasted_iota(jnp.int32, (1, queries), 1)
        key = key_row + lax.broadcasted_iota(jnp.int32, (keys, 1), 0)
        return (key >= self.start(query)) & (key <= query)


def project_tables(place, table, cos_out, sin_out):
    rows = cos_out.shape[0]
    base_cos, base_sin, freq = table[:rows, :], table[rows : 2 * rows, :], table[2 * rows :, :]
    where = Layout(place, rows)
    row = where.offset + lax.broadcasted_iota(jnp.int32, (rows, 1), 0)
    turns = []
    for start in (0, where.end0, where.end1):
        angle = (where.offset - start).astype(F32) * freq
        turns.append((jnp.cos(angle)[0:1, :], jnp.sin(angle)[0:1, :]))
    late, later = row >= where.end0, row >= where.end1
    cos_turn = jnp.where(later, turns[2][0], jnp.where(late, turns[1][0], turns[0][0]))
    sin_turn = jnp.where(later, turns[2][1], jnp.where(late, turns[1][1], turns[0][1]))
    cosine = base_cos * cos_turn - base_sin * sin_turn
    sine = base_sin * cos_turn + base_cos * sin_turn
    lane = lax.broadcasted_iota(jnp.int32, (rows, PAIR), 1)
    cos_out[...] = cosine
    sin_out[...] = jnp.where(lane % HEAD_DIM < HEAD_DIM // 2, -sine, sine)


def project_group(group, place, tokens, wq, wk, wv, bq, bk, bv, cos, sin, own_out, far_out):
    cosine, sine = cos[...], sin[...]
    onward = place[0] < place[1] // 2
    for slot, pair in enumerate(group):
        span = slice(pair * PAIR, (pair + 1) * PAIR)
        weight = jnp.concatenate([wq[:, span], wk[:, span], wv[:, span]], axis=1)
        pre = dot(tokens[...], weight)
        query = pre[:, :PAIR] + bq[span].reshape(1, PAIR)
        key = pre[:, PAIR : 2 * PAIR] + bk[span].reshape(1, PAIR)
        query = (query * cosine + swap_halves(query) * sine).astype(BF16)
        key = (key * cosine + swap_halves(key) * sine).astype(BF16)
        value = (pre[:, 2 * PAIR :] + bv[span].reshape(1, PAIR)).astype(BF16)
        own, far = window(own_out, slot, 3), window(far_out, slot, 2)
        own[:, :PAIR] = query
        own[:, PAIR : 2 * PAIR] = key
        own[:, 2 * PAIR :] = value
        far[:, :PAIR] = jnp.where(onward, key, query)
        far[:, PAIR:] = jnp.where(onward, value, query)


def first_project_kernel(place, *refs):
    count = (len(refs) - 7) // 2
    sources, (own_out, far_out, cos_out, sin_out) = refs[:count + 1], refs[count + 1 : count + 5]
    copies, table, sems = refs[count + 5 : 2 * count + 5], refs[-2], refs[-1]
    moves = [
        pltpu.make_async_copy(source, target, sems.at[index])
        for index, (source, target) in enumerate(zip(sources, (table, *copies)))
    ]
    for move in moves:
        move.start()
    moves[0].wait()
    project_tables(place, table, cos_out, sin_out)
    for move in moves[1:]:
        move.wait()
    project_group(GROUPS[0], place, *copies, cos_out, sin_out, own_out, far_out)


def load_kernel(*refs):
    count = len(refs) // 2
    moves = [
        pltpu.make_async_copy(refs[index], refs[count + index], refs[-1].at[index])
        for index in range(count)
    ]
    for move in moves:
        move.start()
    for move in moves:
        move.wait()


def output_kernel(
    low0, low1, low2, other0, other1, wo, wo_other, w_in, w_out,
    attn_out, w_in_out, w_out_out, sems,
):
    moves = [
        pltpu.make_async_copy(source, target, sems.at[index])
        for index, (source, target) in enumerate(((w_in, w_in_out), (w_out, w_out_out)))
    ]
    for move in moves:
        move.start()
    low = jnp.concatenate([low0[...], low1[...], low2[...]], axis=1)
    other = jnp.concatenate([other0[...], other1[...]], axis=1)
    attn_out[...] = dot(low, wo[...]) + dot(other, wo_other[: 2 * PAIR, :])
    for move in moves:
        move.wait()


def project_kernel(group):
    def kernel(*refs):
        project_group(group, *refs)

    return kernel


def attend_kernel(slot):
    def kernel(
        place, own, mate, far, cross,
        low_out, lse_out, high, q_masked, peak, total, accum,
    ):
        own, mate = window(own, slot, 3), window(mate, slot, 3)
        far, cross = window(far, slot, 2), window(cross, slot, 2)
        rows = own.shape[0]
        where = Layout(place, rows)
        turned_q = own[:, :PAIR].astype(F32).T * 0.125
        for head in range(2):
            other = slice(HEAD_DIM * (1 - head), HEAD_DIM * (2 - head))
            mine = slice(HEAD_DIM * head, HEAD_DIM * (head + 1))
            q_masked[head, mine, :] = turned_q[mine, :].astype(BF16)
            q_masked[head, other, :] = jnp.zeros((HEAD_DIM, rows), BF16)

        def visit(keys, values, key_row, query, width, first):
            turned = values.astype(F32).T.astype(BF16)
            lanes = pl.ds(query, width)
            mask = where.allowed(where.offset + query, width, key_row, keys.shape[0])
            for head in range(2):
                span = slice(HEAD_DIM * head, HEAD_DIM * (head + 1))
                scores = dot(keys, q_masked[head, :, lanes])
                scores = jnp.where(mask, scores, MASKED)
                top = jnp.max(scores, axis=0, keepdims=True)
                if not first:
                    old = peak[head : head + 1, lanes]
                    top = jnp.maximum(old, top)
                    decay = jnp.exp(old - top)
                prob = jnp.exp(scores - top)
                sums = jnp.sum(prob, axis=0, keepdims=True)
                product = dot(turned[span, :], prob.astype(BF16))
                if not first:
                    sums += total[head : head + 1, lanes] * decay
                    product += accum[span, lanes] * decay
                peak[head : head + 1, lanes] = top
                total[head : head + 1, lanes] = sums
                accum[span, lanes] = product

        half = rows // 2
        visit(
            own[:half, PAIR : 2 * PAIR], own[:half, 2 * PAIR :], where.offset, 0, rows, True
        )
        visit(
            own[half:, PAIR : 2 * PAIR], own[half:, 2 * PAIR :], where.offset + half, half, half,
            False,
        )
        first_start = where.start(where.offset)

        @pl.when(first_start < where.offset)
        def _():
            odd = (where.me & 1) == 1
            visit(
                jnp.where(odd, mate[:, PAIR : 2 * PAIR], cross[:, :PAIR]),
                jnp.where(odd, mate[:, 2 * PAIR :], cross[:, PAIR:]), where.offset - rows,
                0, rows, False,
            )

        @pl.when(first_start < where.offset - rows)
        def _():
            base = where.offset - 2 * rows
            visit(far[half:, :PAIR], far[half:, PAIR:], base + half, 0, rows, False)
            visit(far[:half, :PAIR], far[:half, PAIR:], base, 0, half, False)

        for head in range(2):
            sums = total[head : head + 1, :]
            lse_out[head : head + 1, :] = peak[head : head + 1, :] + jnp.log(sums)
            span = slice(HEAD_DIM * head, HEAD_DIM * (head + 1))
            high[span, :] = accum[span, :] / sums
        low_out[...] = high[...].T.astype(BF16)

    return kernel


def forward_kernel(chunk, units):
    def kernel(
        tokens, attn_part, other, wo_other, bias, gain, shift, w_in, b_in, w_out,
        normed_out, inverse_out, first_out, hidden_out, slope_out, part_out,
    ):
        width = tokens.shape[1]
        last = wo_other.shape[0] - PAIR
        attn = attn_part[tile(chunk), :] + dot(other[tile(chunk), :], wo_other[last:, :])
        attn += bias[...].reshape(1, width)
        normed, inverse = normalize(tokens[tile(chunk), :].astype(F32) + attn)
        normed_out[...] = normed.astype(BF16)
        inverse_out[...] = inverse
        first = normed * gain[...].reshape(1, width) + shift[...].reshape(1, width)
        first_low = first.astype(BF16)
        first_out[...] = first_low
        total = None
        unit = w_in.shape[1] // units
        for index in range(units):
            span = slice(index * unit, (index + 1) * unit)
            pre = dot(first_low, w_in[:, span]) + b_in[span].reshape(1, unit)
            cdf = 0.5 * (1.0 + lax.erf(pre * 0.7071067811865476))
            density = jnp.exp(-0.5 * pre * pre) * 0.3989422804014327
            hidden = (pre * cdf).astype(BF16)
            hidden_out[:, span] = hidden
            slope_out[:, span] = (cdf + pre * density).astype(BF16)
            product = dot(hidden, w_out[span, :])
            total = product if total is None else total + product
        part_out[...] = total.astype(BF16)

    return kernel


def backward_kernel(chunk, units):
    def kernel(
        normed_first, part, other, out_grad, first_gain, first_shift, bias, gain, shift,
        slope, w_in, w_out,
        layer_out, ffn_grad_out, pre_grad_out, part_out, sums_out, inner_out,
    ):
        width = part.shape[1]

        def row(ref):
            return ref[...].reshape(1, width)

        first = normed_first[...].astype(F32) * row(first_gain) + row(first_shift)
        ffn = part[...].astype(F32) + other[...].astype(F32) + row(bias)
        normed, inverse = normalize(first + ffn)
        layer_out[...] = (normed * row(gain) + row(shift)).astype(BF16)
        upstream = out_grad[tile(chunk), :].astype(F32)
        res_grad = norm_back(upstream * row(gain), normed, inverse)
        ffn_grad = res_grad.astype(BF16)
        ffn_grad_out[...] = ffn_grad
        sums_out[0:1, :] = sum_rows(upstream * normed)
        sums_out[1:2, :] = sum_rows(upstream)
        sums_out[2:3, :] = sum_rows(ffn_grad)
        total = None
        unit = w_in.shape[1] // units
        for index in range(units):
            span = slice(index * unit, (index + 1) * unit)
            hidden_grad = dot(ffn_grad, w_out[span, :], NT)
            pre_grad = (hidden_grad * slope[:, span].astype(F32)).astype(BF16)
            pre_grad_out[:, span] = pre_grad
            inner_out[0:1, span] = sum_rows(pre_grad)
            product = dot(pre_grad, w_in[:, span], NT)
            total = product if total is None else total + product
        part_out[...] = total.astype(BF16)

    return kernel


def split_three(value):
    high = value.astype(BF16)
    rest = value - high.astype(F32)
    middle = rest.astype(BF16)
    return high, middle, (rest - middle.astype(F32)).astype(BF16)


def middle_kernel(chunk):
    def kernel(
        ffn_grad, part, other, normed, inverse, gain, wo, high0, high1, high2, lse0, lse1, lse2,
        *rest,
    ):
        grad_out, head_out, sums_out, stats = rest[-4:]
        base = chunk * GRAD_ROWS
        if chunk:
            head_out[:base, :] = rest[0][...]
        width = part.shape[1]
        local = wo.shape[0]
        first_grad = (
            ffn_grad[...].astype(F32) + part[...].astype(F32) + other[...].astype(F32)
        )
        unit = normed[...].astype(F32)
        res_grad = norm_back(first_grad * gain[...].reshape(1, width), unit, inverse[...])
        attn_grad = res_grad.astype(BF16)
        grad_out[...] = attn_grad
        sums_out[0:1, :] = sum_rows(first_grad * unit)
        sums_out[1:2, :] = sum_rows(first_grad)
        sums_out[2:3, :] = sum_rows(attn_grad)
        head_grad = dot(attn_grad, wo[...], NT).astype(BF16)
        head_out[base : base + TILE, :] = head_grad
        high = jnp.concatenate([ref[:, tile(chunk)] for ref in (high0, high1, high2)], axis=0)
        turned = head_grad.astype(F32).T * high
        stats[...] = jnp.zeros_like(stats)
        for index, lse in enumerate((lse0, lse1, lse2)):
            stats[2 * index : 2 * index + 2, :] = lse[:, tile(chunk)]
        for head in range(local // HEAD_DIM):
            span = slice(HEAD_DIM * head, HEAD_DIM * (head + 1))
            stats[8 + head : 9 + head, :] = jnp.sum(turned[span, :], axis=0, keepdims=True)
        begin = base + TILE
        head_out[begin:, :] = jnp.zeros((GRAD_ROWS - TILE, local), BF16)
        for index, value in enumerate(split_three(stats[...])):
            head_out[begin + 16 * index : begin + 16 * (index + 1), :TILE] = value

    return kernel


def stat_rows(grad, chunk):
    begin = chunk * GRAD_ROWS + TILE
    pieces = [
        grad[begin + 16 * index : begin + 16 * (index + 1), :TILE].astype(F32)
        for index in range(3)
    ]
    return pieces[0] + (pieces[1] + pieces[2])


def pair_terms(keys, values, queries, grads, mask, log_row, dot_row):
    scores = jnp.where(mask, dot(keys, queries, NT), MASKED)
    prob = jnp.exp(scores - log_row)
    prob_grad = dot(values, grads, NT)
    return prob.astype(BF16), (prob * (prob_grad - dot_row)).astype(BF16)


def query_side_kernel(pair, slot):
    pair_span = slice(pair * PAIR, (pair + 1) * PAIR)

    def kernel(
        place, own, grad, mate, far, cross, cos, sin,
        q_grad_out, k_part_out, v_part_out,
        q_masked, grad_masked, stats, q_turned,
    ):
        own, mate = window(own, slot, 3), window(mate, slot, 3)
        far, cross = window(far, slot, 2), window(cross, slot, 2)
        rows = own.shape[0]
        where = Layout(place, rows)
        for index in range(rows // TILE):
            stats[:, tile(index)] = stat_rows(grad, index)
            some = grad[index * GRAD_ROWS : index * GRAD_ROWS + TILE, pair_span]
            for head in range(2):
                mask = head_mask((TILE, PAIR), head)
                q_masked[head, tile(index), :] = jnp.where(
                    mask, own[tile(index), :PAIR] * 0.125, 0
                ).astype(BF16)
                grad_masked[head, tile(index), :] = jnp.where(mask, some, 0).astype(BF16)

        def visit(keys, values, key_row, query, width, own_rows=None, fresh=False):
            turned = keys.astype(F32).T.astype(BF16)
            lanes = pl.ds(query, width)
            mask = where.allowed(where.offset + query, width, key_row, keys.shape[0])
            key_sum = value_sum = None
            for head in range(2):
                index = 2 * pair + head
                span = slice(HEAD_DIM * head, HEAD_DIM * (head + 1))
                prob, score_grad = pair_terms(
                    keys, values, q_masked[head, lanes, :], grad_masked[head, lanes, :],
                    mask, stats[index : index + 1, lanes], stats[8 + index : 9 + index, lanes],
                )
                product = dot(turned[span, :], score_grad)
                if fresh:
                    q_turned[span, lanes] = product
                else:
                    q_turned[span, lanes] += product
                if own_rows is not None:
                    key_part = dot(score_grad, q_masked[head, lanes, :])
                    value_part = dot(prob, grad_masked[head, lanes, :])
                    key_sum = key_part if key_sum is None else key_sum + key_part
                    value_sum = value_part if value_sum is None else value_sum + value_part
            if own_rows is not None:
                k_part_out[own_rows, :] = key_sum
                v_part_out[own_rows, :] = value_sum

        half = rows // 2
        low, high = slice(0, half), slice(half, rows)
        visit(
            own[low, PAIR : 2 * PAIR], own[low, 2 * PAIR :], where.offset, 0, rows, low, True
        )
        visit(
            own[high, PAIR : 2 * PAIR], own[high, 2 * PAIR :], where.offset + half, half, half,
            high,
        )
        first_start = where.start(where.offset)

        @pl.when(first_start < where.offset)
        def _():
            odd = (where.me & 1) == 1
            visit(
                jnp.where(odd, mate[:, PAIR : 2 * PAIR], cross[:, :PAIR]),
                jnp.where(odd, mate[:, 2 * PAIR :], cross[:, PAIR:]), where.offset - rows,
                0, rows,
            )

        @pl.when(first_start < where.offset - rows)
        def _():
            base = where.offset - 2 * rows
            visit(far[high, :PAIR], far[high, PAIR:], base + half, 0, rows)
            visit(far[low, :PAIR], far[low, PAIR:], base, 0, half)

        turned = q_turned[...].T * 0.125
        q_grad_out[...] = (turned * cos[...] - swap_halves(turned) * sin[...]).astype(BF16)

    return kernel


def key_side_kernel(pair, slot):
    pair_span = slice(pair * PAIR, (pair + 1) * PAIR)

    def kernel(
        place, own, k_part, v_part, cos, sin, mate, far, cross,
        grad_mate, grad_far, grad_cross,
        k_grad_out, v_grad_out,
        k_masked, v_masked, k_turned, v_sum,
    ):
        own, mate = window(own, slot, 3), window(mate, slot, 3)
        far, cross = window(far, slot, 2), window(cross, slot, 2)
        rows = own.shape[0]
        where = Layout(place, rows)
        span_rows = place[1] * rows
        end = where.offset + rows
        k_turned[...] = k_part[...]
        v_sum[...] = v_part[...]

        def some(ref, chunk):
            return ref[chunk * GRAD_ROWS : chunk * GRAD_ROWS + TILE, pair_span]

        near = (end < span_rows) & (where.start(end) < end)
        beyond = (end + rows < span_rows) & (where.start(end + rows) < end)

        @pl.when(near)
        def _():
            for head in range(2):
                mask = head_mask((rows, PAIR), head)
                k_masked[head] = jnp.where(mask, own[:, PAIR : 2 * PAIR] * 0.125, 0).astype(BF16)
                v_masked[head] = jnp.where(mask, own[:, 2 * PAIR :], 0).astype(BF16)

        def visit(queries, grads, stats, query_row):
            first_head = head_mask((rows, PAIR), 0)
            for index in range(rows // TILE):
                mask = where.allowed(query_row + index * TILE, TILE, where.offset, rows)
                part = queries[index * TILE : (index + 1) * TILE, :]
                key_parts, value_parts = [], []
                for head in range(2):
                    line = 2 * pair + head
                    prob, score_grad = pair_terms(
                        k_masked[head], v_masked[head], part, grads[index], mask,
                        stats[index][line : line + 1, :], stats[index][8 + line : 9 + line, :],
                    )
                    key_parts.append(dot(score_grad, part))
                    value_parts.append(dot(prob, grads[index]))
                k_turned[...] += jnp.where(first_head, *key_parts) * 0.125
                v_sum[...] += jnp.where(first_head, *value_parts)

        @pl.when(near)
        def _():
            even = (where.me & 1) == 0
            chunks = range(rows // TILE)
            visit(
                jnp.where(even, mate[:, :PAIR], cross[:, :PAIR]),
                [jnp.where(even, some(grad_mate, i), some(grad_cross, i)) for i in chunks],
                [
                    jnp.where(even, stat_rows(grad_mate, i), stat_rows(grad_cross, i))
                    for i in chunks
                ],
                end,
            )

        @pl.when(beyond)
        def _():
            chunks = range(rows // TILE)
            visit(
                far[:, :PAIR], [some(grad_far, i) for i in chunks],
                [stat_rows(grad_far, i) for i in chunks], end + rows,
            )

        turned = k_turned[...]
        k_grad_out[...] = (turned * cos[...] - swap_halves(turned) * sin[...]).astype(BF16)
        v_grad_out[...] = v_sum[...].astype(BF16)

    return kernel


def input_kernel(*refs):
    grads, weights, out = refs[:9], refs[9:12], refs[12]
    total = None
    for index, weight in enumerate(weights):
        value = jnp.concatenate([ref[...] for ref in grads[3 * index : 3 * index + 3]], axis=1)
        product = dot(value, weight[...], NT)
        total = product if total is None else total + product
    out[...] = total.astype(BF16)


def finish_input_kernel(part, other, grad0, grad1, out):
    for index, grad in enumerate((grad0, grad1)):
        rows = tile(index)
        out[rows, :] = (
            part[rows, :].astype(F32) + other[rows, :].astype(F32) + grad[...].astype(F32)
        ).astype(BF16)


def stack_kernel(*refs):
    for index, ref in enumerate(refs[:-1]):
        refs[-1][tile(index), :] = ref[...]


def finish_inner_kernel(bit_ref, own, rest, inner_out, o_out):
    upper = bit_ref[0]
    half, wide = own.shape[0], inner_out.shape[1]
    for begin, ref in ((upper, own), (1 - upper, rest)):
        span = pl.ds(pl.multiple_of(begin * half, half), half)
        inner_out[span, :] = ref[:, :wide].astype(F32)
        o_out[:, span] = ref[:, wide:].astype(F32)


def finish_attention_kernel(bit_ref, own, rest, q_out, k_out, v_out, *vector_outs):
    upper = bit_ref[0]
    half, local = own.shape[0], q_out.shape[1]
    for begin, ref in ((upper, own), (1 - upper, rest)):
        span = pl.ds(pl.multiple_of(begin * half, half), half)
        q_out[span, :] = ref[:, :local].astype(F32)
        k_out[span, :] = ref[:, local : 2 * local].astype(F32)
        v_out[span, :] = ref[:, 2 * local : 3 * local].astype(F32)

        @pl.when(begin == 0)
        def _():
            tail = ref[:128, 3 * local :].astype(F32)
            tail = tail + pltpu.roll(tail, HEAD_DIM, 1)
            lane = lax.broadcasted_iota(jnp.int32, (1, PAIR), 1)
            line = 0
            for out in vector_outs:
                for index in range(out.shape[0] // PAIR):
                    value = jnp.where(
                        lane < HEAD_DIM, tail[line : line + 1, :], tail[line + 1 : line + 2, :]
                    )
                    out[index * PAIR : (index + 1) * PAIR] = value[0, :]
                    line += 2


def halves_of(place, rows):
    half = rows // 2
    bit = place[2]
    return (
        pl.multiple_of((1 - bit) * half, half), pl.multiple_of(bit * half, half)
    )


def weight_grad_kernel(place, left0, left1, right0, right1, send_out, keep_out):
    half = left0.shape[1] // 2
    for begin, out in zip(halves_of(place, 2 * half), (send_out, keep_out)):
        span = pl.ds(begin, half)
        out[...] = (
            dot(left0[:, span], right0[...], TN) + dot(left1[:, span], right1[...], TN)
        ).astype(BF16)


def inner_weight_kernel(
    place, first0, first1, pre0, pre1, low0, low1, low2, attn0, attn1, send_out, keep_out
):
    half = first0.shape[1] // 2
    wide = pre0.shape[1]
    lows = jnp.concatenate([low0[...], low1[...], low2[...]], axis=1)
    for begin, out in zip(halves_of(place, 2 * half), (send_out, keep_out)):
        span = pl.ds(begin, half)
        out[:, :wide] = (
            dot(first0[:, span], pre0[...], TN) + dot(first1[:, span], pre1[...], TN)
        ).astype(BF16)
        out[:, wide:] = (
            dot(lows[:TILE], attn0[:, span], TN) + dot(lows[TILE:], attn1[:, span], TN)
        ).astype(BF16)


def attention_weight_kernel(*refs):
    place, tokens = refs[:2]
    grads = refs[2:11]
    second0, second1, first0, first1, inner0, inner1 = refs[11:17]
    send_out, keep_out, vectors = refs[17:]
    width = tokens.shape[1]
    half = width // 2
    vectors[...] = jnp.zeros_like(vectors)
    rows_of = []
    for left, right in ((second0, second1), (first0, first1)):
        for index in range(3):
            rows_of.append(left[index : index + 1, :] + right[index : index + 1, :])
    rows_of.append(inner0[0:1, :] + inner1[0:1, :])
    for grad in grads:
        rows_of.append(sum_rows(grad[...]))
    line = 0
    for value in rows_of:
        for index in range(value.shape[1] // PAIR):
            piece = value[:, index * PAIR : (index + 1) * PAIR]
            vectors[line : line + 1, :] = piece
            vectors[line + 1 : line + 2, :] = pltpu.roll(piece, HEAD_DIM, 1)
            line += 2
    tail = high_and_low(vectors[...], pltpu.roll)
    together = jnp.concatenate([ref[...] for ref in grads], axis=1)
    main = together.shape[1]
    for begin, out in zip(halves_of(place, width), (send_out, keep_out)):
        span = pl.ds(begin, half)
        out[:, :main] = dot(tokens[:, span], together, TN).astype(BF16)
        out[:, main:] = jnp.where(begin == 0, tail, 0).astype(BF16)


def high_and_low(value, roll):
    high = value.astype(BF16).astype(F32)
    return jnp.where(head_mask(value.shape, 0), high, roll(value - high, HEAD_DIM, 1))


def add_two(one, two, tail, roll):
    one, two = one.astype(F32), two.astype(F32)
    if not tail:
        return (one + two).astype(BF16)
    main = one.shape[1] - PAIR
    rest = one[:, main:] + two[:, main:]
    rest = high_and_low(rest + roll(rest, HEAD_DIM, 1), roll)
    return jnp.concatenate([(one[:, :main] + two[:, :main]).astype(BF16), rest.astype(BF16)], axis=1)


def fold(bit, keep, received, split, tail):
    rows, width = keep.shape
    half = rows // 2
    if not split:

        def add_kernel(one, two, out):
            out[...] = add_two(one[...], two[...], tail, pltpu.roll)

        return call(add_kernel, [keep, received], [((rows, width), BF16)], cost=2.0)[0]
    if half % 16:
        total = add_two(keep, received, tail, jnp.roll)
        return [
            lax.dynamic_slice_in_dim(total, start * half, half, 0) for start in (1 - bit, bit)
        ]

    def fold_kernel(bit_ref, one, two, send_out, keep_out):
        upper = bit_ref[0]
        for begin, out in ((1 - upper, send_out), (upper, keep_out)):
            span = pl.ds(pl.multiple_of(begin * half, half), half)
            out[...] = add_two(one[span, :], two[span, :], tail, pltpu.roll)

    return call(
        fold_kernel, [bit.reshape(1), keep, received], [((half, width), BF16)] * 2, scalars=1,
        cost=2.0,
    )


def join(bit, own, received, dtype=BF16):
    half, width = own.shape
    if half % 16:
        ordered = jnp.where(
            bit == 1,
            jnp.concatenate([received, own], axis=0),
            jnp.concatenate([own, received], axis=0),
        )
        return ordered.astype(dtype)

    def join_kernel(bit_ref, one, two, out):
        upper = bit_ref[0]
        out[pl.ds(pl.multiple_of(upper * half, half), half), :] = one[...].astype(dtype)
        out[pl.ds(pl.multiple_of((1 - upper) * half, half), half), :] = two[...].astype(dtype)

    return call(
        join_kernel, [bit.reshape(1), own, received], [((2 * half, width), dtype)], scalars=1,
        cost=2.0, final=dtype == F32,
    )[0]


def flip(value, axis, bit):
    size = lax.axis_size(axis)
    return lax.ppermute(value, axis, [(i, i ^ bit) for i in range(size)])


class Sum:
    def __init__(self, pieces, stages, bits, tail=False):
        send, self.value = pieces
        self.tail, self.stages, self.bits, self.index = tail, stages, bits, 0
        self.received = flip(send, *stages[0])

    def step(self):
        stages, index, count = self.stages, self.index, len(self.stages)
        if index == 2 * count - 2:
            return
        self.index += 1
        if index < count - 2:
            stage = stages[index + 1]
            send, self.value = fold(self.bits[stage], self.value, self.received, True, self.tail)
            self.received = flip(send, *stage)
            return
        if index < count:
            self.value = fold(None, self.value, self.received, False, self.tail)
        else:
            self.value = join(self.bits[stages[2 * count - 2 - index]], self.value, self.received)
        self.received = flip(self.value, *stages[count - 1 if index == count - 2 else 2 * count - 3 - index])

    def finish(self):
        while self.index < 2 * len(self.stages) - 2:
            self.step()
        return self.value, self.received


def per_device(
    tokens, out_grad, lengths, query_weight, query_bias, key_weight, key_bias, value_weight,
    value_bias, output_weight, output_bias, first_gain, first_shift, inner_weight, inner_bias,
    outer_weight, outer_bias, second_gain, second_shift,
):
    Order.last = None
    rows, width = tokens.shape
    local = query_weight.shape[1]
    pairs = local // PAIR
    hidden_width = inner_weight.shape[1]
    chunks = rows // TILE
    units = hidden_width // 512
    ctx_size, dp_size = lax.axis_size("ctx"), lax.axis_size("dp")
    me = lax.axis_index("ctx")
    spot = jnp.arange(8)
    place = jnp.pad(lengths[0], (3, 5 - lengths.shape[1])) + jnp.where(
        spot == 0, me, jnp.where(spot == 1, ctx_size, jnp.where(spot == 2, me & 1, 0))
    )
    stage_bits = [
        (axis, 1 << i)
        for axis, size in (("ctx", ctx_size), ("dp", dp_size))
        for i in range((size - 1).bit_length())
    ]
    bits = {
        (axis, bit): ((lax.axis_index(axis) & bit) != 0).astype(jnp.int32)
        for axis, bit in stage_bits
    }
    ctx_stages = [stage for stage in stage_bits if stage[0] == "ctx"]

    frequency = 10000.0 ** (-2.0 * np.arange(HEAD_DIM // 2) / HEAD_DIM)
    lanes = np.tile(frequency, PAIR // (HEAD_DIM // 2))
    angles = np.arange(rows)[:, None] * lanes[None, :]
    trig = jnp.asarray(
        np.concatenate([np.cos(angles), np.sin(angles), np.tile(lanes, (8, 1))]), F32
    )

    weights = [query_weight, key_weight, value_weight, query_bias, key_bias, value_bias]
    owns, fars, mates = [], [], []
    reach = ctx_size // 2
    around = [(i, (i + reach) % ctx_size) for i in range(ctx_size)]
    table = ((rows, PAIR), F32)
    def swap(value):
        return flip(value, "tensor", 1)

    places = [(group, slot) for group, pair_list in enumerate(GROUPS) for slot in range(len(pair_list))]
    for index, group in enumerate(GROUPS):
        shapes = [
            ((rows, 3 * PAIR * len(group)), BF16), ((rows, 2 * PAIR * len(group)), BF16),
        ]
        if index == 0:
            sources = [tokens, *weights]
            own, sent, cosine, sine, *copied = call(
                first_project_kernel, [place, trig, *sources],
                shapes + [table, table] + [(value.shape, value.dtype) for value in sources],
                scratch=[
                    pltpu.VMEM(trig.shape, F32), pltpu.SemaphoreType.DMA((1 + len(sources),)),
                ],
                scalars=1, hbm=1 + len(sources), cost=3.0,
            )
            tokens, weights = copied[0], copied[1:]
        else:
            own, sent = call(
                project_kernel(group), [place, tokens, *weights, cosine, sine], shapes,
                scalars=1, cost=1.0,
            )
        owns.append(own)
        fars.append(lax.ppermute(sent, "ctx", around))

    weight_other = swap(lax.optimization_barrier((output_weight, owns[0]))[0])
    lows, logs, highs, crosses, low_others = [], [], [], [], []

    def load(*values, after=()):
        return call(
            load_kernel, values, [(value.shape, value.dtype) for value in values],
            scratch=[pltpu.SemaphoreType.DMA((len(values),))], hbm=len(values), cost=2.0, after=after,
        )

    def exchange(index):
        if index:
            owns[index], fars[index], _ = lax.optimization_barrier(
                (owns[index], fars[index], lows[-1])
            )
        else:
            fars[0], _ = lax.optimization_barrier((fars[0], owns[-1]))
        mates.append(flip(owns[index], "ctx", 1))
        crosses.append(flip(fars[index], "ctx", 1))

    exchange(0)
    output_bias = load(output_bias)[0]
    for index, slot in places:
        low, lse, high = call(
            attend_kernel(slot),
            [place, owns[index], mates[index], fars[index], crosses[index]],
            [((rows, PAIR), BF16), ((2, rows), F32), ((PAIR, rows), F32)],
            scratch=[
                pltpu.VMEM((2, PAIR, rows), BF16), pltpu.VMEM((2, rows), F32),
                pltpu.VMEM((2, rows), F32), pltpu.VMEM((PAIR, rows), F32),
            ],
            scalars=1, cost=4.0, after=(weight_other,) if len(lows) == 1 else (),
        )
        lows.append(low)
        low_others.append(swap(low))
        logs.append(lse)
        highs.append(high)
        if len(lows) < len(GROUPS):
            exchange(len(lows))
    attn_part, inner_weight, outer_weight = call(
        output_kernel,
        [
            *lows, *low_others[: pairs - 1], output_weight, weight_other, inner_weight,
            outer_weight,
        ],
        [((rows, width), F32)]
        + [(value.shape, value.dtype) for value in (inner_weight, outer_weight)],
        scratch=[pltpu.SemaphoreType.DMA((2,))], hbm=2, cost=2.0,
    )
    block = ((TILE, width), BF16)
    wide = ((TILE, hidden_width), BF16)
    forward = []
    for chunk in range(chunks):
        forward.append(
            call(
                forward_kernel(chunk, units),
                [
                    tokens, attn_part, low_others[-1], weight_other, output_bias, first_gain,
                    first_shift, inner_weight, inner_bias, outer_weight,
                ],
                [block, ((TILE, 1), F32), block, wide, wide, block],
                cost=3.5,
            )
        )
    normed, inverse, first_low, hidden, slope, ffn_parts = zip(*forward)
    ffn_others = [swap(part) for part in ffn_parts]
    backward = []
    for chunk in range(chunks):
        backward.append(
            call(
                backward_kernel(chunk, units),
                [
                    normed[chunk], ffn_parts[chunk], ffn_others[chunk], out_grad, first_gain,
                    first_shift, outer_bias, second_gain, second_shift, slope[chunk],
                    inner_weight, outer_weight,
                ],
                [
                    block, block, wide, block, ((8, width), F32), ((8, hidden_width), F32),
                ],
                cost=3.0,
            )
        )
    layer_out, ffn_grad, pre_grad, first_parts, second_sums, inner_sums = zip(*backward)
    first_others = [swap(part) for part in first_parts]

    back_reach = [(i + reach, i) for i in range(ctx_size - reach)]
    attn_grad, first_sums, head_grad = [], [], []
    for chunk in range(chunks):
        grad, head_part, sums = call(
            middle_kernel(chunk),
            [
                ffn_grad[chunk], first_parts[chunk], first_others[chunk], normed[chunk],
                inverse[chunk], first_gain, output_weight, *highs, *logs, *head_grad[-1:],
            ],
            [block, (((chunk + 1) * GRAD_ROWS, local), BF16), ((8, width), F32)],
            scratch=[pltpu.VMEM((16, TILE), F32)],
            cost=1.5,
        )
        attn_grad.append(grad)
        first_sums.append(sums)
        head_grad.append(head_part)
        if chunk == 0:
            outer_half = ((hidden_width // 2, width), BF16)
            outer_pieces = call(
                weight_grad_kernel, [place, *hidden, *ffn_grad], [outer_half] * 2, scalars=1, cost=2.0
            )
            outer_sum = Sum(outer_pieces, stage_bits, bits)
    head_grad = head_grad[-1]
    grad_far = lax.ppermute(head_grad, "ctx", back_reach)
    grad_mate = flip(head_grad, "ctx", 1)
    outer_sum.step()
    inner_half = ((width // 2, hidden_width + local), BF16)
    inner_pieces = call(
        inner_weight_kernel, [place, *first_low, *pre_grad, *lows, *attn_grad],
        [inner_half] * 2, scalars=1, cost=2.0,
    )
    inner_sum = Sum(inner_pieces, stage_bits, bits)

    q_grads, k_grads, v_grads, key_parts = [], [], [], []
    double = pltpu.VMEM((2, rows, PAIR), BF16)
    single = pltpu.VMEM((rows, PAIR), F32)

    def query_side(pair):
        index, slot = places[pair]
        q_grad, k_part, v_part = call(
            query_side_kernel(pair, slot),
            [
                place, owns[index], head_grad, mates[index], fars[index], crosses[index],
                cosine, sine,
            ],
            [((rows, PAIR), BF16), table, table],
            scratch=[
                double, double, pltpu.VMEM((16, rows), F32), pltpu.VMEM((PAIR, rows), F32),
            ],
            scalars=1, cost=4.0,
        )
        q_grads.append(q_grad)
        key_parts.append((k_part, v_part))

    def key_side(pair):
        index, slot = places[pair]
        k_grad, v_grad = call(
            key_side_kernel(pair, slot),
            [
                place, owns[index], *key_parts[pair], cosine, sine, mates[index],
                fars[index], crosses[index], grad_mate, grad_far, grad_cross,
            ],
            [((rows, PAIR), BF16)] * 2,
            scratch=[double, double, single, single],
            scalars=1, cost=4.0,
        )
        k_grads.append(k_grad)
        v_grads.append(v_grad)

    query_side(0)
    query_side(1)
    inner_sum.step()
    query_side(2)
    outer_sum.step()
    grad_far, _ = lax.optimization_barrier((grad_far, q_grads[1]))
    grad_cross = flip(grad_far, "ctx", 1)
    key_side(0)
    key_side(1)
    outer_sum.step()
    key_side(2)
    inner_sum.step()
    all_grads = [*q_grads, *k_grads, *v_grads]
    attention_half = ((width // 2, 3 * local + PAIR), BF16)
    attention_sum = Sum(
        call(
            attention_weight_kernel,
            [place, tokens, *all_grads, *second_sums, *first_sums, *inner_sums],
            [attention_half] * 2,
            scratch=[pltpu.VMEM((width // 2, PAIR), F32)],
            scalars=1, cost=2.5,
        ),
        stage_bits, bits, True,
    )
    outer_sum.step()
    attention_sum.step()
    input_part = call(
        input_kernel, [*all_grads, *weights[:3]], [((rows, width), BF16)], cost=1.5
    )[0]
    input_other = swap(input_part)
    inner_sum.step()
    layer_out = call(
        stack_kernel, layer_out, [((rows, width), BF16)], cost=0.3, final=True
    )[0]

    attention_sum.step()
    outer_sum.step()
    inner_sum.step()
    attention_sum.step()
    outer_own, outer_rest = outer_sum.finish()
    inner_sum.step()
    attention_sum.step()
    input_grad = call(
        finish_input_kernel, [input_part, input_other, *attn_grad], [((rows, width), BF16)],
        cost=0.5, final=True,
    )[0]
    core = bits[ctx_stages[0]]
    outer_grad = join(core, outer_own, outer_rest, F32)
    attention_sum.step()
    inner_own, inner_rest = inner_sum.finish()
    inner_grad, o_weight_grad = call(
        finish_inner_kernel, [core.reshape(1), inner_own, inner_rest],
        [((width, hidden_width), F32), ((local, width), F32)], scalars=1, cost=2.0, final=True,
    )
    attention_own, attention_rest = attention_sum.finish()
    vector_sizes = [width] * 6 + [hidden_width] + [local] * 3
    (
        q_weight_grad, k_weight_grad, v_weight_grad,
        second_gain_grad, second_shift_grad, outer_bias_grad,
        first_gain_grad, first_shift_grad, output_bias_grad, inner_bias_grad,
        q_bias_grad, k_bias_grad, v_bias_grad,
    ) = call(
        finish_attention_kernel,
        [core.reshape(1), attention_own, attention_rest],
        [((width, local), F32)] * 3 + [((size,), F32) for size in vector_sizes],
        scalars=1, cost=2.0, final=True,
    )
    return (
        layer_out, input_grad,
        q_weight_grad, q_bias_grad, k_weight_grad, k_bias_grad, v_weight_grad, v_bias_grad,
        o_weight_grad, output_bias_grad, first_gain_grad, first_shift_grad,
        inner_grad, inner_bias_grad, outer_grad, outer_bias_grad,
        second_gain_grad, second_shift_grad,
    )


def solution(mesh):
    rows_spec, column_spec, row_spec = P(("dp", "ctx"), None), P(None, "tensor"), P("tensor", None)
    return jax.shard_map(
        per_device,
        mesh=mesh,
        in_specs=(
            rows_spec, rows_spec, P("dp", None),
            column_spec, P("tensor"), column_spec, P("tensor"), column_spec, P("tensor"),
            row_spec, P(), P(), P(), column_spec, P("tensor"), row_spec, P(), P(), P(),
        ),
        out_specs=(
            rows_spec, rows_spec,
            column_spec, P("tensor"), column_spec, P("tensor"), column_spec, P("tensor"),
            row_spec, P(), P(), P(), column_spec, P("tensor"), row_spec, P(), P(), P(),
        ),
        check_vma=False,
    )
```

```python
import jax
import jax.numpy as jnp
import numpy as np
from jax import lax
from jax.experimental import pallas as pl
from jax.experimental.pallas import tpu as pltpu
from jax.sharding import PartitionSpec as P

HEAD_DIM = 64
PAIR = 2 * HEAD_DIM
MASKED = -1e30
EPSILON = 1e-06
TILE = 256
GRAD_ROWS = TILE + 48
GROUPS = ((0,), (1,), (2,))
F32 = jnp.float32
BF16 = jnp.bfloat16
VMEM_BYTES = 12 * 1024 * 1024
FINAL = pltpu.HBM

NN = (((1,), (0,)), ((), ()))
NT = (((1,), (1,)), ((), ()))
TN = (((0,), (0,)), ((), ()))


def dot(left, right, dims=NN):
    return lax.dot_general(left, right, dims, preferred_element_type=F32)


class Order:
    last = None


def call(kernel, inputs, outputs, scratch=(), scalars=0, hbm=0, cost=1.0, ordered=True, final=False, after=()):
    spaces = [pltpu.SMEM] * scalars + [pltpu.VMEM] * (len(inputs) - scalars - hbm)
    spaces += [pltpu.HBM] * hbm
    inputs = list(inputs)
    for index in range(len(inputs) - hbm, len(inputs)):
        inputs[index] = pltpu.with_memory_space_constraint(inputs[index], pltpu.HBM)
    body = kernel
    extra = list(after)
    if ordered and Order.last is not None:
        extra.append(Order.last)
    if extra:
        count = len(inputs)
        inputs += extra
        spaces += [pl.ANY] * len(extra)

        def body(*refs):
            kernel(*refs[:count], *refs[count + len(extra) :])

    results = pl.pallas_call(
        body,
        in_specs=[pl.BlockSpec(memory_space=space) for space in spaces],
        out_specs=[pl.BlockSpec(memory_space=pltpu.VMEM)] * len(outputs),
        out_shape=[
            FINAL(dims, dtype) if final else jax.ShapeDtypeStruct(dims, dtype)
            for dims, dtype in outputs
        ],
        scratch_shapes=list(scratch),
        compiler_params=pltpu.CompilerParams(vmem_limit_bytes=VMEM_BYTES),
        cost_estimate=pl.CostEstimate(
            flops=int(cost * 1e10), bytes_accessed=int(cost * 1e13), transcendentals=0
        ),
    )(*inputs)
    if ordered:
        Order.last = min(results, key=lambda value: value.size * value.dtype.itemsize)
        if final:
            Order.last = pltpu.with_memory_space_constraint(Order.last, pltpu.HBM)
    return results


def tile(index):
    return pl.ds(index * TILE, TILE)


def sum_rows(value):
    return jnp.sum(value.astype(F32), axis=0, keepdims=True)


def mean(value):
    return jnp.mean(value, axis=-1, keepdims=True)


def normalize(rows_in):
    centered = rows_in - mean(rows_in)
    inverse = lax.rsqrt(mean(centered * centered) + EPSILON)
    return centered * inverse, inverse


def norm_back(grad, normed, inverse):
    return inverse * (grad - mean(grad) - normed * mean(grad * normed))


def swap_halves(value):
    lane = lax.broadcasted_iota(jnp.int32, value.shape, 1)
    ahead = pltpu.roll(value, PAIR - HEAD_DIM // 2, 1)
    behind = pltpu.roll(value, HEAD_DIM // 2, 1)
    return jnp.where(lane % HEAD_DIM < HEAD_DIM // 2, ahead, behind)


def window(ref, slot, parts):
    return ref.at[:, slot * parts * PAIR : (slot + 1) * parts * PAIR]


def head_mask(shape, head):
    lane = lax.broadcasted_iota(jnp.int32, shape, 1)
    return (lane // HEAD_DIM) == head


class Layout:
    def __init__(self, place, rows):
        self.me = place[0]
        self.rows = rows
        self.offset = self.me * rows
        self.end0 = place[3]
        self.end1 = self.end0 + place[4]

    def start(self, index):
        return jnp.where(
            index >= self.end1, self.end1, jnp.where(index >= self.end0, self.end0, 0)
        )

    def allowed(self, query_row, queries, key_row, keys):
        query = query_row + lax.broadcasted_iota(jnp.int32, (1, queries), 1)
        key = key_row + lax.broadcasted_iota(jnp.int32, (keys, 1), 0)
        return (key >= self.start(query)) & (key <= query)


def project_tables(place, table, cos_out, sin_out):
    rows = cos_out.shape[0]
    base_cos, base_sin, freq = table[:rows, :], table[rows : 2 * rows, :], table[2 * rows :, :]
    where = Layout(place, rows)
    row = where.offset + lax.broadcasted_iota(jnp.int32, (rows, 1), 0)
    turns = []
    for start in (0, where.end0, where.end1):
        angle = (where.offset - start).astype(F32) * freq
        turns.append((jnp.cos(angle)[0:1, :], jnp.sin(angle)[0:1, :]))
    late, later = row >= where.end0, row >= where.end1
    cos_turn = jnp.where(later, turns[2][0], jnp.where(late, turns[1][0], turns[0][0]))
    sin_turn = jnp.where(later, turns[2][1], jnp.where(late, turns[1][1], turns[0][1]))
    cosine = base_cos * cos_turn - base_sin * sin_turn
    sine = base_sin * cos_turn + base_cos * sin_turn
    lane = lax.broadcasted_iota(jnp.int32, (rows, PAIR), 1)
    cos_out[...] = cosine
    sin_out[...] = jnp.where(lane % HEAD_DIM < HEAD_DIM // 2, -sine, sine)


def project_group(group, place, tokens, wq, wk, wv, bq, bk, bv, cos, sin, own_out, far_out):
    cosine, sine = cos[...], sin[...]
    onward = place[0] < place[1] // 2
    for slot, pair in enumerate(group):
        span = slice(pair * PAIR, (pair + 1) * PAIR)
        weight = jnp.concatenate([wq[:, span], wk[:, span], wv[:, span]], axis=1)
        pre = dot(tokens[...], weight)
        query = pre[:, :PAIR] + bq[span].reshape(1, PAIR)
        key = pre[:, PAIR : 2 * PAIR] + bk[span].reshape(1, PAIR)
        query = (query * cosine + swap_halves(query) * sine).astype(BF16)
        key = (key * cosine + swap_halves(key) * sine).astype(BF16)
        value = (pre[:, 2 * PAIR :] + bv[span].reshape(1, PAIR)).astype(BF16)
        own, far = window(own_out, slot, 3), window(far_out, slot, 2)
        own[:, :PAIR] = query
        own[:, PAIR : 2 * PAIR] = key
        own[:, 2 * PAIR :] = value
        far[:, :PAIR] = jnp.where(onward, key, query)
        far[:, PAIR:] = jnp.where(onward, value, query)


def first_project_kernel(place, *refs):
    count = (len(refs) - 7) // 2
    sources, (own_out, far_out, cos_out, sin_out) = refs[:count + 1], refs[count + 1 : count + 5]
    copies, table, sems = refs[count + 5 : 2 * count + 5], refs[-2], refs[-1]
    moves = [
        pltpu.make_async_copy(source, target, sems.at[index])
        for index, (source, target) in enumerate(zip(sources, (table, *copies)))
    ]
    for move in moves:
        move.start()
    moves[0].wait()
    project_tables(place, table, cos_out, sin_out)
    for move in moves[1:]:
        move.wait()
    project_group(GROUPS[0], place, *copies, cos_out, sin_out, own_out, far_out)


def load_kernel(*refs):
    count = len(refs) // 2
    moves = [
        pltpu.make_async_copy(refs[index], refs[count + index], refs[-1].at[index])
        for index in range(count)
    ]
    for move in moves:
        move.start()
    for move in moves:
        move.wait()


def output_kernel(
    low0, low1, low2, other0, other1, wo, wo_other, w_in, w_out,
    attn_out, w_in_out, w_out_out, sems,
):
    moves = [
        pltpu.make_async_copy(source, target, sems.at[index])
        for index, (source, target) in enumerate(((w_in, w_in_out), (w_out, w_out_out)))
    ]
    for move in moves:
        move.start()
    low = jnp.concatenate([low0[...], low1[...], low2[...]], axis=1)
    other = jnp.concatenate([other0[...], other1[...]], axis=1)
    attn_out[...] = dot(low, wo[...]) + dot(other, wo_other[: 2 * PAIR, :])
    for move in moves:
        move.wait()


def project_kernel(group):
    def kernel(*refs):
        project_group(group, *refs)

    return kernel


def attend_kernel(slot):
    def kernel(
        place, own, mate, far, cross,
        low_out, lse_out, high, q_masked, peak, total, accum,
    ):
        own, mate = window(own, slot, 3), window(mate, slot, 3)
        far, cross = window(far, slot, 2), window(cross, slot, 2)
        rows = own.shape[0]
        where = Layout(place, rows)
        turned_q = own[:, :PAIR].astype(F32).T * 0.125
        for head in range(2):
            other = slice(HEAD_DIM * (1 - head), HEAD_DIM * (2 - head))
            mine = slice(HEAD_DIM * head, HEAD_DIM * (head + 1))
            q_masked[head, mine, :] = turned_q[mine, :].astype(BF16)
            q_masked[head, other, :] = jnp.zeros((HEAD_DIM, rows), BF16)

        def visit(keys, values, key_row, query, width, first):
            turned = values.astype(F32).T.astype(BF16)
            lanes = pl.ds(query, width)
            mask = where.allowed(where.offset + query, width, key_row, keys.shape[0])
            for head in range(2):
                span = slice(HEAD_DIM * head, HEAD_DIM * (head + 1))
                scores = dot(keys, q_masked[head, :, lanes])
                scores = jnp.where(mask, scores, MASKED)
                top = jnp.max(scores, axis=0, keepdims=True)
                if not first:
                    old = peak[head : head + 1, lanes]
                    top = jnp.maximum(old, top)
                    decay = jnp.exp(old - top)
                prob = jnp.exp(scores - top)
                sums = jnp.sum(prob, axis=0, keepdims=True)
                product = dot(turned[span, :], prob.astype(BF16))
                if not first:
                    sums += total[head : head + 1, lanes] * decay
                    product += accum[span, lanes] * decay
                peak[head : head + 1, lanes] = top
                total[head : head + 1, lanes] = sums
                accum[span, lanes] = product

        half = rows // 2
        visit(
            own[:half, PAIR : 2 * PAIR], own[:half, 2 * PAIR :], where.offset, 0, rows, True
        )
        visit(
            own[half:, PAIR : 2 * PAIR], own[half:, 2 * PAIR :], where.offset + half, half, half,
            False,
        )
        first_start = where.start(where.offset)

        @pl.when(first_start < where.offset)
        def _():
            odd = (where.me & 1) == 1
            visit(
                jnp.where(odd, mate[:, PAIR : 2 * PAIR], cross[:, :PAIR]),
                jnp.where(odd, mate[:, 2 * PAIR :], cross[:, PAIR:]), where.offset - rows,
                0, rows, False,
            )

        @pl.when(first_start < where.offset - rows)
        def _():
            base = where.offset - 2 * rows
            visit(far[half:, :PAIR], far[half:, PAIR:], base + half, 0, rows, False)
            visit(far[:half, :PAIR], far[:half, PAIR:], base, 0, half, False)

        for head in range(2):
            sums = total[head : head + 1, :]
            lse_out[head : head + 1, :] = peak[head : head + 1, :] + jnp.log(sums)
            span = slice(HEAD_DIM * head, HEAD_DIM * (head + 1))
            high[span, :] = accum[span, :] / sums
        low_out[...] = high[...].T.astype(BF16)

    return kernel


def forward_kernel(chunk, units):
    def kernel(
        tokens, attn_part, other, wo_other, bias, gain, shift, w_in, b_in, w_out,
        normed_out, inverse_out, first_out, hidden_out, slope_out, part_out,
    ):
        width = tokens.shape[1]
        last = wo_other.shape[0] - PAIR
        attn = attn_part[tile(chunk), :] + dot(other[tile(chunk), :], wo_other[last:, :])
        attn += bias[...].reshape(1, width)
        normed, inverse = normalize(tokens[tile(chunk), :].astype(F32) + attn)
        normed_out[...] = normed.astype(BF16)
        inverse_out[...] = inverse
        first = normed * gain[...].reshape(1, width) + shift[...].reshape(1, width)
        first_low = first.astype(BF16)
        first_out[...] = first_low
        total = None
        unit = w_in.shape[1] // units
        for index in range(units):
            span = slice(index * unit, (index + 1) * unit)
            pre = dot(first_low, w_in[:, span]) + b_in[span].reshape(1, unit)
            cdf = 0.5 * (1.0 + lax.erf(pre * 0.7071067811865476))
            density = jnp.exp(-0.5 * pre * pre) * 0.3989422804014327
            hidden = (pre * cdf).astype(BF16)
            hidden_out[:, span] = hidden
            slope_out[:, span] = (cdf + pre * density).astype(BF16)
            product = dot(hidden, w_out[span, :])
            total = product if total is None else total + product
        part_out[...] = total.astype(BF16)

    return kernel


def backward_kernel(chunk, units):
    def kernel(
        normed_first, part, other, out_grad, first_gain, first_shift, bias, gain, shift,
        slope, w_in, w_out,
        layer_out, ffn_grad_out, pre_grad_out, part_out, sums_out, inner_out,
    ):
        width = part.shape[1]

        def row(ref):
            return ref[...].reshape(1, width)

        first = normed_first[...].astype(F32) * row(first_gain) + row(first_shift)
        ffn = part[...].astype(F32) + other[...].astype(F32) + row(bias)
        normed, inverse = normalize(first + ffn)
        layer_out[...] = (normed * row(gain) + row(shift)).astype(BF16)
        upstream = out_grad[tile(chunk), :].astype(F32)
        res_grad = norm_back(upstream * row(gain), normed, inverse)
        ffn_grad = res_grad.astype(BF16)
        ffn_grad_out[...] = ffn_grad
        sums_out[0:1, :] = sum_rows(upstream * normed)
        sums_out[1:2, :] = sum_rows(upstream)
        sums_out[2:3, :] = sum_rows(ffn_grad)
        total = None
        unit = w_in.shape[1] // units
        for index in range(units):
            span = slice(index * unit, (index + 1) * unit)
            hidden_grad = dot(ffn_grad, w_out[span, :], NT)
            pre_grad = (hidden_grad * slope[:, span].astype(F32)).astype(BF16)
            pre_grad_out[:, span] = pre_grad
            inner_out[0:1, span] = sum_rows(pre_grad)
            product = dot(pre_grad, w_in[:, span], NT)
            total = product if total is None else total + product
        part_out[...] = total.astype(BF16)

    return kernel


def split_three(value):
    high = value.astype(BF16)
    rest = value - high.astype(F32)
    middle = rest.astype(BF16)
    return high, middle, (rest - middle.astype(F32)).astype(BF16)


def middle_kernel(chunk):
    def kernel(
        ffn_grad, part, other, normed, inverse, gain, wo, high0, high1, high2, lse0, lse1, lse2,
        *rest,
    ):
        grad_out, head_out, sums_out, stats = rest[-4:]
        base = chunk * GRAD_ROWS
        if chunk:
            head_out[:base, :] = rest[0][...]
        width = part.shape[1]
        local = wo.shape[0]
        first_grad = (
            ffn_grad[...].astype(F32) + part[...].astype(F32) + other[...].astype(F32)
        )
        unit = normed[...].astype(F32)
        res_grad = norm_back(first_grad * gain[...].reshape(1, width), unit, inverse[...])
        attn_grad = res_grad.astype(BF16)
        grad_out[...] = attn_grad
        sums_out[0:1, :] = sum_rows(first_grad * unit)
        sums_out[1:2, :] = sum_rows(first_grad)
        sums_out[2:3, :] = sum_rows(attn_grad)
        head_grad = dot(attn_grad, wo[...], NT).astype(BF16)
        head_out[base : base + TILE, :] = head_grad
        high = jnp.concatenate([ref[:, tile(chunk)] for ref in (high0, high1, high2)], axis=0)
        turned = head_grad.astype(F32).T * high
        stats[...] = jnp.zeros_like(stats)
        for index, lse in enumerate((lse0, lse1, lse2)):
            stats[2 * index : 2 * index + 2, :] = lse[:, tile(chunk)]
        for head in range(local // HEAD_DIM):
            span = slice(HEAD_DIM * head, HEAD_DIM * (head + 1))
            stats[8 + head : 9 + head, :] = jnp.sum(turned[span, :], axis=0, keepdims=True)
        begin = base + TILE
        head_out[begin:, :] = jnp.zeros((GRAD_ROWS - TILE, local), BF16)
        for index, value in enumerate(split_three(stats[...])):
            head_out[begin + 16 * index : begin + 16 * (index + 1), :TILE] = value

    return kernel


def stat_rows(grad, chunk):
    begin = chunk * GRAD_ROWS + TILE
    pieces = [
        grad[begin + 16 * index : begin + 16 * (index + 1), :TILE].astype(F32)
        for index in range(3)
    ]
    return pieces[0] + (pieces[1] + pieces[2])


def pair_terms(keys, values, queries, grads, mask, log_row, dot_row):
    scores = jnp.where(mask, dot(keys, queries, NT), MASKED)
    prob = jnp.exp(scores - log_row)
    prob_grad = dot(values, grads, NT)
    return prob.astype(BF16), (prob * (prob_grad - dot_row)).astype(BF16)


def query_side_kernel(pair, slot):
    pair_span = slice(pair * PAIR, (pair + 1) * PAIR)

    def kernel(
        place, own, grad, mate, far, cross, cos, sin,
        q_grad_out, k_part_out, v_part_out,
        q_masked, grad_masked, stats, q_turned,
    ):
        own, mate = window(own, slot, 3), window(mate, slot, 3)
        far, cross = window(far, slot, 2), window(cross, slot, 2)
        rows = own.shape[0]
        where = Layout(place, rows)
        for index in range(rows // TILE):
            stats[:, tile(index)] = stat_rows(grad, index)
            some = grad[index * GRAD_ROWS : index * GRAD_ROWS + TILE, pair_span]
            for head in range(2):
                mask = head_mask((TILE, PAIR), head)
                q_masked[head, tile(index), :] = jnp.where(
                    mask, own[tile(index), :PAIR] * 0.125, 0
                ).astype(BF16)
                grad_masked[head, tile(index), :] = jnp.where(mask, some, 0).astype(BF16)

        def visit(keys, values, key_row, query, width, own_rows=None, fresh=False):
            turned = keys.astype(F32).T.astype(BF16)
            lanes = pl.ds(query, width)
            mask = where.allowed(where.offset + query, width, key_row, keys.shape[0])
            key_sum = value_sum = None
            for head in range(2):
                index = 2 * pair + head
                span = slice(HEAD_DIM * head, HEAD_DIM * (head + 1))
                prob, score_grad = pair_terms(
                    keys, values, q_masked[head, lanes, :], grad_masked[head, lanes, :],
                    mask, stats[index : index + 1, lanes], stats[8 + index : 9 + index, lanes],
                )
                product = dot(turned[span, :], score_grad)
                if fresh:
                    q_turned[span, lanes] = product
                else:
                    q_turned[span, lanes] += product
                if own_rows is not None:
                    key_part = dot(score_grad, q_masked[head, lanes, :])
                    value_part = dot(prob, grad_masked[head, lanes, :])
                    key_sum = key_part if key_sum is None else key_sum + key_part
                    value_sum = value_part if value_sum is None else value_sum + value_part
            if own_rows is not None:
                k_part_out[own_rows, :] = key_sum
                v_part_out[own_rows, :] = value_sum

        half = rows // 2
        low, high = slice(0, half), slice(half, rows)
        visit(
            own[low, PAIR : 2 * PAIR], own[low, 2 * PAIR :], where.offset, 0, rows, low, True
        )
        visit(
            own[high, PAIR : 2 * PAIR], own[high, 2 * PAIR :], where.offset + half, half, half,
            high,
        )
        first_start = where.start(where.offset)

        @pl.when(first_start < where.offset)
        def _():
            odd = (where.me & 1) == 1
            visit(
                jnp.where(odd, mate[:, PAIR : 2 * PAIR], cross[:, :PAIR]),
                jnp.where(odd, mate[:, 2 * PAIR :], cross[:, PAIR:]), where.offset - rows,
                0, rows,
            )

        @pl.when(first_start < where.offset - rows)
        def _():
            base = where.offset - 2 * rows
            visit(far[high, :PAIR], far[high, PAIR:], base + half, 0, rows)
            visit(far[low, :PAIR], far[low, PAIR:], base, 0, half)

        turned = q_turned[...].T * 0.125
        q_grad_out[...] = (turned * cos[...] - swap_halves(turned) * sin[...]).astype(BF16)

    return kernel


def key_side_kernel(pair, slot):
    pair_span = slice(pair * PAIR, (pair + 1) * PAIR)

    def kernel(
        place, own, k_part, v_part, cos, sin, mate, far, cross,
        grad_mate, grad_far, grad_cross,
        k_grad_out, v_grad_out,
        k_masked, v_masked, k_turned, v_sum,
    ):
        own, mate = window(own, slot, 3), window(mate, slot, 3)
        far, cross = window(far, slot, 2), window(cross, slot, 2)
        rows = own.shape[0]
        where = Layout(place, rows)
        span_rows = place[1] * rows
        end = where.offset + rows
        k_turned[...] = k_part[...]
        v_sum[...] = v_part[...]

        def some(ref, chunk):
            return ref[chunk * GRAD_ROWS : chunk * GRAD_ROWS + TILE, pair_span]

        near = (end < span_rows) & (where.start(end) < end)
        beyond = (end + rows < span_rows) & (where.start(end + rows) < end)

        @pl.when(near)
        def _():
            for head in range(2):
                mask = head_mask((rows, PAIR), head)
                k_masked[head] = jnp.where(mask, own[:, PAIR : 2 * PAIR] * 0.125, 0).astype(BF16)
                v_masked[head] = jnp.where(mask, own[:, 2 * PAIR :], 0).astype(BF16)

        def visit(queries, grads, stats, query_row):
            first_head = head_mask((rows, PAIR), 0)
            for index in range(rows // TILE):
                mask = where.allowed(query_row + index * TILE, TILE, where.offset, rows)
                part = queries[index * TILE : (index + 1) * TILE, :]
                key_parts, value_parts = [], []
                for head in range(2):
                    line = 2 * pair + head
                    prob, score_grad = pair_terms(
                        k_masked[head], v_masked[head], part, grads[index], mask,
                        stats[index][line : line + 1, :], stats[index][8 + line : 9 + line, :],
                    )
                    key_parts.append(dot(score_grad, part))
                    value_parts.append(dot(prob, grads[index]))
                k_turned[...] += jnp.where(first_head, *key_parts) * 0.125
                v_sum[...] += jnp.where(first_head, *value_parts)

        @pl.when(near)
        def _():
            even = (where.me & 1) == 0
            chunks = range(rows // TILE)
            visit(
                jnp.where(even, mate[:, :PAIR], cross[:, :PAIR]),
                [jnp.where(even, some(grad_mate, i), some(grad_cross, i)) for i in chunks],
                [
                    jnp.where(even, stat_rows(grad_mate, i), stat_rows(grad_cross, i))
                    for i in chunks
                ],
                end,
            )

        @pl.when(beyond)
        def _():
            chunks = range(rows // TILE)
            visit(
                far[:, :PAIR], [some(grad_far, i) for i in chunks],
                [stat_rows(grad_far, i) for i in chunks], end + rows,
            )

        turned = k_turned[...]
        k_grad_out[...] = (turned * cos[...] - swap_halves(turned) * sin[...]).astype(BF16)
        v_grad_out[...] = v_sum[...].astype(BF16)

    return kernel


def input_kernel(*refs):
    grads, weights, out = refs[:9], refs[9:12], refs[12]
    total = None
    for index, weight in enumerate(weights):
        value = jnp.concatenate([ref[...] for ref in grads[3 * index : 3 * index + 3]], axis=1)
        product = dot(value, weight[...], NT)
        total = product if total is None else total + product
    out[...] = total.astype(BF16)


def finish_input_kernel(part, other, grad0, grad1, out):
    for index, grad in enumerate((grad0, grad1)):
        rows = tile(index)
        out[rows, :] = (
            part[rows, :].astype(F32) + other[rows, :].astype(F32) + grad[...].astype(F32)
        ).astype(BF16)


def stack_kernel(*refs):
    for index, ref in enumerate(refs[:-1]):
        refs[-1][tile(index), :] = ref[...]


def finish_inner_kernel(bit_ref, own, rest, inner_out, o_out):
    upper = bit_ref[0]
    half, wide = own.shape[0], inner_out.shape[1]
    for begin, ref in ((upper, own), (1 - upper, rest)):
        span = pl.ds(pl.multiple_of(begin * half, half), half)
        inner_out[span, :] = ref[:, :wide].astype(F32)
        o_out[:, span] = ref[:, wide:].astype(F32)


def finish_attention_kernel(bit_ref, own, rest, q_out, k_out, v_out, *vector_outs):
    upper = bit_ref[0]
    half, local = own.shape[0], q_out.shape[1]
    for begin, ref in ((upper, own), (1 - upper, rest)):
        span = pl.ds(pl.multiple_of(begin * half, half), half)
        q_out[span, :] = ref[:, :local].astype(F32)
        k_out[span, :] = ref[:, local : 2 * local].astype(F32)
        v_out[span, :] = ref[:, 2 * local : 3 * local].astype(F32)

        @pl.when(begin == 0)
        def _():
            tail = ref[:128, 3 * local :].astype(F32)
            tail = tail + pltpu.roll(tail, HEAD_DIM, 1)
            lane = lax.broadcasted_iota(jnp.int32, (1, PAIR), 1)
            line = 0
            for out in vector_outs:
                for index in range(out.shape[0] // PAIR):
                    value = jnp.where(
                        lane < HEAD_DIM, tail[line : line + 1, :], tail[line + 1 : line + 2, :]
                    )
                    out[index * PAIR : (index + 1) * PAIR] = value[0, :]
                    line += 2


def halves_of(place, rows):
    half = rows // 2
    bit = place[2]
    return (
        pl.multiple_of((1 - bit) * half, half), pl.multiple_of(bit * half, half)
    )


def weight_grad_kernel(place, left0, left1, right0, right1, send_out, keep_out):
    half = left0.shape[1] // 2
    for begin, out in zip(halves_of(place, 2 * half), (send_out, keep_out)):
        span = pl.ds(begin, half)
        out[...] = (
            dot(left0[:, span], right0[...], TN) + dot(left1[:, span], right1[...], TN)
        ).astype(BF16)


def inner_weight_kernel(
    place, first0, first1, pre0, pre1, low0, low1, low2, attn0, attn1, send_out, keep_out
):
    half = first0.shape[1] // 2
    wide = pre0.shape[1]
    lows = jnp.concatenate([low0[...], low1[...], low2[...]], axis=1)
    for begin, out in zip(halves_of(place, 2 * half), (send_out, keep_out)):
        span = pl.ds(begin, half)
        out[:, :wide] = (
            dot(first0[:, span], pre0[...], TN) + dot(first1[:, span], pre1[...], TN)
        ).astype(BF16)
        out[:, wide:] = (
            dot(lows[:TILE], attn0[:, span], TN) + dot(lows[TILE:], attn1[:, span], TN)
        ).astype(BF16)


def attention_weight_kernel(*refs):
    place, tokens = refs[:2]
    grads = refs[2:11]
    second0, second1, first0, first1, inner0, inner1 = refs[11:17]
    send_out, keep_out, vectors = refs[17:]
    width = tokens.shape[1]
    half = width // 2
    vectors[...] = jnp.zeros_like(vectors)
    rows_of = []
    for left, right in ((second0, second1), (first0, first1)):
        for index in range(3):
            rows_of.append(left[index : index + 1, :] + right[index : index + 1, :])
    rows_of.append(inner0[0:1, :] + inner1[0:1, :])
    for grad in grads:
        rows_of.append(sum_rows(grad[...]))
    line = 0
    for value in rows_of:
        for index in range(value.shape[1] // PAIR):
            piece = value[:, index * PAIR : (index + 1) * PAIR]
            vectors[line : line + 1, :] = piece
            vectors[line + 1 : line + 2, :] = pltpu.roll(piece, HEAD_DIM, 1)
            line += 2
    tail = high_and_low(vectors[...], pltpu.roll)
    together = jnp.concatenate([ref[...] for ref in grads], axis=1)
    main = together.shape[1]
    for begin, out in zip(halves_of(place, width), (send_out, keep_out)):
        span = pl.ds(begin, half)
        out[:, :main] = dot(tokens[:, span], together, TN).astype(BF16)
        out[:, main:] = jnp.where(begin == 0, tail, 0).astype(BF16)


def high_and_low(value, roll):
    high = value.astype(BF16).astype(F32)
    return jnp.where(head_mask(value.shape, 0), high, roll(value - high, HEAD_DIM, 1))


def add_two(one, two, tail, roll):
    one, two = one.astype(F32), two.astype(F32)
    if not tail:
        return (one + two).astype(BF16)
    main = one.shape[1] - PAIR
    rest = one[:, main:] + two[:, main:]
    rest = high_and_low(rest + roll(rest, HEAD_DIM, 1), roll)
    return jnp.concatenate([(one[:, :main] + two[:, :main]).astype(BF16), rest.astype(BF16)], axis=1)


def fold(bit, keep, received, split, tail):
    rows, width = keep.shape
    half = rows // 2
    if not split:

        def add_kernel(one, two, out):
            out[...] = add_two(one[...], two[...], tail, pltpu.roll)

        return call(add_kernel, [keep, received], [((rows, width), BF16)], cost=2.0)[0]
    if half % 16:
        total = add_two(keep, received, tail, jnp.roll)
        return [
            lax.dynamic_slice_in_dim(total, start * half, half, 0) for start in (1 - bit, bit)
        ]

    def fold_kernel(bit_ref, one, two, send_out, keep_out):
        upper = bit_ref[0]
        for begin, out in ((1 - upper, send_out), (upper, keep_out)):
            span = pl.ds(pl.multiple_of(begin * half, half), half)
            out[...] = add_two(one[span, :], two[span, :], tail, pltpu.roll)

    return call(
        fold_kernel, [bit.reshape(1), keep, received], [((half, width), BF16)] * 2, scalars=1,
        cost=2.0,
    )


def join(bit, own, received, dtype=BF16):
    half, width = own.shape
    if half % 16:
        ordered = jnp.where(
            bit == 1,
            jnp.concatenate([received, own], axis=0),
            jnp.concatenate([own, received], axis=0),
        )
        return ordered.astype(dtype)

    def join_kernel(bit_ref, one, two, out):
        upper = bit_ref[0]
        out[pl.ds(pl.multiple_of(upper * half, half), half), :] = one[...].astype(dtype)
        out[pl.ds(pl.multiple_of((1 - upper) * half, half), half), :] = two[...].astype(dtype)

    return call(
        join_kernel, [bit.reshape(1), own, received], [((2 * half, width), dtype)], scalars=1,
        cost=2.0, final=dtype == F32,
    )[0]


def flip(value, axis, bit):
    size = lax.axis_size(axis)
    return lax.ppermute(value, axis, [(i, i ^ bit) for i in range(size)])


class Sum:
    def __init__(self, pieces, stages, bits, tail=False):
        send, self.value = pieces
        self.tail, self.stages, self.bits, self.index = tail, stages, bits, 0
        self.received = flip(send, *stages[0])

    def step(self):
        stages, index, count = self.stages, self.index, len(self.stages)
        if index == 2 * count - 2:
            return
        self.index += 1
        if index < count - 2:
            stage = stages[index + 1]
            send, self.value = fold(self.bits[stage], self.value, self.received, True, self.tail)
            self.received = flip(send, *stage)
            return
        if index < count:
            self.value = fold(None, self.value, self.received, False, self.tail)
        else:
            self.value = join(self.bits[stages[2 * count - 2 - index]], self.value, self.received)
        self.received = flip(self.value, *stages[count - 1 if index == count - 2 else 2 * count - 3 - index])

    def finish(self):
        while self.index < 2 * len(self.stages) - 2:
            self.step()
        return self.value, self.received


def per_device(
    tokens, out_grad, lengths, query_weight, query_bias, key_weight, key_bias, value_weight,
    value_bias, output_weight, output_bias, first_gain, first_shift, inner_weight, inner_bias,
    outer_weight, outer_bias, second_gain, second_shift,
):
    Order.last = None
    rows, width = tokens.shape
    local = query_weight.shape[1]
    pairs = local // PAIR
    hidden_width = inner_weight.shape[1]
    chunks = rows // TILE
    units = hidden_width // 512
    ctx_size, dp_size = lax.axis_size("ctx"), lax.axis_size("dp")
    me = lax.axis_index("ctx")
    spot = jnp.arange(8)
    place = jnp.pad(lengths[0], (3, 5 - lengths.shape[1])) + jnp.where(
        spot == 0, me, jnp.where(spot == 1, ctx_size, jnp.where(spot == 2, me & 1, 0))
    )
    stage_bits = [
        (axis, 1 << i)
        for axis, size in (("ctx", ctx_size), ("dp", dp_size))
        for i in range((size - 1).bit_length())
    ]
    bits = {
        (axis, bit): ((lax.axis_index(axis) & bit) != 0).astype(jnp.int32)
        for axis, bit in stage_bits
    }
    ctx_stages = [stage for stage in stage_bits if stage[0] == "ctx"]

    frequency = 10000.0 ** (-2.0 * np.arange(HEAD_DIM // 2) / HEAD_DIM)
    lanes = np.tile(frequency, PAIR // (HEAD_DIM // 2))
    angles = np.arange(rows)[:, None] * lanes[None, :]
    trig = jnp.asarray(
        np.concatenate([np.cos(angles), np.sin(angles), np.tile(lanes, (8, 1))]), F32
    )

    weights = [query_weight, key_weight, value_weight, query_bias, key_bias, value_bias]
    owns, fars, mates = [], [], []
    reach = ctx_size // 2
    around = [(i, (i + reach) % ctx_size) for i in range(ctx_size)]
    table = ((rows, PAIR), F32)
    def swap(value):
        return flip(value, "tensor", 1)

    places = [(group, slot) for group, pair_list in enumerate(GROUPS) for slot in range(len(pair_list))]
    for index, group in enumerate(GROUPS):
        shapes = [
            ((rows, 3 * PAIR * len(group)), BF16), ((rows, 2 * PAIR * len(group)), BF16),
        ]
        if index == 0:
            sources = [tokens, *weights]
            own, sent, cosine, sine, *copied = call(
                first_project_kernel, [place, trig, *sources],
                shapes + [table, table] + [(value.shape, value.dtype) for value in sources],
                scratch=[
                    pltpu.VMEM(trig.shape, F32), pltpu.SemaphoreType.DMA((1 + len(sources),)),
                ],
                scalars=1, hbm=1 + len(sources), cost=3.0,
            )
            tokens, weights = copied[0], copied[1:]
        else:
            own, sent = call(
                project_kernel(group), [place, tokens, *weights, cosine, sine], shapes,
                scalars=1, cost=1.0,
            )
        owns.append(own)
        fars.append(lax.ppermute(sent, "ctx", around))

    weight_other = swap(lax.optimization_barrier((output_weight, owns[0]))[0])
    lows, logs, highs, crosses, low_others = [], [], [], [], []

    def load(*values, after=()):
        return call(
            load_kernel, values, [(value.shape, value.dtype) for value in values],
            scratch=[pltpu.SemaphoreType.DMA((len(values),))], hbm=len(values), cost=2.0, after=after,
        )

    def exchange(index):
        if index:
            owns[index], fars[index], _ = lax.optimization_barrier(
                (owns[index], fars[index], lows[-1])
            )
        else:
            fars[0], _ = lax.optimization_barrier((fars[0], owns[-1]))
        mates.append(flip(owns[index], "ctx", 1))
        crosses.append(flip(fars[index], "ctx", 1))

    exchange(0)
    output_bias = load(output_bias)[0]
    for index, slot in places:
        low, lse, high = call(
            attend_kernel(slot),
            [place, owns[index], mates[index], fars[index], crosses[index]],
            [((rows, PAIR), BF16), ((2, rows), F32), ((PAIR, rows), F32)],
            scratch=[
                pltpu.VMEM((2, PAIR, rows), BF16), pltpu.VMEM((2, rows), F32),
                pltpu.VMEM((2, rows), F32), pltpu.VMEM((PAIR, rows), F32),
            ],
            scalars=1, cost=4.0, after=(weight_other,) if len(lows) == 1 else (),
        )
        lows.append(low)
        low_others.append(swap(low))
        logs.append(lse)
        highs.append(high)
        if len(lows) < len(GROUPS):
            exchange(len(lows))
    attn_part, inner_weight, outer_weight = call(
        output_kernel,
        [
            *lows, *low_others[: pairs - 1], output_weight, weight_other, inner_weight,
            outer_weight,
        ],
        [((rows, width), F32)]
        + [(value.shape, value.dtype) for value in (inner_weight, outer_weight)],
        scratch=[pltpu.SemaphoreType.DMA((2,))], hbm=2, cost=2.0,
    )
    block = ((TILE, width), BF16)
    wide = ((TILE, hidden_width), BF16)
    forward = []
    for chunk in range(chunks):
        forward.append(
            call(
                forward_kernel(chunk, units),
                [
                    tokens, attn_part, low_others[-1], weight_other, output_bias, first_gain,
                    first_shift, inner_weight, inner_bias, outer_weight,
                ],
                [block, ((TILE, 1), F32), block, wide, wide, block],
                cost=3.5,
            )
        )
    normed, inverse, first_low, hidden, slope, ffn_parts = zip(*forward)
    ffn_others = [swap(part) for part in ffn_parts]
    backward = []
    for chunk in range(chunks):
        backward.append(
            call(
                backward_kernel(chunk, units),
                [
                    normed[chunk], ffn_parts[chunk], ffn_others[chunk], out_grad, first_gain,
                    first_shift, outer_bias, second_gain, second_shift, slope[chunk],
                    inner_weight, outer_weight,
                ],
                [
                    block, block, wide, block, ((8, width), F32), ((8, hidden_width), F32),
                ],
                cost=3.0,
            )
        )
    layer_out, ffn_grad, pre_grad, first_parts, second_sums, inner_sums = zip(*backward)
    first_others = [swap(part) for part in first_parts]

    back_reach = [(i + reach, i) for i in range(ctx_size - reach)]
    attn_grad, first_sums, head_grad = [], [], []
    for chunk in range(chunks):
        grad, head_part, sums = call(
            middle_kernel(chunk),
            [
                ffn_grad[chunk], first_parts[chunk], first_others[chunk], normed[chunk],
                inverse[chunk], first_gain, output_weight, *highs, *logs, *head_grad[-1:],
            ],
            [block, (((chunk + 1) * GRAD_ROWS, local), BF16), ((8, width), F32)],
            scratch=[pltpu.VMEM((16, TILE), F32)],
            cost=1.5,
        )
        attn_grad.append(grad)
        first_sums.append(sums)
        head_grad.append(head_part)
        if chunk == 0:
            outer_half = ((hidden_width // 2, width), BF16)
            outer_pieces = call(
                weight_grad_kernel, [place, *hidden, *ffn_grad], [outer_half] * 2, scalars=1, cost=2.0
            )
            outer_sum = Sum(outer_pieces, stage_bits, bits)
    head_grad = head_grad[-1]
    grad_far = lax.ppermute(head_grad, "ctx", back_reach)
    grad_mate = flip(head_grad, "ctx", 1)
    outer_sum.step()
    inner_half = ((width // 2, hidden_width + local), BF16)
    inner_pieces = call(
        inner_weight_kernel, [place, *first_low, *pre_grad, *lows, *attn_grad],
        [inner_half] * 2, scalars=1, cost=2.0,
    )
    inner_sum = Sum(inner_pieces, stage_bits, bits)

    q_grads, k_grads, v_grads, key_parts = [], [], [], []
    double = pltpu.VMEM((2, rows, PAIR), BF16)
    single = pltpu.VMEM((rows, PAIR), F32)

    def query_side(pair):
        index, slot = places[pair]
        q_grad, k_part, v_part = call(
            query_side_kernel(pair, slot),
            [
                place, owns[index], head_grad, mates[index], fars[index], crosses[index],
                cosine, sine,
            ],
            [((rows, PAIR), BF16), table, table],
            scratch=[
                double, double, pltpu.VMEM((16, rows), F32), pltpu.VMEM((PAIR, rows), F32),
            ],
            scalars=1, cost=4.0,
        )
        q_grads.append(q_grad)
        key_parts.append((k_part, v_part))

    def key_side(pair):
        index, slot = places[pair]
        k_grad, v_grad = call(
            key_side_kernel(pair, slot),
            [
                place, owns[index], *key_parts[pair], cosine, sine, mates[index],
                fars[index], crosses[index], grad_mate, grad_far, grad_cross,
            ],
            [((rows, PAIR), BF16)] * 2,
            scratch=[double, double, single, single],
            scalars=1, cost=4.0,
        )
        k_grads.append(k_grad)
        v_grads.append(v_grad)

    query_side(0)
    inner_sum.step()
    query_side(1)
    query_side(2)
    outer_sum.step()
    grad_far, _ = lax.optimization_barrier((grad_far, q_grads[1]))
    grad_cross = flip(grad_far, "ctx", 1)
    key_side(0)
    key_side(1)
    outer_sum.step()
    key_side(2)
    inner_sum.step()
    all_grads = [*q_grads, *k_grads, *v_grads]
    attention_half = ((width // 2, 3 * local + PAIR), BF16)
    attention_sum = Sum(
        call(
            attention_weight_kernel,
            [place, tokens, *all_grads, *second_sums, *first_sums, *inner_sums],
            [attention_half] * 2,
            scratch=[pltpu.VMEM((width // 2, PAIR), F32)],
            scalars=1, cost=2.5,
        ),
        stage_bits, bits, True,
    )
    outer_sum.step()
    attention_sum.step()
    input_part = call(
        input_kernel, [*all_grads, *weights[:3]], [((rows, width), BF16)], cost=1.5
    )[0]
    input_other = swap(input_part)
    inner_sum.step()
    layer_out = call(
        stack_kernel, layer_out, [((rows, width), BF16)], cost=0.3, final=True
    )[0]

    attention_sum.step()
    outer_sum.step()
    inner_sum.step()
    attention_sum.step()
    outer_own, outer_rest = outer_sum.finish()
    inner_sum.step()
    attention_sum.step()
    input_grad = call(
        finish_input_kernel, [input_part, input_other, *attn_grad], [((rows, width), BF16)],
        cost=0.5, final=True,
    )[0]
    core = bits[ctx_stages[0]]
    outer_grad = join(core, outer_own, outer_rest, F32)
    attention_sum.step()
    inner_own, inner_rest = inner_sum.finish()
    inner_grad, o_weight_grad = call(
        finish_inner_kernel, [core.reshape(1), inner_own, inner_rest],
        [((width, hidden_width), F32), ((local, width), F32)], scalars=1, cost=2.0, final=True,
    )
    attention_own, attention_rest = attention_sum.finish()
    vector_sizes = [width] * 6 + [hidden_width] + [local] * 3
    (
        q_weight_grad, k_weight_grad, v_weight_grad,
        second_gain_grad, second_shift_grad, outer_bias_grad,
        first_gain_grad, first_shift_grad, output_bias_grad, inner_bias_grad,
        q_bias_grad, k_bias_grad, v_bias_grad,
    ) = call(
        finish_attention_kernel,
        [core.reshape(1), attention_own, attention_rest],
        [((width, local), F32)] * 3 + [((size,), F32) for size in vector_sizes],
        scalars=1, cost=2.0, final=True,
    )
    return (
        layer_out, input_grad,
        q_weight_grad, q_bias_grad, k_weight_grad, k_bias_grad, v_weight_grad, v_bias_grad,
        o_weight_grad, output_bias_grad, first_gain_grad, first_shift_grad,
        inner_grad, inner_bias_grad, outer_grad, outer_bias_grad,
        second_gain_grad, second_shift_grad,
    )


def solution(mesh):
    rows_spec, column_spec, row_spec = P(("dp", "ctx"), None), P(None, "tensor"), P("tensor", None)
    return jax.shard_map(
        per_device,
        mesh=mesh,
        in_specs=(
            rows_spec, rows_spec, P("dp", None),
            column_spec, P("tensor"), column_spec, P("tensor"), column_spec, P("tensor"),
            row_spec, P(), P(), P(), column_spec, P("tensor"), row_spec, P(), P(), P(),
        ),
        out_specs=(
            rows_spec, rows_spec,
            column_spec, P("tensor"), column_spec, P("tensor"), column_spec, P("tensor"),
            row_spec, P(), P(), P(), column_spec, P("tensor"), row_spec, P(), P(), P(),
        ),
        check_vma=False,
    )
```
